32 devices in a mesh: groups: 2 (over y), tm: 4 (over z), space: 2 (over x), yz: 2 (over core).
Axes of the slice: x: 2, y: 2, z: 4, core: 2. Of those that a mesh axis runs over, the one named last changes fastest.
Arguments:
- initial: float32 [96, 32, 128], P(('groups', 'space'), 'yz'), parts along dimension 0, may hold values from -6 to 6
- diffusion: float32 [96, 32, 128], P(('groups', 'space'), 'yz'), parts along dimension 0, may hold values from 0.008 to 0.024
- velocity: float32 [3, 96, 32, 128], P(None, ('groups', 'space'), 'yz'), parts along dimension 1, may hold values from -0.013 to 0.013
- control: float32 [4, 96, 32, 128], P('tm', ('groups', 'space'), 'yz'), parts along dimension 1, may hold values from -0.6 to 0.6
- target: float32 [4, 96, 32, 128], P('tm', ('groups', 'space'), 'yz'), parts along dimension 1, may hold values from -6 to 6
- state_guess: float32 [4, 96, 32, 128], P('tm', ('groups', 'space'), 'yz'), parts along dimension 1, may hold values from -6 to 6
- adjoint_guess: float32 [4, 96, 32, 128], P('tm', ('groups', 'space'), 'yz'), parts along dimension 1, may hold values from -6 to 6
Outputs:
- state_new: float32 [4, 96, 32, 128], P('tm', ('groups', 'space'), 'yz'), parts along dimension 1
- gradient: float32 [4, 96, 32, 128], P('tm', ('groups', 'space'), 'yz'), parts along dimension 1
The draws below stay inside these ranges and needn't reach their ends.
There are 2 independent parts, one for each index of `groups`. The reference program is written for one: setup_inputs(seed, part) draws one part's arguments, and reference() takes and returns one part's arrays. A program takes and returns all parts, laid end to end along the dimension named above; each array names one. Nothing has to cross between parts.
All inputs are finite; a program needn't handle non-finite values.
Results may differ from the reference program's by a relative error of at most 0.00002.
Values sent between devices are 32-bit elements; how exact they have to be, the bound alone decides.
No kernel may reach another device: no remote copies, remote signals or barrier semaphores. Data moves between devices by JAX's collectives and lax.ppermute only.
A program may use at most 64 MiB of HBM per device.

```python
import math
import jax
import jax.numpy as jnp

NZ = 128
STEPS = 6
SLABS = 4
NX = 48
NY = 32


def block_levels(stream_key, dims, shards, smallest, high):
    loudness, own = 1.0, jax.random.fold_in(stream_key, 6)
    for axis_at, blocks in shards:
        draws = jnp.exp(jax.random.uniform(jax.random.fold_in(own, axis_at), (blocks,), jnp.float32, smallest / len(shards), high / len(shards)))
        loudness = loudness * jnp.repeat(draws, dims[axis_at] // blocks).reshape([-1 if axis == axis_at else 1 for axis in range(len(dims))])
    return loudness


def centred(rng, extent, width, bound, cuts=(), held_as=jnp.bfloat16):
    array = jax.random.normal(rng, extent, jnp.float32) * width
    if len(cuts) > 0:
        array = block_levels(rng, extent, cuts, -0.22, 0.18) * array
    return jnp.clip(array, min=-bound, max=bound).astype(held_as)


def setup_inputs(seed: int = 0, part: int = 0) -> dict:
    splits = jax.random.split(jax.random.key(seed), 8)
    part_splits = jax.random.split(jax.random.fold_in(splits[7], part), 8)
    return {
        "initial": centred(part_splits[0], (NX, NY, NZ), 1.0, 6.0, ((0, 2), (1, 2)), jnp.float32),
        "diffusion": jnp.clip(jnp.exp(math.log(0.024) - 1.09861225 * jax.random.uniform(part_splits[1], (NX, NY, NZ), jnp.float32) ** block_levels(part_splits[1], (NX, NY, NZ), ((0, 2), (1, 2)), -0.2, 0.2)), 0.008, 0.024),
        "velocity": jnp.clip(jax.random.uniform(part_splits[2], (3, NX, NY, NZ), jnp.float32, -0.013, 0.013) * block_levels(part_splits[2], (3, NX, NY, NZ), ((1, 2), (2, 2)), -0.4, 0.0), -0.013, 0.013),
        "control": centred(part_splits[3], (SLABS, NX, NY, NZ), 0.1, 0.6, ((0, 4), (1, 2), (2, 2)), jnp.float32),
        "target": centred(part_splits[4], (SLABS, NX, NY, NZ), 1.0, 6.0, ((0, 4), (1, 2), (2, 2)), jnp.float32),
        "state_guess": centred(part_splits[5], (SLABS, NX, NY, NZ), 1.0, 6.0, ((0, 4), (1, 2), (2, 2)), jnp.float32),
        "adjoint_guess": centred(part_splits[6], (SLABS, NX, NY, NZ), 1.0, 6.0, ((0, 4), (1, 2), (2, 2)), jnp.float32),
    }


def neighbour_cells(field):
    widths = [(0, 0)] * (field.ndim - 3) + [(1, 1)] * 3
    padded = jnp.pad(field, widths)
    upper = (padded[..., 2:, 1:-1, 1:-1], padded[..., 1:-1, 2:, 1:-1], padded[..., 1:-1, 1:-1, 2:])
    lower = (padded[..., :-2, 1:-1, 1:-1], padded[..., 1:-1, :-2, 1:-1], padded[..., 1:-1, 1:-1, :-2])
    return upper, lower


def forward_map(field, diffusion, velocity, factor):
    upper, lower = neighbour_cells(field)
    laplace = upper[0] + lower[0] + upper[1] + lower[1] + upper[2] + lower[2] - 6.0 * field
    transport = velocity[0] * (upper[0] - lower[0]) + velocity[1] * (upper[1] - lower[1]) + velocity[2] * (upper[2] - lower[2])
    return field + factor * (diffusion * laplace - transport)


def adjoint_map(field, diffusion, velocity, factor):
    spread = diffusion * field
    upper, lower = neighbour_cells(spread)
    laplace = upper[0] + lower[0] + upper[1] + lower[1] + upper[2] + lower[2] - 6.0 * spread
    transport = jnp.zeros_like(field)
    for axis_number in range(3):
        up_cells, low_cells = neighbour_cells(velocity[axis_number] * field)
        transport = transport + (up_cells[axis_number] - low_cells[axis_number])
    return field + factor * (laplace + transport)


def reference(initial, diffusion, velocity, control, target, state_guess, adjoint_guess):
    coarse = float(STEPS)
    start = jnp.concatenate([initial[None], state_guess[:-1]], 0)
    fine = start
    for step_index in range(STEPS):
        fine = forward_map(fine, diffusion, velocity, 1.0) + control
    state_residual = fine - state_guess
    correction = state_residual[0]
    pieces = [correction]
    for slab in range(1, SLABS):
        correction = state_residual[slab] + forward_map(correction, diffusion, velocity, coarse)
        pieces.append(correction)
    state_new = state_guess + jnp.stack(pieces, 0)
    sweep = adjoint_guess
    for step_index in range(STEPS):
        sweep = adjoint_map(sweep, diffusion, velocity, 1.0)
    from_next = jnp.concatenate([sweep[1:], jnp.zeros_like(sweep[:1])], 0)
    adjoint_residual = from_next + state_new - target - adjoint_guess
    correction = adjoint_residual[SLABS - 1]
    pieces = [correction]
    for slab in range(SLABS - 2, -1, -1):
        correction = adjoint_residual[slab] + adjoint_map(correction, diffusion, velocity, coarse)
        pieces.append(correction)
    multiplier = adjoint_guess + jnp.stack(pieces[::-1], 0)
    running_sum = multiplier
    for step_index in range(STEPS - 1):
        multiplier = adjoint_map(multiplier, diffusion, velocity, 1.0)
        running_sum = running_sum + multiplier
    gradient = running_sum / coarse + 0.5 * control
    return state_new, gradient
```

```python
import functools

import jax
import jax.numpy as jnp
from jax import lax
from jax.experimental import pallas as pl
from jax.experimental.pallas import tpu as pltpu
from jax.sharding import PartitionSpec as P

STEPS = 6
BLOCK = 4
EDGE = 8
COEF = 9
LATE = 5
MSG = 7
FAR_X = 10
FAR_E = 7
RIMS = (COEF, COEF, COEF, COEF, 6, 6, 7, 1)
STARTS = tuple(sum(RIMS[:i]) for i in range(len(RIMS)))


def extended(array, sides, width):
    for axis, dim in sides:
        peers, length = (lax.axis_size(axis), array.shape[dim])
        up = [(i, (i + 1) % peers) for i in range(peers - 1)]
        down = [(j, i) for i, j in up]
        last = lax.slice_in_dim(array, length - width, length, axis=dim)
        first = lax.slice_in_dim(array, 0, width, axis=dim)
        before = lax.ppermute(last, axis, up)
        after = lax.ppermute(first, axis, down)
        array = jnp.concatenate([before, array, after], axis=dim)
    return array


def passed_along(block, axis, distance):
    devices = range(lax.axis_size(axis))
    route = [(i - distance, i) for i in devices if i - distance in devices]
    return lax.ppermute(block, axis, route)


def depth_pad(field):
    return jnp.pad(field, ((0, 0), (0, 0), (1, 1)))


def local_map(padded, coefficients, factor, adjoint):
    centre = padded[1:-1, 1:-1, :]
    if adjoint:
        spread = coefficients[0] * padded
        carried = coefficients[1:4] * padded
        inner_spread = spread[1:-1, 1:-1, :]
        deep = depth_pad(inner_spread)
        laplace = (
            spread[2:, 1:-1, :]
            + spread[:-2, 1:-1, :]
            + spread[1:-1, 2:, :]
            + spread[1:-1, :-2, :]
            + deep[:, :, 2:]
            + deep[:, :, :-2]
            - 6.0 * inner_spread
        )
        deep_carry = depth_pad(carried[2, 1:-1, 1:-1, :])
        transport = (
            carried[0, 2:, 1:-1, :]
            - carried[0, :-2, 1:-1, :]
            + (carried[1, 1:-1, 2:, :] - carried[1, 1:-1, :-2, :])
            + (deep_carry[:, :, 2:] - deep_carry[:, :, :-2])
        )
        return (centre + factor * (laplace + transport)) * coefficients[4, 1:-1, 1:-1, :]
    inner = coefficients[:, 1:-1, 1:-1, :]
    deep = depth_pad(centre)
    laplace = (
        padded[2:, 1:-1, :]
        + padded[:-2, 1:-1, :]
        + padded[1:-1, 2:, :]
        + padded[1:-1, :-2, :]
        + deep[:, :, 2:]
        + deep[:, :, :-2]
        - 6.0 * centre
    )
    transport = (
        inner[1] * (padded[2:, 1:-1, :] - padded[:-2, 1:-1, :])
        + inner[2] * (padded[1:-1, 2:, :] - padded[1:-1, :-2, :])
        + inner[3] * (deep[:, :, 2:] - deep[:, :, :-2])
    )
    return centre + factor * (inner[0] * laplace - transport)


def halo_cells(field):
    return extended(field, (("space", 0), ("yz", 1)), 1)


def coarse_chain(residual, near_coefficients, adjoint, direction):
    factor = float(STEPS)

    def one_turn(turn_index, correction):
        moved = local_map(halo_cells(correction), near_coefficients, factor, adjoint)
        arrived = passed_along(moved, "tm", direction)
        return residual + arrived

    return lax.fori_loop(0, lax.axis_size("tm") - 1, one_turn, residual)


def any_mesh(initial, diffusion, velocity, control, target, state_guess, adjoint_guess):
    source = control[0]
    guess_state = state_guess[0]
    guess_adjoint = adjoint_guess[0]
    stacked = jnp.concatenate([diffusion[None], velocity, jnp.ones_like(diffusion)[None]], 0)
    near_coefficients = extended(stacked, (("space", 1), ("yz", 2)), 1)
    arrived = passed_along(guess_state, "tm", 1)
    fine = jnp.where(lax.axis_index("tm") == 0, initial, arrived)
    sweep = guess_adjoint
    for step_index in range(STEPS):
        fine = local_map(halo_cells(fine), near_coefficients, 1.0, False) + source
    for step_index in range(STEPS):
        sweep = local_map(halo_cells(sweep), near_coefficients, 1.0, True)
    state_residual = fine - guess_state
    state_new = guess_state + coarse_chain(state_residual, near_coefficients, False, 1)
    from_next = passed_along(sweep, "tm", -1)
    adjoint_residual = from_next + state_new - target[0] - guess_adjoint
    multiplier = guess_adjoint + coarse_chain(adjoint_residual, near_coefficients, True, -1)
    running_sum = multiplier
    for step_index in range(STEPS - 1):
        multiplier = local_map(halo_cells(multiplier), near_coefficients, 1.0, True)
        running_sum = running_sum + multiplier
    gradient = running_sum / float(STEPS) + 0.5 * source
    return (state_new[None], gradient[None])


def rolled(value, shift, axis):
    return pltpu.roll(value, shift % value.shape[axis], axis)


class Stencil:
    NAMES = ("c0", "xp", "xm", "yp", "ym", "zp", "zm", "qyp", "qym", "qzp", "qzm")

    def __init__(self, ref):
        self.at = {name: ref.at[i] for i, name in enumerate(self.NAMES)}
        self.ref = ref

    def fill(self, rows, raw, space, core):
        sign = (1 - 2 * space).astype(jnp.float32)

        def one(r, carry):
            d, u0, u1, u2 = raw(r)
            u0 = u0 * sign
            cell = lax.broadcasted_iota(jnp.int32, d.shape, 0)
            depth = lax.broadcasted_iota(jnp.int32, d.shape, 1)
            own = d.shape[0] - EDGE
            top = (cell == own - 1) & (core == 1)
            bottom = (cell == 0) & (core == 0)
            last, first = depth == d.shape[1] - 1, depth == 0
            zero = jnp.zeros_like(d)
            values = {
                "c0": 1.0 - 6.0 * d,
                "xp": d - u0,
                "xm": d + u0,
                "yp": jnp.where(top, zero, d - u1),
                "ym": jnp.where(bottom, zero, d + u1),
                "zp": jnp.where(last, zero, d - u2),
                "zm": jnp.where(first, zero, d + u2),
                "qyp": jnp.where(top, zero, rolled(d + u1, -1, 0)),
                "qym": jnp.where(bottom, zero, rolled(d - u1, 1, 0)),
                "qzp": jnp.where(last, zero, rolled(d + u2, -1, 1)),
                "qzm": jnp.where(first, zero, rolled(d - u2, 1, 1)),
            }
            for name in self.NAMES:
                self.at[name][r + 1] = values[name]
            return carry

        for name in self.NAMES:
            self.at[name][0] = jnp.zeros(self.ref.shape[2:], jnp.float32)
        lax.fori_loop(0, rows, one, 0)

    def both(self, v, start, adjoint):
        here = pl.ds(start + 1, BLOCK)
        at = self.at
        c = v[1:-1]
        if adjoint:
            up, low = at["xm"][pl.ds(start + 2, BLOCK)], at["xp"][pl.ds(start, BLOCK)]
            ends = [at[n][here] for n in ("qyp", "qym", "qzp", "qzm")]
        else:
            up, low = at["xp"][here], at["xm"][here]
            ends = [at[n][here] for n in ("yp", "ym", "zp", "zm")]
        around = up * v[2:] + low * v[:-2]
        around = around + (ends[0] * rolled(c, -1, 1) + ends[1] * rolled(c, 1, 1))
        around = around + (ends[2] * rolled(c, -1, 2) + ends[3] * rolled(c, 1, 2))
        return around, at["c0"][here]

    def fine(self, v, start, adjoint):
        around, own = self.both(v, start, adjoint)
        return own * v[1:-1] + around

    def coarse(self, v, start, adjoint):
        around, own = self.both(v, start, adjoint)
        c = v[1:-1]
        return c + float(STEPS) * (around + (own * c - c))


def padded_rows(rows):
    return -(-rows // BLOCK) * BLOCK + 2


def blocks(rows, body):
    def one(b, carry):
        body(b * BLOCK)
        return carry

    lax.fori_loop(0, -(-rows // BLOCK), one, 0)


def around_rows(ref, start):
    return ref[pl.ds(start, BLOCK + 2)]


def put(ref, start, value):
    ref[pl.ds(start + 1, BLOCK)] = value


def fine_kernel(rows, own, where_ref, d_ref, u_ref, control_ref, sg_ref, ag_ref, initial_ref, target_ref, xr_ref, ya_ref, yb_ref,
                z_out, x_out, base_out, state_out, ext_out, coef, c_a, c_b, g_a, g_b, s_a, s_b, con, tar):
    slab, space, core = where_ref[0], where_ref[1], where_ref[2]
    flip = space == 1

    def natural(r):
        return jnp.where(flip, rows - 1 - r, r)

    def mine(i, read, r):
        at = natural(r)
        return jnp.concatenate([read(at), ya_ref[i, at]], 0)

    def rim(i, j):
        at = STARTS[i] + jnp.where(flip, RIMS[i] - 1 - j, j)
        return jnp.concatenate([xr_ref[at], yb_ref[at]], 0)

    reads = (
        lambda r: d_ref[r],
        lambda r: u_ref[0, r],
        lambda r: u_ref[1, r],
        lambda r: u_ref[2, r],
        lambda r: control_ref[0, r],
        lambda r: sg_ref[0, r],
    )
    first = slab == 0

    def load_own(r, carry):
        for i in range(4):
            ext_out[i, r] = mine(i, reads[i], r)
        con[r + 1] = mine(4, reads[4], r)
        g_a[r + 1] = mine(5, reads[5], r)
        at = natural(r)
        start = jnp.concatenate([initial_ref[at], ya_ref[6, at]], 0)
        c_a[r + 1] = jnp.where(first, start, jnp.zeros_like(start))
        s_a[r + 1] = jnp.concatenate([ag_ref[0, at], ya_ref[6, at]], 0)
        tar[r + 1] = mine(7, lambda n: target_ref[0, n], r)
        return carry

    lax.fori_loop(0, rows, load_own, 0)
    for j in range(COEF):
        for i in range(4):
            ext_out[i, rows + j] = rim(i, j)
    for j in range(RIMS[4]):
        con[rows + 1 + j] = rim(4, j)
    for j in range(RIMS[5]):
        g_a[rows + 1 + j] = rim(5, j)
    for j in range(RIMS[6]):
        start = rim(6, j)
        c_a[rows + 1 + j] = jnp.where(first, start, jnp.zeros_like(start))
        s_a[rows + 1 + j] = start
    tar[rows + 1] = rim(7, 0)
    zero_row = jnp.zeros(c_a.shape[1:], jnp.float32)
    for ref in (c_a, c_b, g_a, g_b, s_a, s_b):
        ref[0] = zero_row

    stencil = Stencil(coef)
    stencil.fill(rows + COEF, lambda r: [ext_out[i, r] for i in range(4)], space, core)

    c, g, s = (c_a, c_b), (g_a, g_b), (s_a, s_b)
    for step in range(STEPS):
        now, later = step % 2, 1 - step % 2

        def one(start, now=now, later=later):
            put(c[later], start, stencil.fine(around_rows(c[now], start), start, False) + con[pl.ds(start + 1, BLOCK)])
            put(g[later], start, stencil.fine(around_rows(g[now], start), start, False))
            put(s[later], start, stencil.fine(around_rows(s[now], start), start, True))

        blocks(rows + STEPS - step, one)
    cc, dd = c_b, s_b

    def differences(r, carry):
        sg = mine(5, reads[5], r)
        fine = c_a[r + 1]
        gap = fine - sg
        ag = jnp.concatenate([ag_ref[0, natural(r)], ya_ref[6, natural(r)]], 0)
        state = sg + gap
        rest = state - tar[r + 1] - ag
        cc[r + 1] = gap
        dd[r + 1] = rest
        state_out[r] = state[:own]
        base_out[r] = (ag + rest)[:own]
        return carry

    lax.fori_loop(0, rows, differences, 0)
    sg = rim(5, 0)
    gap = c_a[rows + 1] - sg
    cc[rows + 1] = gap
    dd[rows + 1] = (sg + gap) - tar[rows + 1] - rim(6, 0)

    def pair(start):
        x = g_a[pl.ds(start + 1, BLOCK)] + stencil.coarse(around_rows(cc, start), start, False)
        e = s_a[pl.ds(start + 1, BLOCK)] + stencil.coarse(around_rows(dd, start), start, True)
        z_out[pl.ds(start, BLOCK)] = x[:, :own]
        z_out[pl.ds(rows + start, BLOCK)] = e[:, :own]

    blocks(rows, pair)
    for j in range(FAR_X):
        x_out[j] = z_out[rows - 1 - j]
    for j in range(FAR_E):
        x_out[FAR_X + j] = z_out[2 * rows - 1 - j]
    for j in range(LATE):
        x_out[FAR_X + FAR_E + j] = base_out[rows - 1 - j]


def pair_kernel(rows, own, where_ref, ext_ref, z_ref, x_ref, zr_ref, xr_ref, xzr_ref, ym_ref, yx_ref, yp_ref, yd_ref, base_ref, state_ref,
                msg_out, base_out, state_out, coef, xa, xb, ea, eb, t0, t1, t2):
    slab, space, core = where_ref[0], where_ref[1], where_ref[2]
    odd = slab % 2 == 1
    upper = slab >= 2
    stencil = Stencil(coef)
    stencil.fill(rows + COEF, lambda r: [ext_ref[i, r] for i in range(4)], space, core)

    def gather(mine_ref, mine_y, other_ref, other_y, lower, upper_, at, to, count):
        def one(r, carry):
            mine = jnp.concatenate([mine_ref[at + r], mine_y[at + r]], 0)
            other = jnp.concatenate([other_ref[at + r], other_y[at + r]], 0)
            lower[to + r + 1] = jnp.where(odd, other, mine)
            upper_[to + r + 1] = jnp.where(odd, mine, other)
            return carry

        lax.fori_loop(0, count, one, 0)

    gather(z_ref, ym_ref, zr_ref, yp_ref, xa, xb, 0, 0, rows)
    gather(z_ref, ym_ref, zr_ref, yp_ref, ea, eb, rows, 0, rows)
    gather(xr_ref, yx_ref, xzr_ref, yd_ref, xa, xb, 0, rows, FAR_X)
    gather(xr_ref, yx_ref, xzr_ref, yd_ref, ea, eb, FAR_X, rows, FAR_E)
    zero_row = jnp.zeros(xa.shape[1:], jnp.float32)
    for ref in (xa, xb, ea, eb, t0, t1, t2):
        ref[0] = zero_row

    def base_at(start):
        return pl.ds(start, BLOCK)

    for j in range(rows):
        base_out[j] = base_ref[j]
        state_out[j] = state_ref[j] + jnp.where(odd, xa[j + 1][:own], jnp.zeros_like(state_ref[j]))
    for j in range(LATE):
        base_out[rows + j] = xr_ref[FAR_X + FAR_E + j]

    width = base_out.shape[0]

    def add_base(value):
        def one(r, carry):
            base_out[r] = base_out[r] + value(r)[:own]
            return carry

        lax.fori_loop(0, rows + LATE, one, 0)

    def send(value_ref):
        def one(r, carry):
            msg_out[r] = value_ref[r + 1][:own]
            return carry

        lax.fori_loop(0, rows + MSG, one, 0)

    @pl.when(jnp.logical_not(upper))
    def _():
        def h(start):
            put(t0, start, xb[pl.ds(start + 1, BLOCK)] + stencil.coarse(around_rows(xa, start), start, False))

        blocks(rows + FAR_X - 1, h)
        send(t0)

        def ph(start):
            put(t1, start, stencil.coarse(around_rows(t0, start), start, False))

        blocks(rows + FAR_X - 2, ph)

        def qph(start):
            put(t2, start, t0[pl.ds(start + 1, BLOCK)] + stencil.coarse(around_rows(t1, start), start, True))

        blocks(rows + FAR_X - 3, qph)

        def nh(start):
            put(t1, start, xa[pl.ds(start + 1, BLOCK)] + stencil.coarse(around_rows(t2, start), start, True))

        blocks(rows + FAR_X - 4, nh)

        @pl.when(odd)
        def _():
            add_base(lambda r: t1[r + 1])

        @pl.when(jnp.logical_not(odd))
        def _():
            def q(start):
                put(t2, start, eb[pl.ds(start + 1, BLOCK)] + stencil.coarse(around_rows(t1, start), start, True))

            blocks(rows + LATE, q)
            add_base(lambda r: t2[r + 1])

    @pl.when(upper)
    def _():
        def q(start):
            put(t0, start, eb[pl.ds(start + 1, BLOCK)] + stencil.coarse(around_rows(xa, start), start, True))

        blocks(rows + FAR_E, q)

        def qq(start):
            put(t1, start, ea[pl.ds(start + 1, BLOCK)] + stencil.coarse(around_rows(t0, start), start, True))

        blocks(rows + FAR_E - 1, qq)
        send(t1)

        @pl.when(odd)
        def _():
            add_base(lambda r: xa[r + 1])

        @pl.when(jnp.logical_not(odd))
        def _():
            add_base(lambda r: t0[r + 1])


def last_kernel(rows, own, where_ref, ext_ref, msg_ref, msg_y, base_ref, base_y, state_ref, control_ref,
                state_out, gradient_out, coef, m, t0, t1, total):
    slab, space, core = where_ref[0], where_ref[1], where_ref[2]
    stencil = Stencil(coef)
    stencil.fill(rows + MSG, lambda r: [ext_ref[i, r] for i in range(4)], space, core)

    def load(r, carry):
        m[r + 1] = jnp.concatenate([msg_ref[r], msg_y[r]], 0)
        return carry

    lax.fori_loop(0, rows + MSG, load, 0)
    zero_row = jnp.zeros(m.shape[1:], jnp.float32)
    for ref in (m, t0, t1):
        ref[0] = zero_row

    def moved(start):
        put(t0, start, stencil.coarse(around_rows(m, start), start, False))

    blocks(rows + MSG - 1, moved)

    def state(r, carry):
        at = jnp.where(space == 1, rows - 1 - r, r)
        came = jnp.where(slab == 2, m[r + 1], jnp.where(slab == 3, t0[r + 1], zero_row))
        state_out[0, at] = state_ref[r] + came[:own]
        return carry

    lax.fori_loop(0, rows, state, 0)

    def source(r, carry):
        m_row, t_row = m[r + 1], t0[r + 1]
        total[r + 1] = jnp.where((slab == 1) | (slab == 2), m_row, jnp.where(slab == 3, t_row, zero_row))
        t0[r + 1] = jnp.where(slab == 0, m_row, jnp.where(slab == 2, t_row, zero_row))
        return carry

    lax.fori_loop(0, rows + MSG - 1, source, 0)

    def multiplier(start):
        put(t1, start, total[pl.ds(start + 1, BLOCK)] + stencil.coarse(around_rows(t0, start), start, True))

    blocks(rows + LATE, multiplier)

    def add(r, carry):
        value = t1[r + 1] + jnp.concatenate([base_ref[r], base_y[r]], 0)
        t1[r + 1] = value
        total[r + 1] = value
        return carry

    lax.fori_loop(0, rows + LATE, add, 0)

    pair = (t1, t0)
    for step in range(STEPS - 1):
        now, later = pair[step % 2], pair[1 - step % 2]

        def one(start, now=now, later=later):
            value = stencil.fine(around_rows(now, start), start, True)
            put(later, start, value)
            put(total, start, total[pl.ds(start + 1, BLOCK)] + value)

        blocks(rows + LATE - 1 - step, one)

    def out(r, carry):
        at = jnp.where(space == 1, rows - 1 - r, r)
        gradient_out[0, at] = total[r + 1][:own] / float(STEPS) + 0.5 * control_ref[0, at]
        return carry

    lax.fori_loop(0, rows, out, 0)


def whole(count):
    return [pl.BlockSpec(memory_space=pltpu.VMEM)] * count


def call(kernel, outs, scratch, cost, *args):
    return pl.pallas_call(
        kernel,
        out_shape=[jax.ShapeDtypeStruct(shape, jnp.float32) for shape in outs],
        in_specs=[pl.BlockSpec(memory_space=pltpu.SMEM)] + whole(len(args) - 1),
        out_specs=whole(len(outs)),
        scratch_shapes=[pltpu.VMEM(shape, jnp.float32) for shape in scratch],
        compiler_params=pltpu.CompilerParams(vmem_limit_bytes=48 * 1024 * 1024),
        cost_estimate=pl.CostEstimate(flops=cost, bytes_accessed=4000000, transcendentals=0),
    )(*args)


def swapped(block, axis):
    return lax.ppermute(block, axis, [(0, 1), (1, 0)])


def across(block, distance):
    return lax.ppermute(block, "tm", [(i, i ^ distance) for i in range(4)])


def across_turned(block, distance):
    route = [(2 * i + j, 2 * (i ^ distance) + 1 - j) for i in range(4) for j in range(2)]
    return lax.ppermute(block, ("tm", "space"), route)


def four_slabs(initial, diffusion, velocity, control, target, state_guess, adjoint_guess):
    rows, own, depth = diffusion.shape
    wide = own + EDGE
    slab, space, core = lax.axis_index("tm"), lax.axis_index("space"), lax.axis_index("yz")
    where = jnp.stack([slab, space, core]).astype(jnp.int32)
    start = jnp.where(slab == 0, initial, adjoint_guess[0])
    fields = (diffusion, velocity[0], velocity[1], velocity[2], control[0], state_guess[0], start, target[0])

    def edge(block):
        return lax.dynamic_slice_in_dim(block, jnp.where(core == 0, own - EDGE, 0), EDGE, axis=block.ndim - 2)

    x_send = jnp.concatenate(
        [lax.dynamic_slice_in_dim(f, jnp.where(space == 0, rows - n, 0), n, axis=0) for f, n in zip(fields, RIMS)], 0
    )
    x_here = swapped(x_send, "space")
    y_a = swapped(jnp.stack([edge(f) for f in fields]), "yz")
    y_b = swapped(edge(x_here), "yz")

    tall = padded_rows(rows + COEF + 3)
    field = (tall, wide, depth)
    coefs = (len(Stencil.NAMES), *field)
    z_out, x_out, base, state, ext = call(
        functools.partial(fine_kernel, rows, own),
        [
            (2 * rows, own, depth),
            (FAR_X + FAR_E + LATE, own, depth),
            (rows, own, depth),
            (rows, own, depth),
            (4, rows + COEF, wide, depth),
        ],
        [coefs] + [field] * 8,
        20000000,
        where, diffusion, velocity, control, state_guess, adjoint_guess, initial, target, x_here, y_a, y_b,
    )
    far = FAR_X + FAR_E
    z_in = across(z_out, 1)
    x_in = swapped(x_out, "space")
    xz_in = across_turned(x_out[:far], 1)
    y_all = swapped(edge(jnp.concatenate([z_out, z_in, x_in[:far], xz_in], 0)), "yz")
    two = 2 * rows
    msg, base, state = call(
        functools.partial(pair_kernel, rows, own),
        [(rows + MSG, own, depth), (rows + LATE, own, depth), (rows, own, depth)],
        [coefs] + [field] * 7,
        8000000,
        where, ext, z_out, x_out, z_in, x_in, xz_in,
        y_all[:two], y_all[2 * two : 2 * two + far], y_all[two : 2 * two], y_all[2 * two + far :], base, state,
    )
    msg_in = across(msg, 2)
    y_last = swapped(edge(jnp.concatenate([msg_in, base], 0)), "yz")
    state_new, gradient = call(
        functools.partial(last_kernel, rows, own),
        [(1, rows, own, depth), (1, rows, own, depth)],
        [coefs] + [field] * 4,
        7000000,
        where, ext, msg_in, y_last[: rows + MSG], base, y_last[rows + MSG :], state, control,
    )
    return state_new, gradient


def solution(mesh):
    sizes = mesh.shape

    def local(*args):
        rows, own, depth = args[1].shape
        fits = (sizes["tm"], sizes["space"], sizes["yz"]) == (4, 2, 2)
        fits = fits and rows >= FAR_X and rows % BLOCK == 0 and own % 8 == 0 and own >= EDGE and depth % 128 == 0
        return four_slabs(*args) if fits else any_mesh(*args)

    field = P(("groups", "space"), "yz", None)
    slabs = P("tm", ("groups", "space"), "yz", None)
    return jax.shard_map(
        local,
        mesh=mesh,
        in_specs=(field, field, P(None, ("groups", "space"), "yz", None), slabs, slabs, slabs, slabs),
        out_specs=(slabs, slabs),
        check_vma=False,
    )
```

```python
import functools

import jax
import jax.numpy as jnp
from jax import lax
from jax.experimental import pallas as pl
from jax.experimental.pallas import tpu as pltpu
from jax.sharding import PartitionSpec as P

STEPS = 6
SIDE = 8
NEAR = 6
LATE = 5
MSG = 7
FAR_X = 10
FAR_E = 7
COEF = FAR_X - 1
RIMS = (NEAR, NEAR, NEAR, NEAR, NEAR, NEAR, NEAR + 1, 1)
STARTS = tuple(sum(RIMS[:i]) for i in range(len(RIMS)))


def extended(array, sides, width):
    for axis, dim in sides:
        peers, length = (lax.axis_size(axis), array.shape[dim])
        up = [(i, (i + 1) % peers) for i in range(peers - 1)]
        down = [(j, i) for i, j in up]
        last = lax.slice_in_dim(array, length - width, length, axis=dim)
        first = lax.slice_in_dim(array, 0, width, axis=dim)
        before = lax.ppermute(last, axis, up)
        after = lax.ppermute(first, axis, down)
        array = jnp.concatenate([before, array, after], axis=dim)
    return array


def passed_along(block, axis, distance):
    devices = range(lax.axis_size(axis))
    route = [(i - distance, i) for i in devices if i - distance in devices]
    return lax.ppermute(block, axis, route)


def depth_pad(field):
    return jnp.pad(field, ((0, 0), (0, 0), (1, 1)))


def local_map(padded, coefficients, factor, adjoint):
    centre = padded[1:-1, 1:-1, :]
    if adjoint:
        spread = coefficients[0] * padded
        carried = coefficients[1:4] * padded
        inner_spread = spread[1:-1, 1:-1, :]
        deep = depth_pad(inner_spread)
        laplace = (
            spread[2:, 1:-1, :]
            + spread[:-2, 1:-1, :]
            + spread[1:-1, 2:, :]
            + spread[1:-1, :-2, :]
            + deep[:, :, 2:]
            + deep[:, :, :-2]
            - 6.0 * inner_spread
        )
        deep_carry = depth_pad(carried[2, 1:-1, 1:-1, :])
        transport = (
            carried[0, 2:, 1:-1, :]
            - carried[0, :-2, 1:-1, :]
            + (carried[1, 1:-1, 2:, :] - carried[1, 1:-1, :-2, :])
            + (deep_carry[:, :, 2:] - deep_carry[:, :, :-2])
        )
        return (centre + factor * (laplace + transport)) * coefficients[4, 1:-1, 1:-1, :]
    inner = coefficients[:, 1:-1, 1:-1, :]
    deep = depth_pad(centre)
    laplace = (
        padded[2:, 1:-1, :]
        + padded[:-2, 1:-1, :]
        + padded[1:-1, 2:, :]
        + padded[1:-1, :-2, :]
        + deep[:, :, 2:]
        + deep[:, :, :-2]
        - 6.0 * centre
    )
    transport = (
        inner[1] * (padded[2:, 1:-1, :] - padded[:-2, 1:-1, :])
        + inner[2] * (padded[1:-1, 2:, :] - padded[1:-1, :-2, :])
        + inner[3] * (deep[:, :, 2:] - deep[:, :, :-2])
    )
    return centre + factor * (inner[0] * laplace - transport)


def halo_cells(field):
    return extended(field, (("space", 0), ("yz", 1)), 1)


def coarse_chain(residual, near_coefficients, adjoint, direction):
    factor = float(STEPS)

    def one_turn(turn_index, correction):
        moved = local_map(halo_cells(correction), near_coefficients, factor, adjoint)
        arrived = passed_along(moved, "tm", direction)
        return residual + arrived

    return lax.fori_loop(0, lax.axis_size("tm") - 1, one_turn, residual)


def any_mesh(initial, diffusion, velocity, control, target, state_guess, adjoint_guess):
    source = control[0]
    guess_state = state_guess[0]
    guess_adjoint = adjoint_guess[0]
    stacked = jnp.concatenate([diffusion[None], velocity, jnp.ones_like(diffusion)[None]], 0)
    near_coefficients = extended(stacked, (("space", 1), ("yz", 2)), 1)
    arrived = passed_along(guess_state, "tm", 1)
    fine = jnp.where(lax.axis_index("tm") == 0, initial, arrived)
    sweep = guess_adjoint
    for step_index in range(STEPS):
        fine = local_map(halo_cells(fine), near_coefficients, 1.0, False) + source
    for step_index in range(STEPS):
        sweep = local_map(halo_cells(sweep), near_coefficients, 1.0, True)
    state_residual = fine - guess_state
    state_new = guess_state + coarse_chain(state_residual, near_coefficients, False, 1)
    from_next = passed_along(sweep, "tm", -1)
    adjoint_residual = from_next + state_new - target[0] - guess_adjoint
    multiplier = guess_adjoint + coarse_chain(adjoint_residual, near_coefficients, True, -1)
    running_sum = multiplier
    for step_index in range(STEPS - 1):
        multiplier = local_map(halo_cells(multiplier), near_coefficients, 1.0, True)
        running_sum = running_sum + multiplier
    gradient = running_sum / float(STEPS) + 0.5 * source
    return (state_new[None], gradient[None])


NAMES = ("c0", "xp", "xm", "yp", "ym", "zp", "zm", "qyp", "qym", "qzp", "qzm")
CHUNK = 8


class Rows:
    def __init__(self, ref, wide, first=-1):
        self.ref, self.wide, self.first = ref, wide, first

    def read(self, row, count=1, shift=0):
        return self.ref[pl.ds((row - self.first) * self.wide + shift, count * self.wide)]

    def write(self, row, value):
        self.ref[pl.ds((row - self.first) * self.wide, value.shape[0])] = value


def shifted(value, step):
    return pltpu.roll(value, step % value.shape[1], 1)


def next_cells(value, step):
    return pltpu.roll(value, step % value.shape[0], 0)


class Stencil:
    def __init__(self, ref, wide):
        self.at = {name: Rows(ref.at[i], wide) for i, name in enumerate(NAMES)}

    def fill(self, row, raw, space, core):
        d, u0, u1, u2 = raw
        u0 = u0 * (1 - 2 * space).astype(jnp.float32)
        cell = lax.broadcasted_iota(jnp.int32, d.shape, 0)
        depth = lax.broadcasted_iota(jnp.int32, d.shape, 1)
        top = (cell == d.shape[0] - 1) & (core == 1)
        bottom = (cell == 0) & (core == 0)
        last, first = depth == d.shape[1] - 1, depth == 0
        zero = jnp.zeros_like(d)
        values = {
            "c0": 1.0 - 6.0 * d,
            "xp": d - u0,
            "xm": d + u0,
            "yp": jnp.where(top, zero, d - u1),
            "ym": jnp.where(bottom, zero, d + u1),
            "zp": jnp.where(last, zero, d - u2),
            "zm": jnp.where(first, zero, d + u2),
            "qyp": jnp.where(top, zero, next_cells(d + u1, -1)),
            "qym": jnp.where(bottom, zero, next_cells(d - u1, 1)),
            "qzp": jnp.where(last, zero, shifted(d + u2, -1)),
            "qzm": jnp.where(first, zero, shifted(d - u2, 1)),
        }
        for name in NAMES:
            self.at[name].write(row, values[name])

    def edge(self):
        for name in NAMES:
            rows = self.at[name]
            rows.write(-1, jnp.zeros((rows.wide, rows.ref.shape[-1]), jnp.float32))

    def terms(self, fields, row, count, adjoint):
        at = self.at
        if adjoint:
            up, low, ends = at["xm"].read(row + 1, count), at["xp"].read(row - 1, count), ("qyp", "qym", "qzp", "qzm")
        else:
            up, low, ends = at["xp"].read(row, count), at["xm"].read(row, count), ("yp", "ym", "zp", "zm")
        yp, ym, zp, zm = (at[n].read(row, count) for n in ends)
        same = at["c0"].read(row, count)
        result = []
        for v in fields:
            c = v.read(row, count)
            around = up * v.read(row + 1, count) + low * v.read(row - 1, count)
            around = around + (yp * v.read(row, count, 1) + ym * v.read(row, count, -1))
            around = around + (zp * shifted(c, -1) + zm * shifted(c, 1))
            result.append((around, c, same * c))
        return result

    def fine(self, fields, row, count, adjoint):
        return [own + around for around, c, own in self.terms(fields, row, count, adjoint)]

    def coarse(self, v, row, count, adjoint):
        ((around, c, own),) = self.terms([v], row, count, adjoint)
        return c + float(STEPS) * (around + (own - c))


def chunks(start, stop, size=CHUNK):
    return [(row, min(size, stop - row)) for row in range(start, stop, size)]


def joined(core, own, side):
    return jnp.where(core == 1, jnp.concatenate([side, own], 0), jnp.concatenate([own, side], 0))


def mid(core, cells):
    return jnp.where(core == 1, cells[SIDE:], cells[:-SIDE])


def zeros(rows):
    return jnp.zeros((rows.wide, rows.ref.shape[-1]), jnp.float32)


def pack_kernel(rows, own, where_ref, d_ref, u_ref, control_ref, sg_ref, ag_ref, initial_ref, target_ref,
                x_out, side_out, d_out, u_out, control_out, sg_out, ag_out, initial_out, target_out, whole_sem, part_sem):
    slab, space, core = where_ref[0], where_ref[1], where_ref[2]
    ins = (d_ref, u_ref, control_ref, sg_ref, ag_ref, initial_ref, target_ref)
    outs = (d_out, u_out, control_out, sg_out, ag_out, initial_out, target_out)
    fields = (d_ref, u_ref.at[0], u_ref.at[1], u_ref.at[2], control_ref.at[0], sg_ref.at[0], None, target_ref.at[0])
    beside = pl.multiple_of(jnp.where(core == 0, own - SIDE, 0), SIDE)
    begin = [jnp.where(space == 0, rows - n, 0) for n in RIMS]
    parts, wholes = [], []
    for i, field in enumerate(fields):
        if field is not None:
            rim = x_out.at[pl.ds(STARTS[i], RIMS[i])]
            parts.append(pltpu.make_async_copy(field.at[pl.ds(begin[i], RIMS[i])], rim, part_sem.at[2 * i]))
            parts.append(pltpu.make_async_copy(field.at[:, pl.ds(beside, SIDE)], side_out.at[i], part_sem.at[2 * i + 1]))
    for i, (source, target) in enumerate(zip(ins, outs)):
        wholes.append(pltpu.make_async_copy(source, target, whole_sem.at[i]))
    for copy in (wholes[4], wholes[5], *parts, *wholes[:4], wholes[6]):
        copy.start()
    wholes[4].wait()
    wholes[5].wait()
    first = slab == 0
    for j in range(RIMS[6]):
        at = begin[6] + j
        x_out[STARTS[6] + j] = jnp.where(first, initial_out[at], ag_out[0, at])
    for row in range(rows):
        cells = jnp.where(first, initial_out[row], ag_out[0, row])
        side_out[6, row] = jnp.where(core == 0, cells[own - SIDE :], cells[:SIDE])
    for copy in (*parts, *wholes[:4], wholes[6]):
        copy.wait()


def inner_kernel(rows, wide, where_ref, d_ref, u_ref, control_ref, sg_ref, ag_ref, initial_ref, target_ref, side_ref,
                 coef_out, hist_out, z_out, base_out, state_out, c_a, c_b, g_a, g_b, s_a, s_b, con_ref):
    slab, space, core = where_ref[0], where_ref[1], where_ref[2]
    first = slab == 0
    c, g, s = ([Rows(r, wide) for r in pair] for pair in ((c_a, c_b), (g_a, g_b), (s_a, s_b)))
    con = Rows(con_ref, wide, 0)
    for field in (*c, *g, *s):
        field.write(-1, zeros(field))
    stencil = Stencil(coef_out, wide)
    stencil.edge()

    def natural(row):
        return jnp.where(space == 1, rows - 1 - row, row)

    def mine(i, own, row):
        return joined(core, own, side_ref[i, natural(row)])

    for row in range(rows):
        at = natural(row)
        stencil.fill(row, [mine(0, d_ref[at], row)] + [mine(1 + i, u_ref[i, at], row) for i in range(3)], space, core)
        con.write(row, mine(4, control_ref[0, at], row))
        g[0].write(row, mine(5, sg_ref[0, at], row))
        start = mine(6, initial_ref[at], row)
        c[0].write(row, jnp.where(first, start, jnp.zeros_like(start)))
        s[0].write(row, mine(6, ag_ref[0, at], row))

    def keep(level, fields):
        for i, field in enumerate(fields):
            hist_out[i, level] = field.read(rows - 2 - level, 2)

    keep(0, (c[0], g[0], s[0]))
    for step in range(STEPS):
        now, later = step % 2, 1 - step % 2
        for row, count in chunks(0, rows - 1 - step, 4):
            to_c, to_g = stencil.fine((c[now], g[now]), row, count, False)
            (to_s,) = stencil.fine((s[now],), row, count, True)
            c[later].write(row, to_c + con.read(row, count))
            g[later].write(row, to_g)
            s[later].write(row, to_s)
        if step < STEPS - 1:
            keep(step + 1, (c[later], g[later], s[later]))
    cc, dd = c[1], s[1]
    ready = rows - STEPS
    for row in range(ready):
        sg = mine(5, sg_ref[0, natural(row)], row)
        gap = c[0].read(row) - sg
        ag = mine(6, ag_ref[0, natural(row)], row)
        state = sg + gap
        rest = state - mine(7, target_ref[0, natural(row)], row) - ag
        cc.write(row, gap)
        dd.write(row, rest)
        state_out[row] = mid(core, state)
        base_out[row] = mid(core, ag + rest)
    keep(STEPS, (cc, g[0], s[0], dd))
    for row, count in chunks(0, ready - 1):
        x = g[0].read(row, count) + stencil.coarse(cc, row, count, False)
        e = s[0].read(row, count) + stencil.coarse(dd, row, count, True)
        for r in range(count):
            z_out[row + r] = mid(core, x[r * wide : (r + 1) * wide])
            z_out[ready - 1 + row + r] = mid(core, e[r * wide : (r + 1) * wide])


def wedge_kernel(rows, wide, where_ref, coef_in, hist_ref, d_ref, u_ref, control_ref, sg_ref, ag_ref, target_ref, side_ref, z_ref, xr_ref, ys_ref,
                 coef_out, z_out, x_out, far_out, base_out, state_out, c_a, c_b, g_a, g_b, s_a, s_b, con_ref, sg_s, tar_s, ag_s):
    slab, space, core = where_ref[0], where_ref[1], where_ref[2]
    first = slab == 0
    flip = space == 1
    c, g, s = (
        [[Rows(r, wide, rows - 2 - level) for r in pair] for level in range(STEPS + 1)]
        for pair in ((c_a, c_b), (g_a, g_b), (s_a, s_b))
    )
    at_level = lambda field, level: field[level][level % 2]
    low = rows - STEPS
    con, sgs, tars, ags = (Rows(r, wide, low) for r in (con_ref, sg_s, tar_s, ag_s))
    stencil = Stencil(coef_out, wide)

    def natural(row):
        return jnp.where(flip, rows - 1 - row, row)

    def rim(i, j):
        at = STARTS[i] + jnp.where(flip, RIMS[i] - 1 - j, j)
        return joined(core, xr_ref[at], ys_ref[at])

    for j in range(NEAR):
        stencil.fill(rows + j, [rim(i, j) for i in range(4)], space, core)
    for row in range(low, rows):
        at = natural(row)
        con.write(row, joined(core, control_ref[0, at], side_ref[4, at]))
        sgs.write(row, joined(core, sg_ref[0, at], side_ref[5, at]))
        ags.write(row, joined(core, ag_ref[0, at], side_ref[6, at]))
        tars.write(row, joined(core, target_ref[0, at], side_ref[7, at]))
    for j in range(NEAR):
        con.write(rows + j, rim(4, j))
    sgs.write(rows, rim(5, 0))
    ags.write(rows, rim(6, 0))
    tars.write(rows, rim(7, 0))
    for j in range(NEAR + 1):
        start = rim(6, j)
        c[0][0].write(rows + j, jnp.where(first, start, jnp.zeros_like(start)))
        if j < NEAR:
            s[0][0].write(rows + j, start)
            g[0][0].write(rows + j, rim(5, j))

    def restore(level, fields):
        for i, field in enumerate(fields):
            field.write(rows - 2 - level, hist_ref[i, level])

    restore(0, (c[0][0], g[0][0], s[0][0]))
    for level in range(STEPS):
        row = rows - 1 - level
        nc, ng, ns = (at_level(f, level) for f in (c, g, s))
        lc, lg, ls = (at_level(f, level + 1) for f in (c, g, s))
        to_c, to_g = stencil.fine((nc, ng), row, NEAR, False)
        (to_s,) = stencil.fine((ns,), row, NEAR, True)
        lc.write(row, to_c + con.read(row, NEAR))
        lg.write(row, to_g)
        ls.write(row, to_s)
        (to_c,) = stencil.fine((nc,), row + NEAR, 1, False)
        lc.write(row + NEAR, to_c + con.read(row + NEAR))
        if level < STEPS - 1:
            restore(level + 1, (lc, lg, ls))
    fc, fg, fs = (at_level(f, STEPS) for f in (c, g, s))
    cc, dd = c[STEPS][1], s[STEPS][1]
    restore(STEPS, (cc, fg, fs, dd))
    count = NEAR + 1
    sg = sgs.read(low, count)
    gap = fc.read(low, count) - sg
    state = sg + gap
    ag = ags.read(low, count)
    rest = state - tars.read(low, count) - ag
    cc.write(low, gap)
    dd.write(low, rest)
    base = ag + rest
    x = fg.read(low - 1, count) + stencil.coarse(cc, low - 1, count, False)
    e = fs.read(low - 1, count) + stencil.coarse(dd, low - 1, count, True)

    def cells(value, r):
        return mid(core, value[r * wide : (r + 1) * wide])

    for r in range(NEAR):
        state_out[r] = cells(state, r)
        base_out[r] = cells(base, r)
    for r in range(count):
        x_row, e_row = cells(x, r), cells(e, r)
        z_out[r] = x_row
        z_out[count + r] = e_row
        for out in (x_out, far_out):
            out[count - 1 - r] = x_row
            out[FAR_X + count - 1 - r] = e_row
    for j in range(count, FAR_X):
        x_row = z_ref[rows - 1 - j]
        for out in (x_out, far_out):
            out[j] = x_row
    late = FAR_X + FAR_E
    for j in range(LATE):
        x_out[late + j] = cells(base, NEAR - 1 - j)
    for j in range(COEF - NEAR):
        at = natural(rows - 1 - NEAR - j)
        for i, value in enumerate([d_ref[at]] + [u_ref[i, at] for i in range(3)]):
            x_out[late + LATE + i * (COEF - NEAR) + j] = value


def message_kernel(rows, wide, where_ref, coef_in, za, zb, ra, rb, xr, xzr, za_y, zb_y, ra_y, rb_y, xr_y, xzr_y,
                   coef_out, msg_out, h_out, xa_out, eb_out, xb_s, ea_s):
    slab, space, core = where_ref[0], where_ref[1], where_ref[2]
    odd = slab % 2 == 1
    upper = slab >= 2
    stencil = Stencil(coef_out, wide)
    late = FAR_X + FAR_E
    for j in range(COEF - NEAR):
        at = [late + LATE + i * (COEF - NEAR) + j for i in range(4)]
        stencil.fill(rows + NEAR + j, [joined(core, xr[r], xr_y[late + r - late - LATE]) for r in at], space, core)
    xa, xb, ea, eb, h = (Rows(r, wide) for r in (xa_out, xb_s, ea_s, eb_out, h_out))
    for field in (xa, xb, ea, eb, h):
        field.write(-1, zeros(field))

    def both(lower, higher, row, mine, mine_y, other, other_y, at):
        a, b = joined(core, mine[at], mine_y[at]), joined(core, other[at], other_y[at])
        lower.write(row, jnp.where(odd, b, a))
        higher.write(row, jnp.where(odd, a, b))

    inner = rows - NEAR - 1
    for row in range(rows):
        if row < inner:
            both(xa, xb, row, za, za_y, ra, ra_y, row)
            both(ea, eb, row, za, za_y, ra, ra_y, inner + row)
        else:
            both(xa, xb, row, zb, zb_y, rb, rb_y, row - inner)
            both(ea, eb, row, zb, zb_y, rb, rb_y, rows - inner + row - inner)
    for j in range(FAR_X):
        both(xa, xb, rows + j, xr, xr_y, xzr, xzr_y, j)
    for j in range(FAR_E):
        both(ea, eb, rows + j, xr, xr_y, xzr, xzr_y, FAR_X + j)

    @pl.when(jnp.logical_not(upper))
    def _():
        for row, count in chunks(0, rows + FAR_X - 1):
            h.write(row, xb.read(row, count) + stencil.coarse(xa, row, count, False))
        for row in range(rows + MSG):
            msg_out[row] = mid(core, h.read(row))

    @pl.when(upper)
    def _():
        for row, count in chunks(0, rows + FAR_E):
            h.write(row, eb.read(row, count) + stencil.coarse(xa, row, count, True))
        for row, count in chunks(0, rows + FAR_E - 1):
            value = ea.read(row, count) + stencil.coarse(h, row, count, True)
            for r in range(count):
                msg_out[row + r] = mid(core, value[r * wide : (r + 1) * wide])
        msg_out[rows + FAR_E - 1] = mid(core, zeros(ea))


def base_kernel(rows, wide, where_ref, coef_ref, h_ref, xa_ref, eb_ref, start_a, start_b, start_x, base_out, t1_s, t2_s):
    slab, core = where_ref[0], where_ref[2]
    odd = slab % 2 == 1
    upper = slab >= 2
    stencil = Stencil(coef_ref, wide)
    h, xa, eb, t1, t2 = (Rows(r, wide) for r in (h_ref, xa_ref, eb_ref, t1_s, t2_s))
    for field in (t1, t2):
        field.write(-1, zeros(field))

    def start(row):
        if row >= rows:
            return start_x[FAR_X + FAR_E + row - rows]
        return start_a[row] if row < start_a.shape[0] else start_b[row - start_a.shape[0]]

    def put(source):
        for row in range(rows + LATE):
            base_out[row] = start(row) + mid(core, source.read(row))

    @pl.when(jnp.logical_not(upper))
    def _():
        for row, count in chunks(0, rows + FAR_X - 2):
            t1.write(row, stencil.coarse(h, row, count, False))
        for row, count in chunks(0, rows + FAR_X - 3):
            t2.write(row, h.read(row, count) + stencil.coarse(t1, row, count, True))
        for row, count in chunks(0, rows + FAR_X - 4):
            t1.write(row, xa.read(row, count) + stencil.coarse(t2, row, count, True))

        @pl.when(odd)
        def _():
            put(t1)

        @pl.when(jnp.logical_not(odd))
        def _():
            for row, count in chunks(0, rows + LATE):
                t2.write(row, eb.read(row, count) + stencil.coarse(t1, row, count, True))
            put(t2)

    @pl.when(upper & odd)
    def _():
        put(xa)

    @pl.when(upper & jnp.logical_not(odd))
    def _():
        put(h)


def last_kernel(rows, wide, where_ref, coef_ref, msg, msg_y, base, base_y, xa_ref, state_a, state_b, control_ref,
                state_out, gradient_out, m_s, t0_s, t1_s, total_s):
    slab, space, core = where_ref[0], where_ref[1], where_ref[2]
    stencil = Stencil(coef_ref, wide)
    m, t0, t1, total, xa = (Rows(r, wide) for r in (m_s, t0_s, t1_s, total_s, xa_ref))
    for field in (m, t0, t1):
        field.write(-1, zeros(field))

    def natural(row):
        return jnp.where(space == 1, rows - 1 - row, row)

    def state(came):
        for row in range(rows):
            before = state_a[row] if row < state_a.shape[0] else state_b[row - state_a.shape[0]]
            state_out[0, natural(row)] = before + mid(core, came(row)) if came else before

    def begin(extra):
        for row, count in chunks(0, rows + LATE):
            ready = jnp.concatenate([joined(core, base[r], base_y[r]) for r in range(row, row + count)], 0)
            t1.write(row, ready + extra(row, count))

    for row in range(rows + MSG):
        m.write(row, joined(core, msg[row], msg_y[row]))

    @pl.when(slab == 0)
    def _():
        begin(lambda row, count: stencil.coarse(m, row, count, True))
        state(None)

    @pl.when(slab == 1)
    def _():
        begin(m.read)
        state(xa.read)

    @pl.when(slab >= 2)
    def _():
        for row, count in chunks(0, rows + MSG - 1):
            t0.write(row, stencil.coarse(m, row, count, False))

    @pl.when(slab == 2)
    def _():
        begin(lambda row, count: m.read(row, count) + stencil.coarse(t0, row, count, True))
        state(m.read)

    @pl.when(slab == 3)
    def _():
        begin(t0.read)
        state(lambda row: xa.read(row) + t0.read(row))

    pair = (t1, m)
    for step in range(STEPS - 1):
        now, later = pair[step % 2], pair[1 - step % 2]
        for row, count in chunks(0, rows + LATE - 1 - step):
            (value,) = stencil.fine((now,), row, count, True)
            if step < STEPS - 2:
                later.write(row, value)
            count = min(count, rows - row)
            if count > 0:
                value = value[: count * wide] + (total if step else now).read(row, count)
                if step < STEPS - 2:
                    total.write(row, value)
                else:
                    for r in range(count):
                        at = natural(row + r)
                        own = mid(core, value[r * wide : (r + 1) * wide])
                        gradient_out[0, at] = own / float(STEPS) + 0.5 * control_ref[0, at]


def call(kernel, outs, scratch, flops, *args, alias=None, source=pltpu.VMEM, moved=4000000):
    whole = pl.BlockSpec(memory_space=pltpu.VMEM)
    return pl.pallas_call(
        kernel,
        out_shape=[jax.ShapeDtypeStruct(shape, jnp.float32) for shape in outs],
        in_specs=[pl.BlockSpec(memory_space=pltpu.SMEM)] + [pl.BlockSpec(memory_space=source)] * (len(args) - 1),
        out_specs=[whole] * len(outs),
        scratch_shapes=[pltpu.VMEM(shape, jnp.float32) if isinstance(shape, tuple) else shape for shape in scratch],
        input_output_aliases=alias or {},
        compiler_params=pltpu.CompilerParams(vmem_limit_bytes=24 * 1024 * 1024),
        cost_estimate=pl.CostEstimate(flops=flops, bytes_accessed=moved, transcendentals=0),
    )(*args)


def swapped(block, axis):
    return lax.ppermute(block, axis, [(0, 1), (1, 0)])


def across(block, distance):
    return lax.ppermute(block, "tm", [(i, i ^ distance) for i in range(4)])


def across_turned(block, distance):
    route = [(2 * i + j, 2 * (i ^ distance) + 1 - j) for i in range(4) for j in range(2)]
    return lax.ppermute(block, ("tm", "space"), route)


def four_slabs(initial, diffusion, velocity, control, target, state_guess, adjoint_guess):
    rows, own, depth = diffusion.shape
    wide = own + SIDE
    slab, space, core = lax.axis_index("tm"), lax.axis_index("space"), lax.axis_index("yz")
    where = jnp.stack([slab, space, core]).astype(jnp.int32)
    def edge(block):
        return lax.dynamic_slice_in_dim(block, jnp.where(core == 0, own - SIDE, 0), SIDE, axis=block.ndim - 2)

    def flat(count):
        return (count * wide, depth)

    def through(fields, axis):
        got = swapped(jnp.concatenate([edge(f) for f in fields], 0), axis)
        ends = [sum(f.shape[0] for f in fields[: i + 1]) for i in range(len(fields))]
        return [got[e - f.shape[0] : e] for f, e in zip(fields, ends)]

    inputs = (diffusion, velocity, control, state_guess, adjoint_guess, initial, target)
    x_send, side_send, *inputs = call(
        functools.partial(pack_kernel, rows, own),
        [(sum(RIMS), own, depth), (len(RIMS), rows, SIDE, depth)] + [a.shape for a in inputs],
        [pltpu.SemaphoreType.DMA((len(inputs),)), pltpu.SemaphoreType.DMA((2 * len(RIMS),))],
        100000,
        where, *(pltpu.with_memory_space_constraint(a, pltpu.HBM) for a in inputs),
        source=pltpu.HBM,
        moved=1000,
    )
    diffusion, velocity, control, state_guess, adjoint_guess, initial, target = inputs
    x_here = swapped(x_send, "space")
    side = swapped(side_send, "yz")
    coefs = (len(NAMES), *flat(rows + COEF + 1))
    inner = rows - NEAR - 1
    tall = flat(rows + FAR_X + 2)
    cells = lambda count: (count, own, depth)
    coef, hist, z_a, base_a, state_a = call(
        functools.partial(inner_kernel, rows, wide),
        [coefs, (4, STEPS + 1, *flat(2)), cells(2 * inner), cells(inner + 1), cells(inner + 1)],
        [flat(rows + 2)] * 6 + [flat(rows)],
        16000000,
        where, *inputs, side,
    )
    r_a = across(z_a, 1)
    x_here, coef = lax.optimization_barrier((x_here, coef))
    x_side = swapped(edge(x_here), "yz")
    small = flat(NEAR + 5)
    count = FAR_X + FAR_E
    coef, z_b, x_out, far, base_b, state_b = call(
        functools.partial(wedge_kernel, rows, wide),
        [coefs, cells(2 * NEAR + 2), cells(count + LATE + 4 * (COEF - NEAR)), cells(count), cells(NEAR), cells(NEAR)],
        [small] * 6 + [flat(2 * NEAR)] + [flat(NEAR + 1)] * 3,
        6000000,
        where, coef, hist, diffusion, velocity, control, state_guess, adjoint_guess, target, side, z_a, x_here, x_side,
        alias={1: 0},
    )
    x_in = swapped(x_out, "space")
    xz_in = across_turned(far, 1)
    r_b = across(z_b, 1)
    za_y, ra_y = through([z_a, r_a], "yz")
    zb_y, rb_y, xr_y, xzr_y = through([z_b, r_b, jnp.concatenate([x_in[:count], x_in[count + LATE :]], 0), xz_in], "yz")
    coef, msg, h, xa, eb = call(
        functools.partial(message_kernel, rows, wide),
        [coefs, cells(rows + MSG), tall, tall, tall],
        [tall, tall],
        6000000,
        where, coef, z_a, z_b, r_a, r_b, x_in, xz_in, za_y, zb_y, ra_y, rb_y, xr_y, xzr_y,
        alias={1: 0},
    )
    msg_in = across(msg, 2)
    (base,) = call(
        functools.partial(base_kernel, rows, wide),
        [(rows + LATE, own, depth)],
        [tall, tall],
        8000000,
        where, coef, h, xa, eb, base_a, base_b, x_in,
    )
    (base_y,) = through([base], "yz")
    (msg_y,) = through([msg_in], "yz")
    return call(
        functools.partial(last_kernel, rows, wide),
        [(1, rows, own, depth), (1, rows, own, depth)],
        [tall] * 4,
        8000000,
        where, coef, msg_in, msg_y, base, base_y, xa, state_a, state_b, control,
    )


def solution(mesh):
    sizes = mesh.shape

    def local(*args):
        rows, own, depth = args[1].shape
        fits = (sizes["tm"], sizes["space"], sizes["yz"]) == (4, 2, 2)
        fits = fits and rows >= 2 * FAR_X and own % 8 == 0 and own >= SIDE and depth % 128 == 0
        return four_slabs(*args) if fits else any_mesh(*args)

    field = P(("groups", "space"), "yz", None)
    slabs = P("tm", ("groups", "space"), "yz", None)
    return jax.shard_map(
        local,
        mesh=mesh,
        in_specs=(field, field, P(None, ("groups", "space"), "yz", None), slabs, slabs, slabs, slabs),
        out_specs=(slabs, slabs),
        check_vma=False,
    )
```

```python
import functools

import jax
import jax.numpy as jnp
from jax import lax
from jax.experimental import pallas as pl
from jax.experimental.pallas import tpu as pltpu
from jax.sharding import PartitionSpec as P

STEPS = 6
SIDE = 8
NEAR = 6
LATE = 5
MSG = 7
FAR_X = 10
FAR_E = 7
COEF = FAR_X - 1
RIMS = (NEAR, NEAR, NEAR, NEAR, NEAR, NEAR, NEAR + 1, 1)
STARTS = tuple(sum(RIMS[:i]) for i in range(len(RIMS)))


def extended(array, sides, width):
    for axis, dim in sides:
        peers, length = (lax.axis_size(axis), array.shape[dim])
        up = [(i, (i + 1) % peers) for i in range(peers - 1)]
        down = [(j, i) for i, j in up]
        last = lax.slice_in_dim(array, length - width, length, axis=dim)
        first = lax.slice_in_dim(array, 0, width, axis=dim)
        before = lax.ppermute(last, axis, up)
        after = lax.ppermute(first, axis, down)
        array = jnp.concatenate([before, array, after], axis=dim)
    return array


def passed_along(block, axis, distance):
    devices = range(lax.axis_size(axis))
    route = [(i - distance, i) for i in devices if i - distance in devices]
    return lax.ppermute(block, axis, route)


def depth_pad(field):
    return jnp.pad(field, ((0, 0), (0, 0), (1, 1)))


def local_map(padded, coefficients, factor, adjoint):
    centre = padded[1:-1, 1:-1, :]
    if adjoint:
        spread = coefficients[0] * padded
        carried = coefficients[1:4] * padded
        inner_spread = spread[1:-1, 1:-1, :]
        deep = depth_pad(inner_spread)
        laplace = (
            spread[2:, 1:-1, :]
            + spread[:-2, 1:-1, :]
            + spread[1:-1, 2:, :]
            + spread[1:-1, :-2, :]
            + deep[:, :, 2:]
            + deep[:, :, :-2]
            - 6.0 * inner_spread
        )
        deep_carry = depth_pad(carried[2, 1:-1, 1:-1, :])
        transport = (
            carried[0, 2:, 1:-1, :]
            - carried[0, :-2, 1:-1, :]
            + (carried[1, 1:-1, 2:, :] - carried[1, 1:-1, :-2, :])
            + (deep_carry[:, :, 2:] - deep_carry[:, :, :-2])
        )
        return (centre + factor * (laplace + transport)) * coefficients[4, 1:-1, 1:-1, :]
    inner = coefficients[:, 1:-1, 1:-1, :]
    deep = depth_pad(centre)
    laplace = (
        padded[2:, 1:-1, :]
        + padded[:-2, 1:-1, :]
        + padded[1:-1, 2:, :]
        + padded[1:-1, :-2, :]
        + deep[:, :, 2:]
        + deep[:, :, :-2]
        - 6.0 * centre
    )
    transport = (
        inner[1] * (padded[2:, 1:-1, :] - padded[:-2, 1:-1, :])
        + inner[2] * (padded[1:-1, 2:, :] - padded[1:-1, :-2, :])
        + inner[3] * (deep[:, :, 2:] - deep[:, :, :-2])
    )
    return centre + factor * (inner[0] * laplace - transport)


def halo_cells(field):
    return extended(field, (("space", 0), ("yz", 1)), 1)


def coarse_chain(residual, near_coefficients, adjoint, direction):
    factor = float(STEPS)

    def one_turn(turn_index, correction):
        moved = local_map(halo_cells(correction), near_coefficients, factor, adjoint)
        arrived = passed_along(moved, "tm", direction)
        return residual + arrived

    return lax.fori_loop(0, lax.axis_size("tm") - 1, one_turn, residual)


def any_mesh(initial, diffusion, velocity, control, target, state_guess, adjoint_guess):
    source = control[0]
    guess_state = state_guess[0]
    guess_adjoint = adjoint_guess[0]
    stacked = jnp.concatenate([diffusion[None], velocity, jnp.ones_like(diffusion)[None]], 0)
    near_coefficients = extended(stacked, (("space", 1), ("yz", 2)), 1)
    arrived = passed_along(guess_state, "tm", 1)
    fine = jnp.where(lax.axis_index("tm") == 0, initial, arrived)
    sweep = guess_adjoint
    for step_index in range(STEPS):
        fine = local_map(halo_cells(fine), near_coefficients, 1.0, False) + source
    for step_index in range(STEPS):
        sweep = local_map(halo_cells(sweep), near_coefficients, 1.0, True)
    state_residual = fine - guess_state
    state_new = guess_state + coarse_chain(state_residual, near_coefficients, False, 1)
    from_next = passed_along(sweep, "tm", -1)
    adjoint_residual = from_next + state_new - target[0] - guess_adjoint
    multiplier = guess_adjoint + coarse_chain(adjoint_residual, near_coefficients, True, -1)
    running_sum = multiplier
    for step_index in range(STEPS - 1):
        multiplier = local_map(halo_cells(multiplier), near_coefficients, 1.0, True)
        running_sum = running_sum + multiplier
    gradient = running_sum / float(STEPS) + 0.5 * source
    return (state_new[None], gradient[None])


NAMES = ("c0", "xp", "xm", "yp", "ym", "zp", "zm", "qyp", "qym", "qzp", "qzm")
CHUNK = 2


class Rows:
    def __init__(self, ref, wide, first=-1):
        self.ref, self.wide, self.first = ref, wide, first

    def read(self, row, count=1):
        return self.ref[pl.ds((row - self.first) * self.wide, count * self.wide)]

    def write(self, row, value):
        self.ref[pl.ds((row - self.first) * self.wide, value.shape[0])] = value


def shifted(value, step):
    return pltpu.roll(value, step % value.shape[1], 1)


def next_cells(value, step):
    return pltpu.roll(value, step % value.shape[0], 0)


class Stencil:
    def __init__(self, ref, wide):
        self.at = {name: Rows(ref.at[i], wide) for i, name in enumerate(NAMES)}

    def fill(self, row, raw, space, core):
        d, u0, u1, u2 = raw
        u0 = u0 * (1 - 2 * space).astype(jnp.float32)
        cell = lax.broadcasted_iota(jnp.int32, d.shape, 0)
        depth = lax.broadcasted_iota(jnp.int32, d.shape, 1)
        top = (cell == d.shape[0] - 1) & (core == 1)
        bottom = (cell == 0) & (core == 0)
        last, first = depth == d.shape[1] - 1, depth == 0
        zero = jnp.zeros_like(d)
        values = {
            "c0": 1.0 - 6.0 * d,
            "xp": d - u0,
            "xm": d + u0,
            "yp": jnp.where(top, zero, d - u1),
            "ym": jnp.where(bottom, zero, d + u1),
            "zp": jnp.where(last, zero, d - u2),
            "zm": jnp.where(first, zero, d + u2),
            "qyp": jnp.where(top, zero, next_cells(d + u1, -1)),
            "qym": jnp.where(bottom, zero, next_cells(d - u1, 1)),
            "qzp": jnp.where(last, zero, shifted(d + u2, -1)),
            "qzm": jnp.where(first, zero, shifted(d - u2, 1)),
        }
        for name in NAMES:
            self.at[name].write(row, values[name])

    def edge(self):
        for name in NAMES:
            rows = self.at[name]
            rows.write(-1, jnp.zeros((rows.wide, rows.ref.shape[-1]), jnp.float32))

    def terms(self, fields, row, count, adjoint):
        at = self.at
        if adjoint:
            up, low, ends = at["xm"].read(row + 1, count), at["xp"].read(row - 1, count), ("qyp", "qym", "qzp", "qzm")
        else:
            up, low, ends = at["xp"].read(row, count), at["xm"].read(row, count), ("yp", "ym", "zp", "zm")
        yp, ym, zp, zm = (at[n].read(row, count) for n in ends)
        same = at["c0"].read(row, count)
        result = []
        for v in fields:
            c = v.read(row, count)
            around = up * v.read(row + 1, count) + low * v.read(row - 1, count)
            around = around + (yp * next_cells(c, -1) + ym * next_cells(c, 1))
            around = around + (zp * shifted(c, -1) + zm * shifted(c, 1))
            result.append((around, c, same * c))
        return result

    def fine(self, fields, row, count, adjoint):
        return [own + around for around, c, own in self.terms(fields, row, count, adjoint)]

    def coarse(self, v, row, count, adjoint):
        ((around, c, own),) = self.terms([v], row, count, adjoint)
        return c + float(STEPS) * (around + (own - c))


def chunks(start, stop, size=CHUNK):
    return [(row, min(size, stop - row)) for row in range(start, stop, size)]


def joined(core, own, side):
    return jnp.where(core == 1, jnp.concatenate([side, own], 0), jnp.concatenate([own, side], 0))


def mid(core, cells):
    return jnp.where(core == 1, cells[SIDE:], cells[:-SIDE])


def zeros(rows):
    return jnp.zeros((rows.wide, rows.ref.shape[-1]), jnp.float32)


def pack_kernel(rows, own, where_ref, d_ref, u_ref, control_ref, sg_ref, ag_ref, initial_ref, target_ref,
                x_out, side_out, more_out, rims, sides, sem):
    slab, space, core = where_ref[0], where_ref[1], where_ref[2]
    fields = (d_ref, u_ref.at[0], u_ref.at[1], u_ref.at[2], control_ref.at[0], sg_ref.at[0], None, target_ref.at[0])
    starts = (ag_ref.at[0], initial_ref)
    beside = pl.multiple_of(jnp.where(core == 0, own - SIDE, 0), SIDE)
    copies = []

    def bring(source, to):
        copies.append(pltpu.make_async_copy(source, to, sem.at[len(copies)]))
        copies[-1].start()

    def rim(i):
        return pl.ds(jnp.where(space == 0, rows - RIMS[i], 0), RIMS[i])

    def edge(field):
        return field.at[:, pl.ds(beside, SIDE)]

    for i, field in enumerate(starts):
        bring(field.at[rim(6)], rims.at[i])
        bring(edge(field), sides.at[i])
    for i, field in enumerate(fields):
        if field is not None:
            bring(field.at[rim(i)], x_out.at[pl.ds(STARTS[i], RIMS[i])])
            bring(edge(field), side_out.at[i])
    kept = COEF - NEAR
    for i, field in enumerate(fields[:4]):
        bring(field.at[pl.ds(jnp.where(space == 0, rows - COEF, NEAR), kept)], more_out.at[pl.ds(i * kept, kept)])
    for copy in copies:
        copy.wait()
    x_out[pl.ds(STARTS[6], RIMS[6])] = jnp.where(slab == 0, rims[1], rims[0])
    side_out[6] = jnp.where(slab == 0, sides[1], sides[0])


def inner_kernel(rows, wide, where_ref, d_hbm, u_hbm, control_hbm, sg_hbm, ag_hbm, initial_hbm, target_hbm, side_ref,
                 coef_out, hist_out, kept_out, z_out, base_out, state_out, control_ref,
                 c_a, c_b, g_a, g_b, s_a, s_b, con_ref, d_ref, u_ref, sg_ref, ag_ref, initial_ref, target_ref, sem):
    ins = (d_hbm, u_hbm, control_hbm, sg_hbm, ag_hbm, initial_hbm, target_hbm)
    outs = (d_ref, u_ref, control_ref, sg_ref, ag_ref, initial_ref, target_ref)
    copies = [pltpu.make_async_copy(a, b, sem.at[i]) for i, (a, b) in enumerate(zip(ins, outs))]
    for copy in copies:
        copy.start()
    for copy in copies:
        copy.wait()
    slab, space, core = where_ref[0], where_ref[1], where_ref[2]
    first = slab == 0
    c, g, s = ([Rows(r, wide) for r in pair] for pair in ((c_a, c_b), (g_a, g_b), (s_a, s_b)))
    con = Rows(con_ref, wide, 0)
    for field in (*c, *g, *s):
        field.write(-1, zeros(field))
    stencil = Stencil(coef_out, wide)
    stencil.edge()

    def natural(row):
        return jnp.where(space == 1, rows - 1 - row, row)

    def mine(i, own, row):
        return joined(core, own, side_ref[i, natural(row)])

    for row in range(rows):
        at = natural(row)
        stencil.fill(row, [mine(0, d_ref[at], row)] + [mine(1 + i, u_ref[i, at], row) for i in range(3)], space, core)
        con.write(row, mine(4, control_ref[0, at], row))
        g[0].write(row, mine(5, sg_ref[0, at], row))
        start = mine(6, initial_ref[at], row)
        c[0].write(row, jnp.where(first, start, jnp.zeros_like(start)))
        s[0].write(row, mine(6, ag_ref[0, at], row))

    low = rows - STEPS
    for row in range(low, rows):
        values = (con.read(row), g[0].read(row), s[0].read(row), mine(7, target_ref[0, natural(row)], row))
        for i, value in enumerate(values):
            kept_out[i, pl.ds((row - low) * wide, wide)] = value

    def keep(level, fields):
        for i, field in enumerate(fields):
            hist_out[i, level] = field.read(rows - 2 - level, 2)

    keep(0, (c[0], g[0], s[0]))
    for step in range(STEPS):
        now, later = step % 2, 1 - step % 2
        for row, count in chunks(0, rows - 1 - step):
            to_c, to_g = stencil.fine((c[now], g[now]), row, count, False)
            (to_s,) = stencil.fine((s[now],), row, count, True)
            c[later].write(row, to_c + con.read(row, count))
            g[later].write(row, to_g)
            s[later].write(row, to_s)
        if step < STEPS - 1:
            keep(step + 1, (c[later], g[later], s[later]))
    cc, dd = c[1], s[1]
    ready = rows - STEPS
    for row in range(ready):
        sg = mine(5, sg_ref[0, natural(row)], row)
        gap = c[0].read(row) - sg
        ag = mine(6, ag_ref[0, natural(row)], row)
        state = sg + gap
        rest = state - mine(7, target_ref[0, natural(row)], row) - ag
        cc.write(row, gap)
        dd.write(row, rest)
        state_out[row] = mid(core, state)
        base_out[row] = mid(core, ag + rest)
    keep(STEPS, (cc, g[0], s[0], dd))
    for row, count in chunks(0, ready - 1):
        x = g[0].read(row, count) + stencil.coarse(cc, row, count, False)
        e = s[0].read(row, count) + stencil.coarse(dd, row, count, True)
        for r in range(count):
            z_out[row + r] = mid(core, x[r * wide : (r + 1) * wide])
            z_out[ready - 1 + row + r] = mid(core, e[r * wide : (r + 1) * wide])


def wedge_kernel(rows, wide, where_ref, coef_in, hist_ref, kept_ref, more_ref, z_ref, xr_ref, ys_ref,
                 coef_out, z_out, x_out, far_out, base_out, state_out, c_a, c_b, g_a, g_b, s_a, s_b, con_ref):
    slab, space, core = where_ref[0], where_ref[1], where_ref[2]
    first = slab == 0
    flip = space == 1
    c, g, s = (
        [[Rows(r, wide, rows - 2 - level) for r in pair] for level in range(STEPS + 1)]
        for pair in ((c_a, c_b), (g_a, g_b), (s_a, s_b))
    )
    at_level = lambda field, level: field[level][level % 2]
    low = rows - STEPS
    con = Rows(con_ref, wide, low)
    con.write(low, kept_ref[0])
    stencil = Stencil(coef_out, wide)

    def natural(row):
        return jnp.where(flip, rows - 1 - row, row)

    def rim(i, j):
        at = STARTS[i] + jnp.where(flip, RIMS[i] - 1 - j, j)
        return joined(core, xr_ref[at], ys_ref[at])

    for j in range(NEAR):
        stencil.fill(rows + j, [rim(i, j) for i in range(4)], space, core)
    for j in range(NEAR):
        con.write(rows + j, rim(4, j))
    for j in range(NEAR + 1):
        start = rim(6, j)
        c[0][0].write(rows + j, jnp.where(first, start, jnp.zeros_like(start)))
        if j < NEAR:
            s[0][0].write(rows + j, start)
            g[0][0].write(rows + j, rim(5, j))

    def restore(level, fields):
        for i, field in enumerate(fields):
            field.write(rows - 2 - level, hist_ref[i, level])

    restore(0, (c[0][0], g[0][0], s[0][0]))
    for level in range(STEPS):
        row = rows - 1 - level
        nc, ng, ns = (at_level(f, level) for f in (c, g, s))
        lc, lg, ls = (at_level(f, level + 1) for f in (c, g, s))
        for r, count in chunks(row, row + NEAR):
            to_c, to_g = stencil.fine((nc, ng), r, count, False)
            (to_s,) = stencil.fine((ns,), r, count, True)
            lc.write(r, to_c + con.read(r, count))
            lg.write(r, to_g)
            ls.write(r, to_s)
        (to_c,) = stencil.fine((nc,), row + NEAR, 1, False)
        lc.write(row + NEAR, to_c + con.read(row + NEAR))
        if level < STEPS - 1:
            restore(level + 1, (lc, lg, ls))
    fc, fg, fs = (at_level(f, STEPS) for f in (c, g, s))
    cc, dd = c[STEPS][1], s[STEPS][1]
    restore(STEPS, (cc, fg, fs, dd))
    count = NEAR + 1
    sg = jnp.concatenate([kept_ref[1], rim(5, 0)], 0)
    gap = fc.read(low, count) - sg
    state = sg + gap
    ag = jnp.concatenate([kept_ref[2], rim(6, 0)], 0)
    rest = state - jnp.concatenate([kept_ref[3], rim(7, 0)], 0) - ag
    cc.write(low, gap)
    dd.write(low, rest)
    base = ag + rest

    def cells(value, r):
        return mid(core, value[r * wide : (r + 1) * wide])

    for r in range(NEAR):
        state_out[r] = cells(state, r)
        base_out[r] = cells(base, r)
    for r in range(count):
        row = low - 1 + r
        x_row = mid(core, fg.read(row) + stencil.coarse(cc, row, 1, False))
        e_row = mid(core, fs.read(row) + stencil.coarse(dd, row, 1, True))
        z_out[r] = x_row
        z_out[count + r] = e_row
        for out in (x_out, far_out):
            out[count - 1 - r] = x_row
            out[FAR_X + count - 1 - r] = e_row
    for j in range(count, FAR_X):
        x_row = z_ref[rows - 1 - j]
        for out in (x_out, far_out):
            out[j] = x_row
    late = FAR_X + FAR_E
    for j in range(LATE):
        x_out[late + j] = cells(base, NEAR - 1 - j)
    kept = COEF - NEAR
    for j in range(kept):
        at = jnp.where(flip, j, kept - 1 - j)
        for i in range(4):
            x_out[late + LATE + i * kept + j] = more_ref[i * kept + at]


def sorted_pair(core, odd, lower, higher, row, mine, mine_y, other, other_y, at):
    a, b = joined(core, mine[at], mine_y[at]), joined(core, other[at], other_y[at])
    lower.write(row, jnp.where(odd, b, a))
    higher.write(row, jnp.where(odd, a, b))


def message_kernel(rows, wide, where_ref, coef_in, za, zb, ra, rb, xr, xzr, za_y, zb_y, ra_y, rb_y, xr_y, xzr_y,
                   coef_out, msg_out, h_out, xa_out, eb_out, xb_s, ea_s):
    slab, space, core = where_ref[0], where_ref[1], where_ref[2]
    odd = slab % 2 == 1
    upper = slab >= 2
    stencil = Stencil(coef_out, wide)
    late = FAR_X + FAR_E
    for j in range(COEF - NEAR):
        at = [late + i * (COEF - NEAR) + j for i in range(4)]
        stencil.fill(rows + NEAR + j, [joined(core, xr[r + LATE], xr_y[r]) for r in at], space, core)
    xa, xb, ea, eb, h = fields = [Rows(r, wide) for r in (xa_out, xb_s, ea_s, eb_out, h_out)]
    for field in fields:
        field.write(-1, zeros(field))
    inner = rows - NEAR - 1
    for row in range(inner):
        sorted_pair(core, odd, xa, xb, row, za, za_y, ra, ra_y, row)
        sorted_pair(core, odd, ea, eb, row, za, za_y, ra, ra_y, inner + row)
    for row in range(inner, rows):
        sorted_pair(core, odd, xa, xb, row, zb, zb_y, rb, rb_y, row - inner)
        sorted_pair(core, odd, ea, eb, row, zb, zb_y, rb, rb_y, rows - inner + row - inner)
    for j in range(FAR_X):
        sorted_pair(core, odd, xa, xb, rows + j, xr, xr_y, xzr, xzr_y, j)
    for j in range(FAR_E):
        sorted_pair(core, odd, ea, eb, rows + j, xr, xr_y, xzr, xzr_y, FAR_X + j)

    def send(row, count, value):
        for r in range(row, min(row + count, rows + MSG)):
            msg_out[r] = mid(core, value[(r - row) * wide : (r - row + 1) * wide])

    @pl.when(jnp.logical_not(upper))
    def _():
        for row, count in chunks(0, rows + FAR_X - 1):
            value = xb.read(row, count) + stencil.coarse(xa, row, count, False)
            h.write(row, value)
            send(row, count, value)

    @pl.when(upper)
    def _():
        for row, count in chunks(0, rows + FAR_E):
            h.write(row, eb.read(row, count) + stencil.coarse(xa, row, count, True))
        for row, count in chunks(0, rows + FAR_E - 1):
            send(row, count, ea.read(row, count) + stencil.coarse(h, row, count, True))
        send(rows + FAR_E - 1, 1, zeros(ea))


def base_kernel(rows, wide, where_ref, coef_ref, h_ref, xa_ref, eb_ref, start_a, start_b, start_x, base_out, t1_s, t2_s):
    slab, core = where_ref[0], where_ref[2]
    odd = slab % 2 == 1
    upper = slab >= 2
    stencil = Stencil(coef_ref, wide)
    h, xa, eb, t1, t2 = (Rows(r, wide) for r in (h_ref, xa_ref, eb_ref, t1_s, t2_s))
    for field in (t1, t2):
        field.write(-1, zeros(field))

    def start(row):
        if row >= rows:
            return start_x[FAR_X + FAR_E + row - rows]
        return start_a[row] if row < start_a.shape[0] else start_b[row - start_a.shape[0]]

    def put(source):
        for row in range(rows + LATE):
            base_out[row] = start(row) + mid(core, source.read(row))

    @pl.when(jnp.logical_not(upper))
    def _():
        for row, count in chunks(0, rows + FAR_X - 2):
            t1.write(row, stencil.coarse(h, row, count, False))
        for row, count in chunks(0, rows + FAR_X - 3):
            t2.write(row, h.read(row, count) + stencil.coarse(t1, row, count, True))
        for row, count in chunks(0, rows + FAR_X - 4):
            t1.write(row, xa.read(row, count) + stencil.coarse(t2, row, count, True))

        @pl.when(odd)
        def _():
            put(t1)

        @pl.when(jnp.logical_not(odd))
        def _():
            for row, count in chunks(0, rows + LATE):
                t2.write(row, eb.read(row, count) + stencil.coarse(t1, row, count, True))
            put(t2)

    @pl.when(upper & odd)
    def _():
        put(xa)

    @pl.when(upper & jnp.logical_not(odd))
    def _():
        put(h)


def last_kernel(rows, wide, where_ref, coef_ref, msg, msg_y, base, base_y, xa_ref, state_a, state_b, control_ref,
                state_hbm, gradient_hbm, m_s, t0_s, t1_s, total_s, state_out, gradient_out, sem):
    slab, space, core = where_ref[0], where_ref[1], where_ref[2]
    stencil = Stencil(coef_ref, wide)
    m, t0, t1, total, xa = (Rows(r, wide) for r in (m_s, t0_s, t1_s, total_s, xa_ref))
    for field in (m, t0, t1):
        field.write(-1, zeros(field))

    def natural(row):
        return jnp.where(space == 1, rows - 1 - row, row)

    def state(came):
        for row in range(rows):
            before = state_a[row] if row < state_a.shape[0] else state_b[row - state_a.shape[0]]
            state_out[natural(row)] = before + mid(core, came(row)) if came else before

    def begin(extra):
        for row, count in chunks(0, rows + LATE):
            ready = jnp.concatenate([joined(core, base[r], base_y[r]) for r in range(row, row + count)], 0)
            t1.write(row, ready + extra(row, count))

    for row in range(rows + MSG):
        m.write(row, joined(core, msg[row], msg_y[row]))

    @pl.when(slab == 0)
    def _():
        begin(lambda row, count: stencil.coarse(m, row, count, True))
        state(None)

    @pl.when(slab == 1)
    def _():
        begin(m.read)
        state(xa.read)

    @pl.when(slab >= 2)
    def _():
        for row, count in chunks(0, rows + MSG - 1):
            t0.write(row, stencil.coarse(m, row, count, False))

    @pl.when(slab == 2)
    def _():
        begin(lambda row, count: m.read(row, count) + stencil.coarse(t0, row, count, True))
        state(m.read)

    @pl.when(slab == 3)
    def _():
        begin(t0.read)
        state(lambda row: xa.read(row) + t0.read(row))

    copies = [pltpu.make_async_copy(state_out, state_hbm.at[0], sem.at[0])]
    copies[0].start()
    pair = (t1, m)
    for step in range(STEPS - 1):
        now, later = pair[step % 2], pair[1 - step % 2]
        for row, count in chunks(0, rows + LATE - 1 - step):
            (value,) = stencil.fine((now,), row, count, True)
            if step < STEPS - 2:
                later.write(row, value)
            count = min(count, rows - row)
            if count > 0:
                value = value[: count * wide] + (total if step else now).read(row, count)
                if step < STEPS - 2:
                    total.write(row, value)
                else:
                    for r in range(count):
                        at = natural(row + r)
                        own = mid(core, value[r * wide : (r + 1) * wide])
                        gradient_out[at] = own / float(STEPS) + 0.5 * control_ref[0, at]
                    if (row + count) % 8 and row + count < rows:
                        continue
                    begin_at, size = row + count - 8, 8
                    part = pl.ds(jnp.where(space == 1, rows - begin_at - size, begin_at), size)
                    copies.append(pltpu.make_async_copy(gradient_out.at[part], gradient_hbm.at[0, part], sem.at[len(copies)]))
                    copies[-1].start()
    for copy in copies:
        copy.wait()


def call(kernel, outs, scratch, *args, alias=None, in_hbm=0, target=pltpu.VMEM):
    return pl.pallas_call(
        kernel,
        out_shape=[jax.ShapeDtypeStruct(shape, jnp.float32) for shape in outs],
        in_specs=[pl.BlockSpec(memory_space=pltpu.SMEM)]
        + [pl.BlockSpec(memory_space=pltpu.HBM if i < in_hbm else pltpu.VMEM) for i in range(len(args) - 1)],
        out_specs=[pl.BlockSpec(memory_space=target)] * len(outs),
        scratch_shapes=[pltpu.VMEM(shape, jnp.float32) if isinstance(shape, tuple) else shape for shape in scratch],
        input_output_aliases=alias or {},
        compiler_params=pltpu.CompilerParams(vmem_limit_bytes=24 * 1024 * 1024),
        cost_estimate=pl.CostEstimate(flops=1000, bytes_accessed=1000, transcendentals=0),
    )(*args)


def swapped(block, axis):
    return lax.ppermute(block, axis, [(0, 1), (1, 0)])


def across(block, distance):
    return lax.ppermute(block, "tm", [(i, i ^ distance) for i in range(4)])


def across_turned(block, distance):
    route = [(2 * i + j, 2 * (i ^ distance) + 1 - j) for i in range(4) for j in range(2)]
    return lax.ppermute(block, ("tm", "space"), route)


def four_slabs(initial, diffusion, velocity, control, target, state_guess, adjoint_guess):
    rows, own, depth = diffusion.shape
    wide = own + SIDE
    slab, space, core = lax.axis_index("tm"), lax.axis_index("space"), lax.axis_index("yz")
    where = jnp.stack([slab, space, core]).astype(jnp.int32)
    def edge(block):
        return lax.dynamic_slice_in_dim(block, jnp.where(core == 0, own - SIDE, 0), SIDE, axis=block.ndim - 2)

    def flat(count):
        return (count * wide, depth)

    def through(fields, axis):
        got = swapped(jnp.concatenate([edge(f) for f in fields], 0), axis)
        ends = [sum(f.shape[0] for f in fields[: i + 1]) for i in range(len(fields))]
        return [got[e - f.shape[0] : e] for f, e in zip(fields, ends)]

    inputs = (diffusion, velocity, control, state_guess, adjoint_guess, initial, target)
    shapes = [a.shape for a in inputs]
    inputs = [pltpu.with_memory_space_constraint(a, pltpu.HBM) for a in inputs]
    cells = lambda count: (count, own, depth)
    edges = (rows, SIDE, depth)
    kept = COEF - NEAR
    x_send, side_send, more = call(
        functools.partial(pack_kernel, rows, own),
        [cells(sum(RIMS)), (len(RIMS), *edges), cells(4 * kept)],
        [(2, *cells(RIMS[6])), (2, *edges), pltpu.SemaphoreType.DMA((2 * len(RIMS) + 6,))],
        where, *inputs,
        in_hbm=len(inputs),
    )
    x_here = swapped(x_send, "space")
    side = swapped(side_send, "yz")
    coefs = (len(NAMES), *flat(rows + COEF + 1))
    inner = rows - NEAR - 1
    tall = flat(rows + FAR_X + 2)
    loaded = [shape for i, shape in enumerate(shapes) if i != 2]
    coef, hist, last, z_a, base_a, state_a, control = call(
        functools.partial(inner_kernel, rows, wide),
        [coefs, (4, STEPS + 1, *flat(2)), (4, *flat(NEAR)), cells(2 * inner), cells(inner + 1), cells(inner + 1), shapes[2]],
        [flat(rows + 2)] * 6 + [flat(rows)] + loaded + [pltpu.SemaphoreType.DMA((len(inputs),))],
        where, *inputs, side,
        in_hbm=len(inputs),
    )
    r_a = across(z_a, 1)
    x_here, coef = lax.optimization_barrier((x_here, coef))
    x_side = swapped(edge(x_here), "yz")
    count = FAR_X + FAR_E
    coef, z_b, x_out, far, base_b, state_b = call(
        functools.partial(wedge_kernel, rows, wide),
        [coefs, cells(2 * NEAR + 2), cells(count + LATE + 4 * kept), cells(count), cells(NEAR), cells(NEAR)],
        [flat(NEAR + 5)] * 6 + [flat(2 * NEAR)],
        where, coef, hist, last, more, z_a, x_here, x_side,
        alias={1: 0},
    )
    x_in = swapped(x_out, "space")
    xz_in = across_turned(far, 1)
    r_b = across(z_b, 1)
    za_y, ra_y = through([z_a, r_a], "yz")
    zb_y, rb_y, xr_y, xzr_y = through([z_b, r_b, jnp.concatenate([x_in[:count], x_in[count + LATE :]], 0), xz_in], "yz")
    coef, msg, h, xa, eb = call(
        functools.partial(message_kernel, rows, wide),
        [coefs, cells(rows + MSG), tall, tall, tall],
        [tall, tall],
        where, coef, z_a, z_b, r_a, r_b, x_in, xz_in, za_y, zb_y, ra_y, rb_y, xr_y, xzr_y,
        alias={1: 0},
    )
    msg_in = across(msg, 3)
    (base,) = call(
        functools.partial(base_kernel, rows, wide),
        [cells(rows + LATE)],
        [tall, tall],
        where, coef, h, xa, eb, base_a, base_b, x_in,
    )
    (base_y,) = through([base], "yz")
    (msg_y,) = through([msg_in], "yz")
    return call(
        functools.partial(last_kernel, rows, wide),
        [(1, *cells(rows)), (1, *cells(rows))],
        [tall] * 4 + [cells(rows)] * 2 + [pltpu.SemaphoreType.DMA((1 + rows // 8,))],
        where, coef, msg_in, msg_y, base, base_y, xa, state_a, state_b, control,
        target=pltpu.HBM,
    )


def solution(mesh):
    sizes = mesh.shape

    def local(*args):
        rows, own, depth = args[1].shape
        fits = (sizes["tm"], sizes["space"], sizes["yz"]) == (4, 2, 2)
        fits = fits and rows >= 2 * FAR_X and rows % 8 == 0 and own % 8 == 0 and own >= SIDE and depth % 128 == 0
        return four_slabs(*args) if fits else any_mesh(*args)

    field = P(("groups", "space"), "yz", None)
    slabs = P("tm", ("groups", "space"), "yz", None)
    return jax.shard_map(
        local,
        mesh=mesh,
        in_specs=(field, field, P(None, ("groups", "space"), "yz", None), slabs, slabs, slabs, slabs),
        out_specs=(slabs, slabs),
        check_vma=False,
    )
```

```python
import functools

import jax
import jax.numpy as jnp
from jax import lax
from jax.experimental import pallas as pl
from jax.experimental.pallas import tpu as pltpu
from jax.sharding import PartitionSpec as P

STEPS = 6
SIDE = 8
NEAR = 6
LATE = 5
MSG = 7
FAR_X = 10
FAR_E = 7
COEF = FAR_X - 1
RIMS = (NEAR, NEAR, NEAR, NEAR, NEAR, NEAR, NEAR + 1, 1)
STARTS = tuple(sum(RIMS[:i]) for i in range(len(RIMS)))


def extended(array, sides, width):
    for axis, dim in sides:
        peers, length = (lax.axis_size(axis), array.shape[dim])
        up = [(i, (i + 1) % peers) for i in range(peers - 1)]
        down = [(j, i) for i, j in up]
        last = lax.slice_in_dim(array, length - width, length, axis=dim)
        first = lax.slice_in_dim(array, 0, width, axis=dim)
        before = lax.ppermute(last, axis, up)
        after = lax.ppermute(first, axis, down)
        array = jnp.concatenate([before, array, after], axis=dim)
    return array


def passed_along(block, axis, distance):
    devices = range(lax.axis_size(axis))
    route = [(i - distance, i) for i in devices if i - distance in devices]
    return lax.ppermute(block, axis, route)


def depth_pad(field):
    return jnp.pad(field, ((0, 0), (0, 0), (1, 1)))


def local_map(padded, coefficients, factor, adjoint):
    centre = padded[1:-1, 1:-1, :]
    if adjoint:
        spread = coefficients[0] * padded
        carried = coefficients[1:4] * padded
        inner_spread = spread[1:-1, 1:-1, :]
        deep = depth_pad(inner_spread)
        laplace = (
            spread[2:, 1:-1, :]
            + spread[:-2, 1:-1, :]
            + spread[1:-1, 2:, :]
            + spread[1:-1, :-2, :]
            + deep[:, :, 2:]
            + deep[:, :, :-2]
            - 6.0 * inner_spread
        )
        deep_carry = depth_pad(carried[2, 1:-1, 1:-1, :])
        transport = (
            carried[0, 2:, 1:-1, :]
            - carried[0, :-2, 1:-1, :]
            + (carried[1, 1:-1, 2:, :] - carried[1, 1:-1, :-2, :])
            + (deep_carry[:, :, 2:] - deep_carry[:, :, :-2])
        )
        return (centre + factor * (laplace + transport)) * coefficients[4, 1:-1, 1:-1, :]
    inner = coefficients[:, 1:-1, 1:-1, :]
    deep = depth_pad(centre)
    laplace = (
        padded[2:, 1:-1, :]
        + padded[:-2, 1:-1, :]
        + padded[1:-1, 2:, :]
        + padded[1:-1, :-2, :]
        + deep[:, :, 2:]
        + deep[:, :, :-2]
        - 6.0 * centre
    )
    transport = (
        inner[1] * (padded[2:, 1:-1, :] - padded[:-2, 1:-1, :])
        + inner[2] * (padded[1:-1, 2:, :] - padded[1:-1, :-2, :])
        + inner[3] * (deep[:, :, 2:] - deep[:, :, :-2])
    )
    return centre + factor * (inner[0] * laplace - transport)


def halo_cells(field):
    return extended(field, (("space", 0), ("yz", 1)), 1)


def coarse_chain(residual, near_coefficients, adjoint, direction):
    factor = float(STEPS)

    def one_turn(turn_index, correction):
        moved = local_map(halo_cells(correction), near_coefficients, factor, adjoint)
        arrived = passed_along(moved, "tm", direction)
        return residual + arrived

    return lax.fori_loop(0, lax.axis_size("tm") - 1, one_turn, residual)


def any_mesh(initial, diffusion, velocity, control, target, state_guess, adjoint_guess):
    source = control[0]
    guess_state = state_guess[0]
    guess_adjoint = adjoint_guess[0]
    stacked = jnp.concatenate([diffusion[None], velocity, jnp.ones_like(diffusion)[None]], 0)
    near_coefficients = extended(stacked, (("space", 1), ("yz", 2)), 1)
    arrived = passed_along(guess_state, "tm", 1)
    fine = jnp.where(lax.axis_index("tm") == 0, initial, arrived)
    sweep = guess_adjoint
    for step_index in range(STEPS):
        fine = local_map(halo_cells(fine), near_coefficients, 1.0, False) + source
    for step_index in range(STEPS):
        sweep = local_map(halo_cells(sweep), near_coefficients, 1.0, True)
    state_residual = fine - guess_state
    state_new = guess_state + coarse_chain(state_residual, near_coefficients, False, 1)
    from_next = passed_along(sweep, "tm", -1)
    adjoint_residual = from_next + state_new - target[0] - guess_adjoint
    multiplier = guess_adjoint + coarse_chain(adjoint_residual, near_coefficients, True, -1)
    running_sum = multiplier
    for step_index in range(STEPS - 1):
        multiplier = local_map(halo_cells(multiplier), near_coefficients, 1.0, True)
        running_sum = running_sum + multiplier
    gradient = running_sum / float(STEPS) + 0.5 * source
    return (state_new[None], gradient[None])


NAMES = ("c0", "xp", "xm", "yp", "ym", "zp", "zm", "qyp", "qym", "qzp", "qzm")
CHUNK = 2


class Rows:
    def __init__(self, ref, wide, first=-1):
        self.ref, self.wide, self.first = ref, wide, first

    def read(self, row, count=1):
        return self.ref[pl.ds((row - self.first) * self.wide, count * self.wide)]

    def write(self, row, value):
        self.ref[pl.ds((row - self.first) * self.wide, value.shape[0])] = value


def shifted(value, step):
    return pltpu.roll(value, step % value.shape[1], 1)


def next_cells(value, step):
    return pltpu.roll(value, step % value.shape[0], 0)


class Stencil:
    def __init__(self, ref, wide):
        self.at = {name: Rows(ref.at[i], wide) for i, name in enumerate(NAMES)}

    def fill(self, row, raw, space, core):
        d, u0, u1, u2 = raw
        u0 = u0 * (1 - 2 * space).astype(jnp.float32)
        cell = lax.broadcasted_iota(jnp.int32, d.shape, 0)
        depth = lax.broadcasted_iota(jnp.int32, d.shape, 1)
        top = (cell == d.shape[0] - 1) & (core == 1)
        bottom = (cell == 0) & (core == 0)
        last, first = depth == d.shape[1] - 1, depth == 0
        zero = jnp.zeros_like(d)
        values = {
            "c0": 1.0 - 6.0 * d,
            "xp": d - u0,
            "xm": d + u0,
            "yp": jnp.where(top, zero, d - u1),
            "ym": jnp.where(bottom, zero, d + u1),
            "zp": jnp.where(last, zero, d - u2),
            "zm": jnp.where(first, zero, d + u2),
            "qyp": jnp.where(top, zero, next_cells(d + u1, -1)),
            "qym": jnp.where(bottom, zero, next_cells(d - u1, 1)),
            "qzp": jnp.where(last, zero, shifted(d + u2, -1)),
            "qzm": jnp.where(first, zero, shifted(d - u2, 1)),
        }
        for name in NAMES:
            self.at[name].write(row, values[name])

    def edge(self):
        for name in NAMES:
            rows = self.at[name]
            rows.write(-1, jnp.zeros((rows.wide, rows.ref.shape[-1]), jnp.float32))

    def terms(self, fields, row, count, adjoint):
        at = self.at
        if adjoint:
            up, low, ends = at["xm"].read(row + 1, count), at["xp"].read(row - 1, count), ("qyp", "qym", "qzp", "qzm")
        else:
            up, low, ends = at["xp"].read(row, count), at["xm"].read(row, count), ("yp", "ym", "zp", "zm")
        yp, ym, zp, zm = (at[n].read(row, count) for n in ends)
        same = at["c0"].read(row, count)
        result = []
        for v in fields:
            c = v.read(row, count)
            around = up * v.read(row + 1, count) + low * v.read(row - 1, count)
            around = around + (yp * next_cells(c, -1) + ym * next_cells(c, 1))
            around = around + (zp * shifted(c, -1) + zm * shifted(c, 1))
            result.append((around, c, same * c))
        return result

    def fine(self, fields, row, count, adjoint):
        return [own + around for around, c, own in self.terms(fields, row, count, adjoint)]

    def coarse(self, v, row, count, adjoint):
        ((around, c, own),) = self.terms([v], row, count, adjoint)
        return c + float(STEPS) * (around + (own - c))


def chunks(start, stop, size=CHUNK):
    return [(row, min(size, stop - row)) for row in range(start, stop, size)]


def joined(core, own, side):
    return jnp.where(core == 1, jnp.concatenate([side, own], 0), jnp.concatenate([own, side], 0))


def mid(core, cells):
    return jnp.where(core == 1, cells[SIDE:], cells[:-SIDE])


def zeros(rows):
    return jnp.zeros((rows.wide, rows.ref.shape[-1]), jnp.float32)


def pack_kernel(rows, own, where_ref, d_ref, u_ref, control_ref, sg_ref, ag_ref, initial_ref, target_ref,
                x_out, side_out, more_out, rims, sides, sem):
    slab, space, core = where_ref[0], where_ref[1], where_ref[2]
    fields = (d_ref, u_ref.at[0], u_ref.at[1], u_ref.at[2], control_ref.at[0], sg_ref.at[0], None, target_ref.at[0])
    starts = (ag_ref.at[0], initial_ref)
    beside = pl.multiple_of(jnp.where(core == 0, own - SIDE, 0), SIDE)
    copies = []

    def bring(source, to):
        copies.append(pltpu.make_async_copy(source, to, sem.at[len(copies)]))
        copies[-1].start()

    def rim(i):
        return pl.ds(jnp.where(space == 0, rows - RIMS[i], 0), RIMS[i])

    def edge(field):
        return field.at[:, pl.ds(beside, SIDE)]

    for i, field in enumerate(starts):
        bring(field.at[rim(6)], rims.at[i])
        bring(edge(field), sides.at[i])
    for i, field in enumerate(fields):
        if field is not None:
            bring(field.at[rim(i)], x_out.at[pl.ds(STARTS[i], RIMS[i])])
            bring(edge(field), side_out.at[i])
    kept = COEF - NEAR
    for i, field in enumerate(fields[:4]):
        bring(field.at[pl.ds(jnp.where(space == 0, rows - COEF, NEAR), kept)], more_out.at[pl.ds(i * kept, kept)])
    for copy in copies:
        copy.wait()
    x_out[pl.ds(STARTS[6], RIMS[6])] = jnp.where(slab == 0, rims[1], rims[0])
    side_out[6] = jnp.where(slab == 0, sides[1], sides[0])


def inner_kernel(rows, wide, where_ref, d_hbm, u_hbm, control_hbm, sg_hbm, ag_hbm, initial_hbm, target_hbm, side_ref,
                 coef_out, hist_out, kept_out, z_out, base_out, state_out, control_ref,
                 c_a, c_b, g_a, g_b, s_a, s_b, con_ref, d_ref, u_ref, sg_ref, ag_ref, initial_ref, target_ref, sem):
    ins = (d_hbm, u_hbm, control_hbm, sg_hbm, ag_hbm, initial_hbm, target_hbm)
    outs = (d_ref, u_ref, control_ref, sg_ref, ag_ref, initial_ref, target_ref)
    copies = [pltpu.make_async_copy(a, b, sem.at[i]) for i, (a, b) in enumerate(zip(ins, outs))]
    for copy in copies:
        copy.start()
    for copy in copies:
        copy.wait()
    slab, space, core = where_ref[0], where_ref[1], where_ref[2]
    first = slab == 0
    c, g, s = ([Rows(r, wide) for r in pair] for pair in ((c_a, c_b), (g_a, g_b), (s_a, s_b)))
    con = Rows(con_ref, wide, 0)
    for field in (*c, *g, *s):
        field.write(-1, zeros(field))
    stencil = Stencil(coef_out, wide)
    stencil.edge()

    def natural(row):
        return jnp.where(space == 1, rows - 1 - row, row)

    def mine(i, own, row):
        return joined(core, own, side_ref[i, natural(row)])

    for row in range(rows):
        at = natural(row)
        stencil.fill(row, [mine(0, d_ref[at], row)] + [mine(1 + i, u_ref[i, at], row) for i in range(3)], space, core)
        con.write(row, mine(4, control_ref[0, at], row))
        g[0].write(row, mine(5, sg_ref[0, at], row))
        start = mine(6, initial_ref[at], row)
        c[0].write(row, jnp.where(first, start, jnp.zeros_like(start)))
        s[0].write(row, mine(6, ag_ref[0, at], row))

    low = rows - STEPS
    for row in range(low, rows):
        values = (con.read(row), g[0].read(row), s[0].read(row), mine(7, target_ref[0, natural(row)], row))
        for i, value in enumerate(values):
            kept_out[i, pl.ds((row - low) * wide, wide)] = value

    def keep(level, fields):
        for i, field in enumerate(fields):
            hist_out[i, level] = field.read(rows - 2 - level, 2)

    keep(0, (c[0], g[0], s[0]))
    for step in range(STEPS):
        now, later = step % 2, 1 - step % 2
        for row, count in chunks(0, rows - 1 - step):
            to_c, to_g = stencil.fine((c[now], g[now]), row, count, False)
            (to_s,) = stencil.fine((s[now],), row, count, True)
            c[later].write(row, to_c + con.read(row, count))
            g[later].write(row, to_g)
            s[later].write(row, to_s)
        if step < STEPS - 1:
            keep(step + 1, (c[later], g[later], s[later]))
    cc, dd = c[1], s[1]
    ready = rows - STEPS
    for row in range(ready):
        sg = mine(5, sg_ref[0, natural(row)], row)
        gap = c[0].read(row) - sg
        ag = mine(6, ag_ref[0, natural(row)], row)
        state = sg + gap
        rest = state - mine(7, target_ref[0, natural(row)], row) - ag
        cc.write(row, gap)
        dd.write(row, rest)
        state_out[row] = mid(core, state)
        base_out[row] = mid(core, ag + rest)
    keep(STEPS, (cc, g[0], s[0], dd))
    for row, count in chunks(0, ready - 1):
        x = g[0].read(row, count) + stencil.coarse(cc, row, count, False)
        e = s[0].read(row, count) + stencil.coarse(dd, row, count, True)
        for r in range(count):
            z_out[row + r] = mid(core, x[r * wide : (r + 1) * wide])
            z_out[ready - 1 + row + r] = mid(core, e[r * wide : (r + 1) * wide])


def wedge_kernel(rows, wide, where_ref, coef_in, hist_ref, kept_ref, more_ref, z_ref, xr_ref, ys_ref,
                 coef_out, z_out, x_out, far_out, base_out, state_out, c_a, c_b, g_a, g_b, s_a, s_b, con_ref):
    slab, space, core = where_ref[0], where_ref[1], where_ref[2]
    first = slab == 0
    flip = space == 1
    c, g, s = (
        [[Rows(r, wide, rows - 2 - level) for r in pair] for level in range(STEPS + 1)]
        for pair in ((c_a, c_b), (g_a, g_b), (s_a, s_b))
    )
    at_level = lambda field, level: field[level][level % 2]
    low = rows - STEPS
    con = Rows(con_ref, wide, low)
    con.write(low, kept_ref[0])
    stencil = Stencil(coef_out, wide)

    def natural(row):
        return jnp.where(flip, rows - 1 - row, row)

    def rim(i, j):
        at = STARTS[i] + jnp.where(flip, RIMS[i] - 1 - j, j)
        return joined(core, xr_ref[at], ys_ref[at])

    for j in range(NEAR):
        stencil.fill(rows + j, [rim(i, j) for i in range(4)], space, core)
    for j in range(NEAR):
        con.write(rows + j, rim(4, j))
    for j in range(NEAR + 1):
        start = rim(6, j)
        c[0][0].write(rows + j, jnp.where(first, start, jnp.zeros_like(start)))
        if j < NEAR:
            s[0][0].write(rows + j, start)
            g[0][0].write(rows + j, rim(5, j))

    def restore(level, fields):
        for i, field in enumerate(fields):
            field.write(rows - 2 - level, hist_ref[i, level])

    restore(0, (c[0][0], g[0][0], s[0][0]))
    for level in range(STEPS):
        row = rows - 1 - level
        nc, ng, ns = (at_level(f, level) for f in (c, g, s))
        lc, lg, ls = (at_level(f, level + 1) for f in (c, g, s))
        for r, count in chunks(row, row + NEAR):
            to_c, to_g = stencil.fine((nc, ng), r, count, False)
            (to_s,) = stencil.fine((ns,), r, count, True)
            lc.write(r, to_c + con.read(r, count))
            lg.write(r, to_g)
            ls.write(r, to_s)
        (to_c,) = stencil.fine((nc,), row + NEAR, 1, False)
        lc.write(row + NEAR, to_c + con.read(row + NEAR))
        if level < STEPS - 1:
            restore(level + 1, (lc, lg, ls))
    fc, fg, fs = (at_level(f, STEPS) for f in (c, g, s))
    cc, dd = c[STEPS][1], s[STEPS][1]
    restore(STEPS, (cc, fg, fs, dd))
    count = NEAR + 1
    sg = jnp.concatenate([kept_ref[1], rim(5, 0)], 0)
    gap = fc.read(low, count) - sg
    state = sg + gap
    ag = jnp.concatenate([kept_ref[2], rim(6, 0)], 0)
    rest = state - jnp.concatenate([kept_ref[3], rim(7, 0)], 0) - ag
    cc.write(low, gap)
    dd.write(low, rest)
    base = ag + rest

    def cells(value, r):
        return mid(core, value[r * wide : (r + 1) * wide])

    for r in range(NEAR):
        state_out[r] = cells(state, r)
        base_out[r] = cells(base, r)
    for r in range(count):
        row = low - 1 + r
        x_row = mid(core, fg.read(row) + stencil.coarse(cc, row, 1, False))
        e_row = mid(core, fs.read(row) + stencil.coarse(dd, row, 1, True))
        z_out[r] = x_row
        z_out[count + r] = e_row
        for out in (x_out, far_out):
            out[count - 1 - r] = x_row
            out[FAR_X + count - 1 - r] = e_row
    for j in range(count, FAR_X):
        x_row = z_ref[rows - 1 - j]
        for out in (x_out, far_out):
            out[j] = x_row
    late = FAR_X + FAR_E
    for j in range(LATE):
        x_out[late + j] = cells(base, NEAR - 1 - j)
    kept = COEF - NEAR
    for j in range(kept):
        at = jnp.where(flip, j, kept - 1 - j)
        for i in range(4):
            x_out[late + LATE + i * kept + j] = more_ref[i * kept + at]


def sorted_pair(core, odd, lower, higher, row, mine, mine_y, other, other_y, at):
    a, b = joined(core, mine[at], mine_y[at]), joined(core, other[at], other_y[at])
    lower.write(row, jnp.where(odd, b, a))
    higher.write(row, jnp.where(odd, a, b))


def message_kernel(rows, wide, where_ref, coef_in, za, zb, ra, rb, xr, xzr, za_y, zb_y, ra_y, rb_y, xr_y, xzr_y,
                   coef_out, msg_out, h_out, xa_out, eb_out, xb_s, ea_s):
    slab, space, core = where_ref[0], where_ref[1], where_ref[2]
    odd = slab % 2 == 1
    upper = slab >= 2
    stencil = Stencil(coef_out, wide)
    late = FAR_X + FAR_E
    for j in range(COEF - NEAR):
        at = [late + i * (COEF - NEAR) + j for i in range(4)]
        stencil.fill(rows + NEAR + j, [joined(core, xr[r + LATE], xr_y[r]) for r in at], space, core)
    xa, xb, ea, eb, h = fields = [Rows(r, wide) for r in (xa_out, xb_s, ea_s, eb_out, h_out)]
    for field in fields:
        field.write(-1, zeros(field))
    inner = rows - NEAR - 1
    for row in range(inner):
        sorted_pair(core, odd, xa, xb, row, za, za_y, ra, ra_y, row)
        sorted_pair(core, odd, ea, eb, row, za, za_y, ra, ra_y, inner + row)
    for row in range(inner, rows):
        sorted_pair(core, odd, xa, xb, row, zb, zb_y, rb, rb_y, row - inner)
        sorted_pair(core, odd, ea, eb, row, zb, zb_y, rb, rb_y, rows - inner + row - inner)
    for j in range(FAR_X):
        sorted_pair(core, odd, xa, xb, rows + j, xr, xr_y, xzr, xzr_y, j)
    for j in range(FAR_E):
        sorted_pair(core, odd, ea, eb, rows + j, xr, xr_y, xzr, xzr_y, FAR_X + j)

    def send(row, count, value):
        for r in range(row, min(row + count, rows + MSG)):
            msg_out[r] = mid(core, value[(r - row) * wide : (r - row + 1) * wide])

    @pl.when(jnp.logical_not(upper))
    def _():
        for row, count in chunks(0, rows + FAR_X - 1):
            value = xb.read(row, count) + stencil.coarse(xa, row, count, False)
            h.write(row, value)
            send(row, count, value)

    @pl.when(upper)
    def _():
        for row, count in chunks(0, rows + FAR_E):
            h.write(row, eb.read(row, count) + stencil.coarse(xa, row, count, True))
        for row, count in chunks(0, rows + FAR_E - 1):
            send(row, count, ea.read(row, count) + stencil.coarse(h, row, count, True))
        send(rows + FAR_E - 1, 1, zeros(ea))


def base_kernel(rows, wide, where_ref, coef_ref, h_ref, xa_ref, eb_ref, start_a, start_b, start_x, base_out, t1_s, t2_s):
    slab, core = where_ref[0], where_ref[2]
    odd = slab % 2 == 1
    upper = slab >= 2
    stencil = Stencil(coef_ref, wide)
    h, xa, eb, t1, t2 = (Rows(r, wide) for r in (h_ref, xa_ref, eb_ref, t1_s, t2_s))
    for field in (t1, t2):
        field.write(-1, zeros(field))

    def start(row):
        if row >= rows:
            return start_x[FAR_X + FAR_E + row - rows]
        return start_a[row] if row < start_a.shape[0] else start_b[row - start_a.shape[0]]

    def put(source):
        for row in range(rows + LATE):
            base_out[row] = start(row) + mid(core, source.read(row))

    @pl.when(jnp.logical_not(upper))
    def _():
        for row, count in chunks(0, rows + FAR_X - 2):
            t1.write(row, stencil.coarse(h, row, count, False))
        for row, count in chunks(0, rows + FAR_X - 3):
            t2.write(row, h.read(row, count) + stencil.coarse(t1, row, count, True))
        for row, count in chunks(0, rows + FAR_X - 4):
            t1.write(row, xa.read(row, count) + stencil.coarse(t2, row, count, True))

        @pl.when(odd)
        def _():
            put(t1)

        @pl.when(jnp.logical_not(odd))
        def _():
            for row, count in chunks(0, rows + LATE):
                t2.write(row, eb.read(row, count) + stencil.coarse(t1, row, count, True))
            put(t2)

    @pl.when(upper & odd)
    def _():
        put(xa)

    @pl.when(upper & jnp.logical_not(odd))
    def _():
        put(h)


def last_kernel(rows, wide, where_ref, coef_ref, msg, msg_y, base, base_y, xa_ref, state_a, state_b, control_ref,
                state_hbm, gradient_hbm, m_s, t0_s, t1_s, total_s, state_out, gradient_out, sem):
    slab, space, core = where_ref[0], where_ref[1], where_ref[2]
    stencil = Stencil(coef_ref, wide)
    m, t0, t1, total, xa = (Rows(r, wide) for r in (m_s, t0_s, t1_s, total_s, xa_ref))
    for field in (m, t0, t1):
        field.write(-1, zeros(field))

    def natural(row):
        return jnp.where(space == 1, rows - 1 - row, row)

    def state(came):
        for row in range(rows):
            before = state_a[row] if row < state_a.shape[0] else state_b[row - state_a.shape[0]]
            state_out[natural(row)] = before + mid(core, came(row)) if came else before

    def begin(extra):
        for row, count in chunks(0, rows + LATE):
            ready = jnp.concatenate([joined(core, base[r], base_y[r]) for r in range(row, row + count)], 0)
            t1.write(row, ready + extra(row, count))

    for row in range(rows + MSG):
        m.write(row, joined(core, msg[row], msg_y[row]))

    @pl.when(slab == 0)
    def _():
        begin(lambda row, count: stencil.coarse(m, row, count, True))
        state(None)

    @pl.when(slab == 1)
    def _():
        begin(m.read)
        state(xa.read)

    @pl.when(slab >= 2)
    def _():
        for row, count in chunks(0, rows + MSG - 1):
            t0.write(row, stencil.coarse(m, row, count, False))

    @pl.when(slab == 2)
    def _():
        begin(lambda row, count: m.read(row, count) + stencil.coarse(t0, row, count, True))
        state(m.read)

    @pl.when(slab == 3)
    def _():
        begin(t0.read)
        state(lambda row: xa.read(row) + t0.read(row))

    copies = [pltpu.make_async_copy(state_out, state_hbm.at[0], sem.at[0])]
    copies[0].start()
    pair = (t1, m)
    for step in range(STEPS - 1):
        now, later = pair[step % 2], pair[1 - step % 2]
        for row, count in chunks(0, rows + LATE - 1 - step):
            (value,) = stencil.fine((now,), row, count, True)
            if step < STEPS - 2:
                later.write(row, value)
            count = min(count, rows - row)
            if count > 0:
                value = value[: count * wide] + (total if step else now).read(row, count)
                if step < STEPS - 2:
                    total.write(row, value)
                else:
                    for r in range(count):
                        at = natural(row + r)
                        own = mid(core, value[r * wide : (r + 1) * wide])
                        gradient_out[at] = own / float(STEPS) + 0.5 * control_ref[0, at]
                    if (row + count) % 8 and row + count < rows:
                        continue
                    begin_at, size = row + count - 8, 8
                    part = pl.ds(jnp.where(space == 1, rows - begin_at - size, begin_at), size)
                    copies.append(pltpu.make_async_copy(gradient_out.at[part], gradient_hbm.at[0, part], sem.at[len(copies)]))
                    copies[-1].start()
    for copy in copies:
        copy.wait()


def call(kernel, outs, scratch, *args, alias=None, in_hbm=0, target=pltpu.VMEM):
    return pl.pallas_call(
        kernel,
        out_shape=[jax.ShapeDtypeStruct(shape, jnp.float32) for shape in outs],
        in_specs=[pl.BlockSpec(memory_space=pltpu.SMEM)]
        + [pl.BlockSpec(memory_space=pltpu.HBM if i < in_hbm else pltpu.VMEM) for i in range(len(args) - 1)],
        out_specs=[pl.BlockSpec(memory_space=target)] * len(outs),
        scratch_shapes=[pltpu.VMEM(shape, jnp.float32) if isinstance(shape, tuple) else shape for shape in scratch],
        input_output_aliases=alias or {},
        compiler_params=pltpu.CompilerParams(vmem_limit_bytes=24 * 1024 * 1024),
        cost_estimate=pl.CostEstimate(flops=1000, bytes_accessed=1000, transcendentals=0),
    )(*args)


def swapped(block, axis):
    return lax.ppermute(block, axis, [(0, 1), (1, 0)])


def across(block, distance):
    return lax.ppermute(block, "tm", [(i, i ^ distance) for i in range(4)])


def across_turned(block, distance):
    route = [(2 * i + j, 2 * (i ^ distance) + 1 - j) for i in range(4) for j in range(2)]
    return lax.ppermute(block, ("tm", "space"), route)


def four_slabs(initial, diffusion, velocity, control, target, state_guess, adjoint_guess):
    rows, own, depth = diffusion.shape
    wide = own + SIDE
    slab, space, core = lax.axis_index("tm"), lax.axis_index("space"), lax.axis_index("yz")
    where = jnp.stack([slab, space, core]).astype(jnp.int32)
    def edge(block):
        return lax.dynamic_slice_in_dim(block, jnp.where(core == 0, own - SIDE, 0), SIDE, axis=block.ndim - 2)

    def flat(count):
        return (count * wide, depth)

    def sent(*groups):
        sizes = [sum(e.shape[0] for e in group) for group in groups]
        got = swapped(jnp.concatenate([e for group in groups for e in group], 0), "yz")
        return [got[sum(sizes[:i]) : sum(sizes[: i + 1])] for i in range(len(sizes))]

    inputs = (diffusion, velocity, control, state_guess, adjoint_guess, initial, target)
    shapes = [a.shape for a in inputs]
    inputs = [pltpu.with_memory_space_constraint(a, pltpu.HBM) for a in inputs]
    cells = lambda count: (count, own, depth)
    edges = (rows, SIDE, depth)
    kept = COEF - NEAR
    x_send, side_send, more = call(
        functools.partial(pack_kernel, rows, own),
        [cells(sum(RIMS)), (len(RIMS), *edges), cells(4 * kept)],
        [(2, *cells(RIMS[6])), (2, *edges), pltpu.SemaphoreType.DMA((2 * len(RIMS) + 6,))],
        where, *inputs,
        in_hbm=len(inputs),
    )
    x_here = swapped(x_send, "space")
    side = swapped(side_send, "yz")
    coefs = (len(NAMES), *flat(rows + COEF + 1))
    inner = rows - NEAR - 1
    tall = flat(rows + FAR_X + 2)
    loaded = [shape for i, shape in enumerate(shapes) if i != 2]
    coef, hist, last, z_a, base_a, state_a, control = call(
        functools.partial(inner_kernel, rows, wide),
        [coefs, (4, STEPS + 1, *flat(2)), (4, *flat(NEAR)), cells(2 * inner), cells(inner + 1), cells(inner + 1), shapes[2]],
        [flat(rows + 2)] * 6 + [flat(rows)] + loaded + [pltpu.SemaphoreType.DMA((len(inputs),))],
        where, *inputs, side,
        in_hbm=len(inputs),
    )
    r_a = across(z_a, 1)
    x_here, coef = lax.optimization_barrier((x_here, coef))
    x_side = swapped(edge(x_here), "yz")
    count = FAR_X + FAR_E
    coef, z_b, x_out, far, base_b, state_b = call(
        functools.partial(wedge_kernel, rows, wide),
        [coefs, cells(2 * NEAR + 2), cells(count + LATE + 4 * kept), cells(count), cells(NEAR), cells(NEAR)],
        [flat(NEAR + 5)] * 6 + [flat(2 * NEAR)],
        where, coef, hist, last, more, z_a, x_here, x_side,
        alias={1: 0},
    )
    x_in = swapped(x_out, "space")
    xz_in = across_turned(far, 1)
    r_b = across(z_b, 1)
    za_y, ra_y = sent([edge(z_a)], [edge(r_a)])
    x_edge, xz_in, r_b = lax.optimization_barrier((edge(x_in), xz_in, r_b))
    xz_edge, r_b = lax.optimization_barrier((edge(xz_in), r_b))
    xr_y, xzr_y, zb_y, rb_y = sent([x_edge[:count], x_edge[count + LATE :]], [xz_edge], [edge(z_b)], [edge(r_b)])
    coef, msg, h, xa, eb = call(
        functools.partial(message_kernel, rows, wide),
        [coefs, cells(rows + MSG), tall, tall, tall],
        [tall, tall],
        where, coef, z_a, z_b, r_a, r_b, x_in, xz_in, za_y, zb_y, ra_y, rb_y, xr_y, xzr_y,
        alias={1: 0},
    )
    msg_in = across(msg, 3)
    (base,) = call(
        functools.partial(base_kernel, rows, wide),
        [cells(rows + LATE)],
        [tall, tall],
        where, coef, h, xa, eb, base_a, base_b, x_in,
    )
    base_y = swapped(edge(base), "yz")
    msg_in, base_y = lax.optimization_barrier((msg_in, base_y))
    msg_y = swapped(edge(msg_in), "yz")
    return call(
        functools.partial(last_kernel, rows, wide),
        [(1, *cells(rows)), (1, *cells(rows))],
        [tall] * 4 + [cells(rows)] * 2 + [pltpu.SemaphoreType.DMA((1 + rows // 8,))],
        where, coef, msg_in, msg_y, base, base_y, xa, state_a, state_b, control,
        target=pltpu.HBM,
    )


def solution(mesh):
    sizes = mesh.shape

    def local(*args):
        rows, own, depth = args[1].shape
        fits = (sizes["tm"], sizes["space"], sizes["yz"]) == (4, 2, 2)
        fits = fits and rows >= 2 * FAR_X and rows % 8 == 0 and own % 8 == 0 and own >= SIDE and depth % 128 == 0
        return four_slabs(*args) if fits else any_mesh(*args)

    field = P(("groups", "space"), "yz", None)
    slabs = P("tm", ("groups", "space"), "yz", None)
    return jax.shard_map(
        local,
        mesh=mesh,
        in_specs=(field, field, P(None, ("groups", "space"), "yz", None), slabs, slabs, slabs, slabs),
        out_specs=(slabs, slabs),
        check_vma=False,
    )
```

```python
import functools

import jax
import jax.numpy as jnp
from jax import lax
from jax.experimental import pallas as pl
from jax.experimental.pallas import tpu as pltpu
from jax.sharding import PartitionSpec as P

STEPS = 6
SIDE = 8
NEAR = 6
LATE = 5
MSG = 7
FAR_X = 5
FAR_E = 1
RIMS = (NEAR, NEAR, NEAR, NEAR, NEAR, NEAR, NEAR + 1, 1)
STARTS = tuple(sum(RIMS[:i]) for i in range(len(RIMS)))


def extended(array, sides, width):
    for axis, dim in sides:
        peers, length = (lax.axis_size(axis), array.shape[dim])
        up = [(i, (i + 1) % peers) for i in range(peers - 1)]
        down = [(j, i) for i, j in up]
        last = lax.slice_in_dim(array, length - width, length, axis=dim)
        first = lax.slice_in_dim(array, 0, width, axis=dim)
        before = lax.ppermute(last, axis, up)
        after = lax.ppermute(first, axis, down)
        array = jnp.concatenate([before, array, after], axis=dim)
    return array


def passed_along(block, axis, distance):
    devices = range(lax.axis_size(axis))
    route = [(i - distance, i) for i in devices if i - distance in devices]
    return lax.ppermute(block, axis, route)


def depth_pad(field):
    return jnp.pad(field, ((0, 0), (0, 0), (1, 1)))


def local_map(padded, coefficients, factor, adjoint):
    centre = padded[1:-1, 1:-1, :]
    if adjoint:
        spread = coefficients[0] * padded
        carried = coefficients[1:4] * padded
        inner_spread = spread[1:-1, 1:-1, :]
        deep = depth_pad(inner_spread)
        laplace = (
            spread[2:, 1:-1, :]
            + spread[:-2, 1:-1, :]
            + spread[1:-1, 2:, :]
            + spread[1:-1, :-2, :]
            + deep[:, :, 2:]
            + deep[:, :, :-2]
            - 6.0 * inner_spread
        )
        deep_carry = depth_pad(carried[2, 1:-1, 1:-1, :])
        transport = (
            carried[0, 2:, 1:-1, :]
            - carried[0, :-2, 1:-1, :]
            + (carried[1, 1:-1, 2:, :] - carried[1, 1:-1, :-2, :])
            + (deep_carry[:, :, 2:] - deep_carry[:, :, :-2])
        )
        return (centre + factor * (laplace + transport)) * coefficients[4, 1:-1, 1:-1, :]
    inner = coefficients[:, 1:-1, 1:-1, :]
    deep = depth_pad(centre)
    laplace = (
        padded[2:, 1:-1, :]
        + padded[:-2, 1:-1, :]
        + padded[1:-1, 2:, :]
        + padded[1:-1, :-2, :]
        + deep[:, :, 2:]
        + deep[:, :, :-2]
        - 6.0 * centre
    )
    transport = (
        inner[1] * (padded[2:, 1:-1, :] - padded[:-2, 1:-1, :])
        + inner[2] * (padded[1:-1, 2:, :] - padded[1:-1, :-2, :])
        + inner[3] * (deep[:, :, 2:] - deep[:, :, :-2])
    )
    return centre + factor * (inner[0] * laplace - transport)


def halo_cells(field):
    return extended(field, (("space", 0), ("yz", 1)), 1)


def coarse_chain(residual, near_coefficients, adjoint, direction):
    factor = float(STEPS)

    def one_turn(turn_index, correction):
        moved = local_map(halo_cells(correction), near_coefficients, factor, adjoint)
        arrived = passed_along(moved, "tm", direction)
        return residual + arrived

    return lax.fori_loop(0, lax.axis_size("tm") - 1, one_turn, residual)


def any_mesh(initial, diffusion, velocity, control, target, state_guess, adjoint_guess):
    source = control[0]
    guess_state = state_guess[0]
    guess_adjoint = adjoint_guess[0]
    stacked = jnp.concatenate([diffusion[None], velocity, jnp.ones_like(diffusion)[None]], 0)
    near_coefficients = extended(stacked, (("space", 1), ("yz", 2)), 1)
    arrived = passed_along(guess_state, "tm", 1)
    fine = jnp.where(lax.axis_index("tm") == 0, initial, arrived)
    sweep = guess_adjoint
    for step_index in range(STEPS):
        fine = local_map(halo_cells(fine), near_coefficients, 1.0, False) + source
    for step_index in range(STEPS):
        sweep = local_map(halo_cells(sweep), near_coefficients, 1.0, True)
    state_residual = fine - guess_state
    state_new = guess_state + coarse_chain(state_residual, near_coefficients, False, 1)
    from_next = passed_along(sweep, "tm", -1)
    adjoint_residual = from_next + state_new - target[0] - guess_adjoint
    multiplier = guess_adjoint + coarse_chain(adjoint_residual, near_coefficients, True, -1)
    running_sum = multiplier
    for step_index in range(STEPS - 1):
        multiplier = local_map(halo_cells(multiplier), near_coefficients, 1.0, True)
        running_sum = running_sum + multiplier
    gradient = running_sum / float(STEPS) + 0.5 * source
    return (state_new[None], gradient[None])


NAMES = ("c0", "xp", "xm", "yp", "ym", "zp", "zm", "qyp", "qym", "qzp", "qzm")
CHUNK = 2


class Rows:
    def __init__(self, ref, wide, first=-1):
        self.ref, self.wide, self.first = ref, wide, first

    def read(self, row, count=1):
        return self.ref[pl.ds((row - self.first) * self.wide, count * self.wide)]

    def write(self, row, value):
        self.ref[pl.ds((row - self.first) * self.wide, value.shape[0])] = value


def shifted(value, step):
    return pltpu.roll(value, step % value.shape[1], 1)


def next_cells(value, step):
    return pltpu.roll(value, step % value.shape[0], 0)


class Stencil:
    def __init__(self, ref, wide):
        self.at = {name: Rows(ref.at[i], wide) for i, name in enumerate(NAMES)}

    def fill(self, row, raw, space, core):
        d, u0, u1, u2 = raw
        u0 = u0 * (1 - 2 * space).astype(jnp.float32)
        cell = lax.broadcasted_iota(jnp.int32, d.shape, 0)
        depth = lax.broadcasted_iota(jnp.int32, d.shape, 1)
        top = (cell == d.shape[0] - 1) & (core == 1)
        bottom = (cell == 0) & (core == 0)
        last, first = depth == d.shape[1] - 1, depth == 0
        zero = jnp.zeros_like(d)
        values = {
            "c0": 1.0 - 6.0 * d,
            "xp": d - u0,
            "xm": d + u0,
            "yp": jnp.where(top, zero, d - u1),
            "ym": jnp.where(bottom, zero, d + u1),
            "zp": jnp.where(last, zero, d - u2),
            "zm": jnp.where(first, zero, d + u2),
            "qyp": jnp.where(top, zero, next_cells(d + u1, -1)),
            "qym": jnp.where(bottom, zero, next_cells(d - u1, 1)),
            "qzp": jnp.where(last, zero, shifted(d + u2, -1)),
            "qzm": jnp.where(first, zero, shifted(d - u2, 1)),
        }
        for name in NAMES:
            self.at[name].write(row, values[name])

    def edge(self):
        for name in NAMES:
            rows = self.at[name]
            rows.write(-1, jnp.zeros((rows.wide, rows.ref.shape[-1]), jnp.float32))

    def terms(self, fields, row, count, adjoint):
        at = self.at
        if adjoint:
            up, low, ends = at["xm"].read(row + 1, count), at["xp"].read(row - 1, count), ("qyp", "qym", "qzp", "qzm")
        else:
            up, low, ends = at["xp"].read(row, count), at["xm"].read(row, count), ("yp", "ym", "zp", "zm")
        yp, ym, zp, zm = (at[n].read(row, count) for n in ends)
        same = at["c0"].read(row, count)
        result = []
        for v in fields:
            c = v.read(row, count)
            around = up * v.read(row + 1, count) + low * v.read(row - 1, count)
            around = around + (yp * next_cells(c, -1) + ym * next_cells(c, 1))
            around = around + (zp * shifted(c, -1) + zm * shifted(c, 1))
            result.append((around, c, same * c))
        return result

    def fine(self, fields, row, count, adjoint):
        return [own + around for around, c, own in self.terms(fields, row, count, adjoint)]

    def coarse(self, v, row, count, adjoint):
        ((around, c, own),) = self.terms([v], row, count, adjoint)
        return c + float(STEPS) * (around + (own - c))


def chunks(start, stop, size=CHUNK):
    return [(row, min(size, stop - row)) for row in range(start, stop, size)]


def joined(core, own, side):
    return jnp.where(core == 1, jnp.concatenate([side, own], 0), jnp.concatenate([own, side], 0))


def mid(core, cells):
    return jnp.where(core == 1, cells[SIDE:], cells[:-SIDE])


def zeros(rows):
    return jnp.zeros((rows.wide, rows.ref.shape[-1]), jnp.float32)


def pack_kernel(rows, own, where_ref, d_ref, u_ref, control_ref, sg_ref, ag_ref, initial_ref, target_ref,
                x_out, side_out, rims, sides, sem):
    slab, space, core = where_ref[0], where_ref[1], where_ref[2]
    fields = (d_ref, u_ref.at[0], u_ref.at[1], u_ref.at[2], control_ref.at[0], sg_ref.at[0], None, target_ref.at[0])
    starts = (ag_ref.at[0], initial_ref)
    beside = pl.multiple_of(jnp.where(core == 0, own - SIDE, 0), SIDE)
    copies = []

    def bring(source, to):
        copies.append(pltpu.make_async_copy(source, to, sem.at[len(copies)]))
        copies[-1].start()

    def rim(i):
        return pl.ds(jnp.where(space == 0, rows - RIMS[i], 0), RIMS[i])

    def edge(field):
        return field.at[:, pl.ds(beside, SIDE)]

    for i, field in enumerate(starts):
        bring(field.at[rim(6)], rims.at[i])
        bring(edge(field), sides.at[i])
    for i, field in enumerate(fields):
        if field is not None:
            bring(field.at[rim(i)], x_out.at[pl.ds(STARTS[i], RIMS[i])])
            bring(edge(field), side_out.at[i])
    for copy in copies:
        copy.wait()
    x_out[pl.ds(STARTS[6], RIMS[6])] = jnp.where(slab == 0, rims[1], rims[0])
    side_out[6] = jnp.where(slab == 0, sides[1], sides[0])


def inner_kernel(rows, wide, where_ref, d_hbm, u_hbm, control_hbm, sg_hbm, ag_hbm, initial_hbm, target_hbm, side_ref,
                 coef_out, hist_out, kept_out, z_out, base_out, state_out, control_ref,
                 c_a, c_b, g_a, g_b, s_a, s_b, con_ref, d_ref, u_ref, sg_ref, ag_ref, initial_ref, target_ref, sem):
    ins = (d_hbm, u_hbm, control_hbm, sg_hbm, ag_hbm, initial_hbm, target_hbm)
    outs = (d_ref, u_ref, control_ref, sg_ref, ag_ref, initial_ref, target_ref)
    copies = [pltpu.make_async_copy(a, b, sem.at[i]) for i, (a, b) in enumerate(zip(ins, outs))]
    for copy in copies:
        copy.start()
    for copy in copies:
        copy.wait()
    slab, space, core = where_ref[0], where_ref[1], where_ref[2]
    first = slab == 0
    c, g, s = ([Rows(r, wide) for r in pair] for pair in ((c_a, c_b), (g_a, g_b), (s_a, s_b)))
    con = Rows(con_ref, wide, 0)
    for field in (*c, *g, *s):
        field.write(-1, zeros(field))
    stencil = Stencil(coef_out, wide)
    stencil.edge()

    def natural(row):
        return jnp.where(space == 1, rows - 1 - row, row)

    def mine(i, own, row):
        return joined(core, own, side_ref[i, natural(row)])

    for row in range(rows):
        at = natural(row)
        stencil.fill(row, [mine(0, d_ref[at], row)] + [mine(1 + i, u_ref[i, at], row) for i in range(3)], space, core)
        con.write(row, mine(4, control_ref[0, at], row))
        g[0].write(row, mine(5, sg_ref[0, at], row))
        start = mine(6, initial_ref[at], row)
        c[0].write(row, jnp.where(first, start, jnp.zeros_like(start)))
        s[0].write(row, mine(6, ag_ref[0, at], row))

    low = rows - STEPS
    for row in range(low, rows):
        values = (con.read(row), g[0].read(row), s[0].read(row), mine(7, target_ref[0, natural(row)], row))
        for i, value in enumerate(values):
            kept_out[i, pl.ds((row - low) * wide, wide)] = value

    def keep(level, fields):
        for i, field in enumerate(fields):
            hist_out[i, level] = field.read(rows - 2 - level, 2)

    keep(0, (c[0], g[0], s[0]))
    for step in range(STEPS):
        now, later = step % 2, 1 - step % 2
        for row, count in chunks(0, rows - 1 - step):
            to_c, to_g = stencil.fine((c[now], g[now]), row, count, False)
            (to_s,) = stencil.fine((s[now],), row, count, True)
            c[later].write(row, to_c + con.read(row, count))
            g[later].write(row, to_g)
            s[later].write(row, to_s)
        if step < STEPS - 1:
            keep(step + 1, (c[later], g[later], s[later]))
    cc, dd = c[1], s[1]
    ready = rows - STEPS
    for row in range(ready):
        sg = mine(5, sg_ref[0, natural(row)], row)
        gap = c[0].read(row) - sg
        ag = mine(6, ag_ref[0, natural(row)], row)
        state = sg + gap
        rest = state - mine(7, target_ref[0, natural(row)], row) - ag
        cc.write(row, gap)
        dd.write(row, rest)
        state_out[row] = mid(core, state)
        base_out[row] = mid(core, ag + rest)
    keep(STEPS, (cc, g[0], s[0], dd))
    for row, count in chunks(0, ready - 1):
        x = g[0].read(row, count) + stencil.coarse(cc, row, count, False)
        e = s[0].read(row, count) + stencil.coarse(dd, row, count, True)
        for r in range(count):
            z_out[row + r] = mid(core, x[r * wide : (r + 1) * wide])
            z_out[ready - 1 + row + r] = mid(core, e[r * wide : (r + 1) * wide])


def wedge_kernel(rows, wide, where_ref, coef_in, hist_ref, kept_ref, xr_ref, ys_ref,
                 coef_out, z_out, x_out, base_out, state_out, c_a, c_b, g_a, g_b, s_a, s_b, con_ref):
    slab, space, core = where_ref[0], where_ref[1], where_ref[2]
    first = slab == 0
    flip = space == 1
    c, g, s = (
        [[Rows(r, wide, rows - 2 - level) for r in pair] for level in range(STEPS + 1)]
        for pair in ((c_a, c_b), (g_a, g_b), (s_a, s_b))
    )
    at_level = lambda field, level: field[level][level % 2]
    low = rows - STEPS
    con = Rows(con_ref, wide, low)
    con.write(low, kept_ref[0])
    stencil = Stencil(coef_out, wide)

    def natural(row):
        return jnp.where(flip, rows - 1 - row, row)

    def rim(i, j):
        at = STARTS[i] + jnp.where(flip, RIMS[i] - 1 - j, j)
        return joined(core, xr_ref[at], ys_ref[at])

    for j in range(NEAR):
        stencil.fill(rows + j, [rim(i, j) for i in range(4)], space, core)
    for j in range(NEAR):
        con.write(rows + j, rim(4, j))
    for j in range(NEAR + 1):
        start = rim(6, j)
        c[0][0].write(rows + j, jnp.where(first, start, jnp.zeros_like(start)))
        if j < NEAR:
            s[0][0].write(rows + j, start)
            g[0][0].write(rows + j, rim(5, j))

    def restore(level, fields):
        for i, field in enumerate(fields):
            field.write(rows - 2 - level, hist_ref[i, level])

    restore(0, (c[0][0], g[0][0], s[0][0]))
    for level in range(STEPS):
        row = rows - 1 - level
        nc, ng, ns = (at_level(f, level) for f in (c, g, s))
        lc, lg, ls = (at_level(f, level + 1) for f in (c, g, s))
        for r, count in chunks(row, row + NEAR):
            to_c, to_g = stencil.fine((nc, ng), r, count, False)
            (to_s,) = stencil.fine((ns,), r, count, True)
            lc.write(r, to_c + con.read(r, count))
            lg.write(r, to_g)
            ls.write(r, to_s)
        (to_c,) = stencil.fine((nc,), row + NEAR, 1, False)
        lc.write(row + NEAR, to_c + con.read(row + NEAR))
        if level < STEPS - 1:
            restore(level + 1, (lc, lg, ls))
    fc, fg, fs = (at_level(f, STEPS) for f in (c, g, s))
    cc, dd = c[STEPS][1], s[STEPS][1]
    restore(STEPS, (cc, fg, fs, dd))
    count = NEAR + 1
    sg = jnp.concatenate([kept_ref[1], rim(5, 0)], 0)
    gap = fc.read(low, count) - sg
    state = sg + gap
    ag = jnp.concatenate([kept_ref[2], rim(6, 0)], 0)
    rest = state - jnp.concatenate([kept_ref[3], rim(7, 0)], 0) - ag
    cc.write(low, gap)
    dd.write(low, rest)
    base = ag + rest

    def cells(value, r):
        return mid(core, value[r * wide : (r + 1) * wide])

    for r in range(NEAR):
        state_out[r] = cells(state, r)
        base_out[r] = cells(base, r)
    for r in range(count):
        row = low - 1 + r
        x_row = mid(core, fg.read(row) + stencil.coarse(cc, row, 1, False))
        e_row = mid(core, fs.read(row) + stencil.coarse(dd, row, 1, True))
        z_out[r] = x_row
        z_out[count + r] = e_row
        if count - 1 - r < FAR_X:
            x_out[count - 1 - r] = x_row
        if count - 1 - r < FAR_E:
            x_out[FAR_X + count - 1 - r] = e_row


def sorted_pair(core, odd, lower, higher, row, mine, mine_y, other, other_y, at):
    a, b = joined(core, mine[at], mine_y[at]), joined(core, other[at], other_y[at])
    lower.write(row, jnp.where(odd, b, a))
    higher.write(row, jnp.where(odd, a, b))


def message_kernel(rows, wide, where_ref, coef_ref, za, zb, ra, rb, xr, xzr, za_y, zb_y, ra_y, rb_y, xr_y, xzr_y,
                   msg_out, turn_out, h_out, xa_out, eb_out, xb_s, ea_s):
    slab, space, core = where_ref[0], where_ref[1], where_ref[2]
    odd = slab % 2 == 1
    upper = slab >= 2
    stencil = Stencil(coef_ref, wide)
    xa, xb, ea, eb, h = fields = [Rows(r, wide) for r in (xa_out, xb_s, ea_s, eb_out, h_out)]
    for field in fields:
        field.write(-1, zeros(field))
    inner = rows - NEAR - 1
    for row in range(inner):
        sorted_pair(core, odd, xa, xb, row, za, za_y, ra, ra_y, row)
        sorted_pair(core, odd, ea, eb, row, za, za_y, ra, ra_y, inner + row)
    for row in range(inner, rows):
        sorted_pair(core, odd, xa, xb, row, zb, zb_y, rb, rb_y, row - inner)
        sorted_pair(core, odd, ea, eb, row, zb, zb_y, rb, rb_y, rows - inner + row - inner)
    for j in range(FAR_X):
        sorted_pair(core, odd, xa, xb, rows + j, xr, xr_y, xzr, xzr_y, j)
    for j in range(FAR_E):
        sorted_pair(core, odd, ea, eb, rows + j, xr, xr_y, xzr, xzr_y, FAR_X + j)

    def send(row, count, value):
        for r in range(row, min(row + count, rows)):
            cells = mid(core, value[(r - row) * wide : (r - row + 1) * wide])
            msg_out[r] = cells
            if r >= rows - MSG:
                turn_out[rows - 1 - r] = cells

    @pl.when(jnp.logical_not(upper))
    def _():
        for row, count in chunks(0, rows + FAR_X - 1):
            value = xb.read(row, count) + stencil.coarse(xa, row, count, False)
            h.write(row, value)
            send(row, count, value)

    @pl.when(upper)
    def _():
        for row, count in chunks(0, rows + 1):
            h.write(row, eb.read(row, count) + stencil.coarse(xa, row, count, True))
        for row, count in chunks(0, rows):
            send(row, count, ea.read(row, count) + stencil.coarse(h, row, count, True))


def base_kernel(rows, wide, where_ref, coef_ref, h_ref, xa_ref, eb_ref, start_a, start_b, base_out, edge_out, t1_s, t2_s):
    slab, core = where_ref[0], where_ref[2]
    odd = slab % 2 == 1
    upper = slab >= 2
    stencil = Stencil(coef_ref, wide)
    h, xa, eb, t1, t2 = (Rows(r, wide) for r in (h_ref, xa_ref, eb_ref, t1_s, t2_s))
    for field in (t1, t2):
        field.write(-1, zeros(field))

    def put(source):
        for row in range(rows):
            start = start_a[row] if row < start_a.shape[0] else start_b[row - start_a.shape[0]]
            value = start + mid(core, source.read(row))
            base_out[row] = value
            if row >= rows - LATE:
                edge_out[rows - 1 - row] = value

    @pl.when(jnp.logical_not(upper))
    def _():
        for row, count in chunks(0, rows + FAR_X - 2):
            t1.write(row, stencil.coarse(h, row, count, False))
        for row, count in chunks(0, rows + FAR_X - 3):
            t2.write(row, h.read(row, count) + stencil.coarse(t1, row, count, True))
        for row, count in chunks(0, rows + FAR_X - 4):
            t1.write(row, xa.read(row, count) + stencil.coarse(t2, row, count, True))

        @pl.when(odd)
        def _():
            put(t1)

        @pl.when(jnp.logical_not(odd))
        def _():
            for row, count in chunks(0, rows):
                t2.write(row, eb.read(row, count) + stencil.coarse(t1, row, count, True))
            put(t2)

    @pl.when(upper & odd)
    def _():
        put(xa)

    @pl.when(upper & jnp.logical_not(odd))
    def _():
        put(h)


def last_kernel(rows, wide, where_ref, coef_ref, msg, msg_y, base, base_y, xa_ref, state_a, state_b, control_ref,
                state_hbm, gradient_hbm, m_s, t0_s, t1_s, total_s, state_out, gradient_out, sem):
    slab, space, core = where_ref[0], where_ref[1], where_ref[2]
    stencil = Stencil(coef_ref, wide)
    m, t0, t1, total, xa = (Rows(r, wide) for r in (m_s, t0_s, t1_s, total_s, xa_ref))
    for field in (m, t0, t1):
        field.write(-1, zeros(field))

    def natural(row):
        return jnp.where(space == 1, rows - 1 - row, row)

    def state(came):
        for row in range(rows):
            before = state_a[row] if row < state_a.shape[0] else state_b[row - state_a.shape[0]]
            state_out[natural(row)] = before + mid(core, came(row)) if came else before

    def begin(extra):
        for row, count in chunks(0, rows + LATE):
            ready = jnp.concatenate([joined(core, base[r], base_y[r]) for r in range(row, row + count)], 0)
            t1.write(row, ready + extra(row, count))

    for row in range(rows + MSG):
        m.write(row, joined(core, msg[row], msg_y[row]))

    @pl.when(slab == 0)
    def _():
        begin(lambda row, count: stencil.coarse(m, row, count, True))
        state(None)

    @pl.when(slab == 1)
    def _():
        begin(m.read)
        state(xa.read)

    @pl.when(slab >= 2)
    def _():
        for row, count in chunks(0, rows + MSG - 1):
            t0.write(row, stencil.coarse(m, row, count, False))

    @pl.when(slab == 2)
    def _():
        begin(lambda row, count: m.read(row, count) + stencil.coarse(t0, row, count, True))
        state(m.read)

    @pl.when(slab == 3)
    def _():
        begin(t0.read)
        state(lambda row: xa.read(row) + t0.read(row))

    copies = [pltpu.make_async_copy(state_out, state_hbm.at[0], sem.at[0])]
    copies[0].start()
    pair = (t1, m)
    for step in range(STEPS - 1):
        now, later = pair[step % 2], pair[1 - step % 2]
        for row, count in chunks(0, rows + LATE - 1 - step):
            (value,) = stencil.fine((now,), row, count, True)
            if step < STEPS - 2:
                later.write(row, value)
            count = min(count, rows - row)
            if count > 0:
                value = value[: count * wide] + (total if step else now).read(row, count)
                if step < STEPS - 2:
                    total.write(row, value)
                else:
                    for r in range(count):
                        at = natural(row + r)
                        own = mid(core, value[r * wide : (r + 1) * wide])
                        gradient_out[at] = own / float(STEPS) + 0.5 * control_ref[0, at]
                    if (row + count) % 8 and row + count < rows:
                        continue
                    begin_at, size = row + count - 8, 8
                    part = pl.ds(jnp.where(space == 1, rows - begin_at - size, begin_at), size)
                    copies.append(pltpu.make_async_copy(gradient_out.at[part], gradient_hbm.at[0, part], sem.at[len(copies)]))
                    copies[-1].start()
    for copy in copies:
        copy.wait()


def call(kernel, outs, scratch, *args, alias=None, in_hbm=0, target=pltpu.VMEM):
    return pl.pallas_call(
        kernel,
        out_shape=[jax.ShapeDtypeStruct(shape, jnp.float32) for shape in outs],
        in_specs=[pl.BlockSpec(memory_space=pltpu.SMEM)]
        + [pl.BlockSpec(memory_space=pltpu.HBM if i < in_hbm else pltpu.VMEM) for i in range(len(args) - 1)],
        out_specs=[pl.BlockSpec(memory_space=target)] * len(outs),
        scratch_shapes=[pltpu.VMEM(shape, jnp.float32) if isinstance(shape, tuple) else shape for shape in scratch],
        input_output_aliases=alias or {},
        compiler_params=pltpu.CompilerParams(vmem_limit_bytes=24 * 1024 * 1024),
        cost_estimate=pl.CostEstimate(flops=1000, bytes_accessed=1000, transcendentals=0),
    )(*args)


def swapped(block, axis):
    return lax.ppermute(block, axis, [(0, 1), (1, 0)])


def across(block, distance):
    return lax.ppermute(block, "tm", [(i, i ^ distance) for i in range(4)])


def across_turned(block, distance):
    route = [(2 * i + j, 2 * (i ^ distance) + 1 - j) for i in range(4) for j in range(2)]
    return lax.ppermute(block, ("tm", "space"), route)


def four_slabs(initial, diffusion, velocity, control, target, state_guess, adjoint_guess):
    rows, own, depth = diffusion.shape
    wide = own + SIDE
    slab, space, core = lax.axis_index("tm"), lax.axis_index("space"), lax.axis_index("yz")
    where = jnp.stack([slab, space, core]).astype(jnp.int32)
    def edge(block):
        return lax.dynamic_slice_in_dim(block, jnp.where(core == 0, own - SIDE, 0), SIDE, axis=block.ndim - 2)

    def flat(count):
        return (count * wide, depth)

    def sent(*groups):
        sizes = [sum(e.shape[0] for e in group) for group in groups]
        got = swapped(jnp.concatenate([e for group in groups for e in group], 0), "yz")
        return [got[sum(sizes[:i]) : sum(sizes[: i + 1])] for i in range(len(sizes))]

    inputs = (diffusion, velocity, control, state_guess, adjoint_guess, initial, target)
    shapes = [a.shape for a in inputs]
    inputs = [pltpu.with_memory_space_constraint(a, pltpu.HBM) for a in inputs]
    cells = lambda count: (count, own, depth)
    edges = (rows, SIDE, depth)
    x_send, side_send = call(
        functools.partial(pack_kernel, rows, own),
        [cells(sum(RIMS)), (len(RIMS), *edges)],
        [(2, *cells(RIMS[6])), (2, *edges), pltpu.SemaphoreType.DMA((2 * len(RIMS) + 2,))],
        where, *inputs,
        in_hbm=len(inputs),
    )
    x_here = swapped(x_send, "space")
    side = swapped(side_send, "yz")
    coefs = (len(NAMES), *flat(rows + NEAR + 1))
    inner = rows - NEAR - 1
    tall = flat(rows + MSG + 2)
    loaded = [shape for i, shape in enumerate(shapes) if i != 2]
    coef, hist, last, z_a, base_a, state_a, control = call(
        functools.partial(inner_kernel, rows, wide),
        [coefs, (4, STEPS + 1, *flat(2)), (4, *flat(NEAR)), cells(2 * inner), cells(inner + 1), cells(inner + 1), shapes[2]],
        [flat(rows + 2)] * 6 + [flat(rows)] + loaded + [pltpu.SemaphoreType.DMA((len(inputs),))],
        where, *inputs, side,
        in_hbm=len(inputs),
    )
    r_a = across(z_a, 1)
    x_here, coef = lax.optimization_barrier((x_here, coef))
    x_side = swapped(edge(x_here), "yz")
    coef, z_b, x_out, base_b, state_b = call(
        functools.partial(wedge_kernel, rows, wide),
        [coefs, cells(2 * NEAR + 2), cells(FAR_X + FAR_E), cells(NEAR), cells(NEAR)],
        [flat(NEAR + 5)] * 6 + [flat(2 * NEAR)],
        where, coef, hist, last, x_here, x_side,
        alias={1: 0},
    )
    x_in = swapped(x_out, "space")
    xz_in = across_turned(x_out, 1)
    r_b = across(z_b, 1)
    za_y, ra_y = sent([edge(z_a)], [edge(r_a)])
    xr_y, xzr_y, zb_y, rb_y = sent([edge(x_in)], [edge(xz_in)], [edge(z_b)], [edge(r_b)])
    msg, turn, h, xa, eb = call(
        functools.partial(message_kernel, rows, wide),
        [cells(rows), cells(MSG), tall, tall, tall],
        [tall, tall],
        where, coef, z_a, z_b, r_a, r_b, x_in, xz_in, za_y, zb_y, ra_y, rb_y, xr_y, xzr_y,
    )
    msg_in = across(msg, 3)
    turn_in = across_turned(turn, 3)
    base, base_edge = call(
        functools.partial(base_kernel, rows, wide),
        [cells(rows), cells(LATE)],
        [tall, tall],
        where, coef, h, xa, eb, base_a, base_b,
    )
    base_x = swapped(base_edge, "space")
    msg_in, base_x = lax.optimization_barrier((jnp.concatenate([msg_in, turn_in], 0), base_x))
    base = jnp.concatenate([base, base_x], 0)
    msg_y, base_y = sent([edge(msg_in)], [edge(base)])
    return call(
        functools.partial(last_kernel, rows, wide),
        [(1, *cells(rows)), (1, *cells(rows))],
        [tall] * 4 + [cells(rows)] * 2 + [pltpu.SemaphoreType.DMA((1 + rows // 8,))],
        where, coef, msg_in, msg_y, base, base_y, xa, state_a, state_b, control,
        target=pltpu.HBM,
    )


def solution(mesh):
    sizes = mesh.shape

    def local(*args):
        rows, own, depth = args[1].shape
        fits = (sizes["tm"], sizes["space"], sizes["yz"]) == (4, 2, 2)
        fits = fits and rows >= 2 * (NEAR + 1) and rows % 8 == 0 and own % 8 == 0 and own >= SIDE and depth % 128 == 0
        return four_slabs(*args) if fits else any_mesh(*args)

    field = P(("groups", "space"), "yz", None)
    slabs = P("tm", ("groups", "space"), "yz", None)
    return jax.shard_map(
        local,
        mesh=mesh,
        in_specs=(field, field, P(None, ("groups", "space"), "yz", None), slabs, slabs, slabs, slabs),
        out_specs=(slabs, slabs),
        check_vma=False,
    )
```

```python
import functools

import jax
import jax.numpy as jnp
from jax import lax
from jax.experimental import pallas as pl
from jax.experimental.pallas import tpu as pltpu
from jax.sharding import PartitionSpec as P

STEPS = 6
SIDE = 8
NEAR = 6
LATE = 5
MSG = 7
FAR_X = 5
FAR_E = 1
RIMS = (NEAR, NEAR, NEAR, NEAR, NEAR, NEAR, NEAR + 1, 1)
STARTS = tuple(sum(RIMS[:i]) for i in range(len(RIMS)))


def extended(array, sides, width):
    for axis, dim in sides:
        peers, length = (lax.axis_size(axis), array.shape[dim])
        up = [(i, (i + 1) % peers) for i in range(peers - 1)]
        down = [(j, i) for i, j in up]
        last = lax.slice_in_dim(array, length - width, length, axis=dim)
        first = lax.slice_in_dim(array, 0, width, axis=dim)
        before = lax.ppermute(last, axis, up)
        after = lax.ppermute(first, axis, down)
        array = jnp.concatenate([before, array, after], axis=dim)
    return array


def passed_along(block, axis, distance):
    devices = range(lax.axis_size(axis))
    route = [(i - distance, i) for i in devices if i - distance in devices]
    return lax.ppermute(block, axis, route)


def depth_pad(field):
    return jnp.pad(field, ((0, 0), (0, 0), (1, 1)))


def local_map(padded, coefficients, factor, adjoint):
    centre = padded[1:-1, 1:-1, :]
    if adjoint:
        spread = coefficients[0] * padded
        carried = coefficients[1:4] * padded
        inner_spread = spread[1:-1, 1:-1, :]
        deep = depth_pad(inner_spread)
        laplace = (
            spread[2:, 1:-1, :]
            + spread[:-2, 1:-1, :]
            + spread[1:-1, 2:, :]
            + spread[1:-1, :-2, :]
            + deep[:, :, 2:]
            + deep[:, :, :-2]
            - 6.0 * inner_spread
        )
        deep_carry = depth_pad(carried[2, 1:-1, 1:-1, :])
        transport = (
            carried[0, 2:, 1:-1, :]
            - carried[0, :-2, 1:-1, :]
            + (carried[1, 1:-1, 2:, :] - carried[1, 1:-1, :-2, :])
            + (deep_carry[:, :, 2:] - deep_carry[:, :, :-2])
        )
        return (centre + factor * (laplace + transport)) * coefficients[4, 1:-1, 1:-1, :]
    inner = coefficients[:, 1:-1, 1:-1, :]
    deep = depth_pad(centre)
    laplace = (
        padded[2:, 1:-1, :]
        + padded[:-2, 1:-1, :]
        + padded[1:-1, 2:, :]
        + padded[1:-1, :-2, :]
        + deep[:, :, 2:]
        + deep[:, :, :-2]
        - 6.0 * centre
    )
    transport = (
        inner[1] * (padded[2:, 1:-1, :] - padded[:-2, 1:-1, :])
        + inner[2] * (padded[1:-1, 2:, :] - padded[1:-1, :-2, :])
        + inner[3] * (deep[:, :, 2:] - deep[:, :, :-2])
    )
    return centre + factor * (inner[0] * laplace - transport)


def halo_cells(field):
    return extended(field, (("space", 0), ("yz", 1)), 1)


def coarse_chain(residual, near_coefficients, adjoint, direction):
    factor = float(STEPS)

    def one_turn(turn_index, correction):
        moved = local_map(halo_cells(correction), near_coefficients, factor, adjoint)
        arrived = passed_along(moved, "tm", direction)
        return residual + arrived

    return lax.fori_loop(0, lax.axis_size("tm") - 1, one_turn, residual)


def any_mesh(initial, diffusion, velocity, control, target, state_guess, adjoint_guess):
    source = control[0]
    guess_state = state_guess[0]
    guess_adjoint = adjoint_guess[0]
    stacked = jnp.concatenate([diffusion[None], velocity, jnp.ones_like(diffusion)[None]], 0)
    near_coefficients = extended(stacked, (("space", 1), ("yz", 2)), 1)
    arrived = passed_along(guess_state, "tm", 1)
    fine = jnp.where(lax.axis_index("tm") == 0, initial, arrived)
    sweep = guess_adjoint
    for step_index in range(STEPS):
        fine = local_map(halo_cells(fine), near_coefficients, 1.0, False) + source
    for step_index in range(STEPS):
        sweep = local_map(halo_cells(sweep), near_coefficients, 1.0, True)
    state_residual = fine - guess_state
    state_new = guess_state + coarse_chain(state_residual, near_coefficients, False, 1)
    from_next = passed_along(sweep, "tm", -1)
    adjoint_residual = from_next + state_new - target[0] - guess_adjoint
    multiplier = guess_adjoint + coarse_chain(adjoint_residual, near_coefficients, True, -1)
    running_sum = multiplier
    for step_index in range(STEPS - 1):
        multiplier = local_map(halo_cells(multiplier), near_coefficients, 1.0, True)
        running_sum = running_sum + multiplier
    gradient = running_sum / float(STEPS) + 0.5 * source
    return (state_new[None], gradient[None])


NAMES = ("c0", "xp", "xm", "yp", "ym", "zp", "zm", "qyp", "qym", "qzp", "qzm")
CHUNK = 2


class Rows:
    def __init__(self, ref, wide, first=-1):
        self.ref, self.wide, self.first = ref, wide, first

    def read(self, row, count=1):
        return self.ref[pl.ds((row - self.first) * self.wide, count * self.wide)]

    def write(self, row, value):
        self.ref[pl.ds((row - self.first) * self.wide, value.shape[0])] = value


def shifted(value, step):
    return pltpu.roll(value, step % value.shape[1], 1)


def next_cells(value, step):
    return pltpu.roll(value, step % value.shape[0], 0)


class Stencil:
    def __init__(self, ref, wide):
        self.at = {name: Rows(ref.at[i], wide) for i, name in enumerate(NAMES)}

    def fill(self, row, raw, space, core):
        d, u0, u1, u2 = raw
        u0 = u0 * (1 - 2 * space).astype(jnp.float32)
        cell = lax.broadcasted_iota(jnp.int32, d.shape, 0)
        depth = lax.broadcasted_iota(jnp.int32, d.shape, 1)
        top = (cell == d.shape[0] - 1) & (core == 1)
        bottom = (cell == 0) & (core == 0)
        last, first = depth == d.shape[1] - 1, depth == 0
        zero = jnp.zeros_like(d)
        values = {
            "c0": 1.0 - 6.0 * d,
            "xp": d - u0,
            "xm": d + u0,
            "yp": jnp.where(top, zero, d - u1),
            "ym": jnp.where(bottom, zero, d + u1),
            "zp": jnp.where(last, zero, d - u2),
            "zm": jnp.where(first, zero, d + u2),
            "qyp": jnp.where(top, zero, next_cells(d + u1, -1)),
            "qym": jnp.where(bottom, zero, next_cells(d - u1, 1)),
            "qzp": jnp.where(last, zero, shifted(d + u2, -1)),
            "qzm": jnp.where(first, zero, shifted(d - u2, 1)),
        }
        for name in NAMES:
            self.at[name].write(row, values[name])

    def edge(self):
        for name in NAMES:
            rows = self.at[name]
            rows.write(-1, jnp.zeros((rows.wide, rows.ref.shape[-1]), jnp.float32))

    def terms(self, fields, row, count, adjoint):
        at = self.at
        if adjoint:
            up, low, ends = at["xm"].read(row + 1, count), at["xp"].read(row - 1, count), ("qyp", "qym", "qzp", "qzm")
        else:
            up, low, ends = at["xp"].read(row, count), at["xm"].read(row, count), ("yp", "ym", "zp", "zm")
        yp, ym, zp, zm = (at[n].read(row, count) for n in ends)
        same = at["c0"].read(row, count)
        result = []
        for v in fields:
            c = v.read(row, count)
            around = up * v.read(row + 1, count) + low * v.read(row - 1, count)
            around = around + (yp * next_cells(c, -1) + ym * next_cells(c, 1))
            around = around + (zp * shifted(c, -1) + zm * shifted(c, 1))
            result.append((around, c, same * c))
        return result

    def fine(self, fields, row, count, adjoint):
        return [own + around for around, c, own in self.terms(fields, row, count, adjoint)]

    def coarse(self, v, row, count, adjoint):
        ((around, c, own),) = self.terms([v], row, count, adjoint)
        return c + float(STEPS) * (around + (own - c))


def chunks(start, stop, size=CHUNK):
    return [(row, min(size, stop - row)) for row in range(start, stop, size)]


def joined(core, own, side):
    return jnp.where(core == 1, jnp.concatenate([side, own], 0), jnp.concatenate([own, side], 0))


def mid(core, cells):
    return jnp.where(core == 1, cells[SIDE:], cells[:-SIDE])


def zeros(rows):
    return jnp.zeros((rows.wide, rows.ref.shape[-1]), jnp.float32)


def pack_kernel(rows, own, where_ref, d_ref, u_ref, control_ref, sg_ref, ag_ref, initial_ref, target_ref,
                x_out, side_out, rims, sides, sem):
    slab, space, core = where_ref[0], where_ref[1], where_ref[2]
    fields = (d_ref, u_ref.at[0], u_ref.at[1], u_ref.at[2], control_ref.at[0], sg_ref.at[0], None, target_ref.at[0])
    starts = (ag_ref.at[0], initial_ref)
    beside = pl.multiple_of(jnp.where(core == 0, own - SIDE, 0), SIDE)
    copies = []

    def bring(source, to):
        copies.append(pltpu.make_async_copy(source, to, sem.at[len(copies)]))
        copies[-1].start()

    def rim(i):
        return pl.ds(jnp.where(space == 0, rows - RIMS[i], 0), RIMS[i])

    def edge(field):
        return field.at[:, pl.ds(beside, SIDE)]

    for i, field in enumerate(starts):
        bring(field.at[rim(6)], rims.at[i])
        bring(edge(field), sides.at[i])
    for i, field in enumerate(fields):
        if field is not None:
            bring(field.at[rim(i)], x_out.at[pl.ds(STARTS[i], RIMS[i])])
            bring(edge(field), side_out.at[i])
    for copy in copies:
        copy.wait()
    x_out[pl.ds(STARTS[6], RIMS[6])] = jnp.where(slab == 0, rims[1], rims[0])
    side_out[6] = jnp.where(slab == 0, sides[1], sides[0])


def inner_kernel(rows, wide, where_ref, d_hbm, u_hbm, control_hbm, sg_hbm, ag_hbm, initial_hbm, target_hbm, side_ref,
                 coef_out, hist_out, kept_out, z_out, base_out, state_out, control_ref,
                 c_a, c_b, g_a, g_b, s_a, s_b, con_ref, d_ref, u_ref, sg_ref, ag_ref, initial_ref, target_ref, sem):
    ins = (d_hbm, u_hbm, control_hbm, sg_hbm, ag_hbm, initial_hbm, target_hbm)
    outs = (d_ref, u_ref, control_ref, sg_ref, ag_ref, initial_ref, target_ref)
    copies = [pltpu.make_async_copy(a, b, sem.at[i]) for i, (a, b) in enumerate(zip(ins, outs))]
    for copy in copies:
        copy.start()
    for copy in copies:
        copy.wait()
    slab, space, core = where_ref[0], where_ref[1], where_ref[2]
    first = slab == 0
    c, g, s = ([Rows(r, wide) for r in pair] for pair in ((c_a, c_b), (g_a, g_b), (s_a, s_b)))
    con = Rows(con_ref, wide, 0)
    for field in (*c, *g, *s):
        field.write(-1, zeros(field))
    stencil = Stencil(coef_out, wide)
    stencil.edge()

    def natural(row):
        return jnp.where(space == 1, rows - 1 - row, row)

    def mine(i, own, row):
        return joined(core, own, side_ref[i, natural(row)])

    for row in range(rows):
        at = natural(row)
        stencil.fill(row, [mine(0, d_ref[at], row)] + [mine(1 + i, u_ref[i, at], row) for i in range(3)], space, core)
        con.write(row, mine(4, control_ref[0, at], row))
        g[0].write(row, mine(5, sg_ref[0, at], row))
        start = mine(6, initial_ref[at], row)
        c[0].write(row, jnp.where(first, start, jnp.zeros_like(start)))
        s[0].write(row, mine(6, ag_ref[0, at], row))

    low = rows - STEPS
    for row in range(low, rows):
        values = (con.read(row), g[0].read(row), s[0].read(row), mine(7, target_ref[0, natural(row)], row))
        for i, value in enumerate(values):
            kept_out[i, pl.ds((row - low) * wide, wide)] = value

    def keep(level, fields):
        for i, field in enumerate(fields):
            hist_out[i, level] = field.read(rows - 2 - level, 2)

    keep(0, (c[0], g[0], s[0]))
    for step in range(STEPS):
        now, later = step % 2, 1 - step % 2
        for row, count in chunks(0, rows - 1 - step):
            to_c, to_g = stencil.fine((c[now], g[now]), row, count, False)
            (to_s,) = stencil.fine((s[now],), row, count, True)
            c[later].write(row, to_c + con.read(row, count))
            g[later].write(row, to_g)
            s[later].write(row, to_s)
        if step < STEPS - 1:
            keep(step + 1, (c[later], g[later], s[later]))
    cc, dd = c[1], s[1]
    ready = rows - STEPS
    for row in range(ready):
        sg = mine(5, sg_ref[0, natural(row)], row)
        gap = c[0].read(row) - sg
        ag = mine(6, ag_ref[0, natural(row)], row)
        state = sg + gap
        rest = state - mine(7, target_ref[0, natural(row)], row) - ag
        cc.write(row, gap)
        dd.write(row, rest)
        state_out[row] = mid(core, state)
        base_out[row] = mid(core, ag + rest)
    keep(STEPS, (cc, g[0], s[0], dd))
    for row, count in chunks(0, ready - 1):
        x = g[0].read(row, count) + stencil.coarse(cc, row, count, False)
        e = s[0].read(row, count) + stencil.coarse(dd, row, count, True)
        for r in range(count):
            z_out[row + r] = mid(core, x[r * wide : (r + 1) * wide])
            z_out[ready - 1 + row + r] = mid(core, e[r * wide : (r + 1) * wide])


def wedge_kernel(rows, wide, where_ref, coef_in, hist_ref, kept_ref, xr_ref, ys_ref,
                 coef_out, z_out, x_out, base_out, state_out, c_a, c_b, g_a, g_b, s_a, s_b, con_ref):
    slab, space, core = where_ref[0], where_ref[1], where_ref[2]
    first = slab == 0
    flip = space == 1
    c, g, s = (
        [[Rows(r, wide, rows - 2 - level) for r in pair] for level in range(STEPS + 1)]
        for pair in ((c_a, c_b), (g_a, g_b), (s_a, s_b))
    )
    at_level = lambda field, level: field[level][level % 2]
    low = rows - STEPS
    con = Rows(con_ref, wide, low)
    con.write(low, kept_ref[0])
    stencil = Stencil(coef_out, wide)

    def natural(row):
        return jnp.where(flip, rows - 1 - row, row)

    def rim(i, j):
        at = STARTS[i] + jnp.where(flip, RIMS[i] - 1 - j, j)
        return joined(core, xr_ref[at], ys_ref[at])

    for j in range(NEAR):
        stencil.fill(rows + j, [rim(i, j) for i in range(4)], space, core)
    for j in range(NEAR):
        con.write(rows + j, rim(4, j))
    for j in range(NEAR + 1):
        start = rim(6, j)
        c[0][0].write(rows + j, jnp.where(first, start, jnp.zeros_like(start)))
        if j < NEAR:
            s[0][0].write(rows + j, start)
            g[0][0].write(rows + j, rim(5, j))

    def restore(level, fields):
        for i, field in enumerate(fields):
            field.write(rows - 2 - level, hist_ref[i, level])

    restore(0, (c[0][0], g[0][0], s[0][0]))
    for level in range(STEPS):
        row = rows - 1 - level
        nc, ng, ns = (at_level(f, level) for f in (c, g, s))
        lc, lg, ls = (at_level(f, level + 1) for f in (c, g, s))
        for r, count in chunks(row, row + NEAR):
            to_c, to_g = stencil.fine((nc, ng), r, count, False)
            (to_s,) = stencil.fine((ns,), r, count, True)
            lc.write(r, to_c + con.read(r, count))
            lg.write(r, to_g)
            ls.write(r, to_s)
        (to_c,) = stencil.fine((nc,), row + NEAR, 1, False)
        lc.write(row + NEAR, to_c + con.read(row + NEAR))
        if level < STEPS - 1:
            restore(level + 1, (lc, lg, ls))
    fc, fg, fs = (at_level(f, STEPS) for f in (c, g, s))
    cc, dd = c[STEPS][1], s[STEPS][1]
    restore(STEPS, (cc, fg, fs, dd))
    count = NEAR + 1
    sg = jnp.concatenate([kept_ref[1], rim(5, 0)], 0)
    gap = fc.read(low, count) - sg
    state = sg + gap
    ag = jnp.concatenate([kept_ref[2], rim(6, 0)], 0)
    rest = state - jnp.concatenate([kept_ref[3], rim(7, 0)], 0) - ag
    cc.write(low, gap)
    dd.write(low, rest)
    base = ag + rest

    def cells(value, r):
        return mid(core, value[r * wide : (r + 1) * wide])

    for r in range(NEAR):
        state_out[r] = cells(state, r)
        base_out[r] = cells(base, r)
    for r in range(count):
        row = low - 1 + r
        x_row = mid(core, fg.read(row) + stencil.coarse(cc, row, 1, False))
        e_row = mid(core, fs.read(row) + stencil.coarse(dd, row, 1, True))
        z_out[r] = x_row
        z_out[count + r] = e_row
        if count - 1 - r < FAR_X:
            x_out[count - 1 - r] = x_row
        if count - 1 - r < FAR_E:
            x_out[FAR_X + count - 1 - r] = e_row


def sorted_pair(core, odd, lower, higher, row, mine, mine_y, other, other_y, at):
    a, b = joined(core, mine[at], mine_y[at]), joined(core, other[at], other_y[at])
    lower.write(row, jnp.where(odd, b, a))
    higher.write(row, jnp.where(odd, a, b))


def message_kernel(rows, wide, where_ref, coef_ref, za, zb, ra, rb, xr, xzr, za_y, zb_y, ra_y, rb_y, xr_y, xzr_y,
                   msg_out, turn_out, h_out, xa_out, eb_out, xb_s, ea_s):
    slab, space, core = where_ref[0], where_ref[1], where_ref[2]
    odd = slab % 2 == 1
    upper = slab >= 2
    stencil = Stencil(coef_ref, wide)
    xa, xb, ea, eb, h = fields = [Rows(r, wide) for r in (xa_out, xb_s, ea_s, eb_out, h_out)]
    for field in fields:
        field.write(-1, zeros(field))
    inner = rows - NEAR - 1
    for row in range(inner):
        sorted_pair(core, odd, xa, xb, row, za, za_y, ra, ra_y, row)
        sorted_pair(core, odd, ea, eb, row, za, za_y, ra, ra_y, inner + row)
    for row in range(inner, rows):
        sorted_pair(core, odd, xa, xb, row, zb, zb_y, rb, rb_y, row - inner)
        sorted_pair(core, odd, ea, eb, row, zb, zb_y, rb, rb_y, rows - inner + row - inner)
    for j in range(FAR_X):
        sorted_pair(core, odd, xa, xb, rows + j, xr, xr_y, xzr, xzr_y, j)
    for j in range(FAR_E):
        sorted_pair(core, odd, ea, eb, rows + j, xr, xr_y, xzr, xzr_y, FAR_X + j)

    def send(row, count, value):
        for r in range(row, min(row + count, rows)):
            cells = mid(core, value[(r - row) * wide : (r - row + 1) * wide])
            msg_out[r] = cells
            if r >= rows - MSG:
                turn_out[rows - 1 - r] = cells

    @pl.when(jnp.logical_not(upper))
    def _():
        for row, count in chunks(0, rows + FAR_X - 1):
            value = xb.read(row, count) + stencil.coarse(xa, row, count, False)
            h.write(row, value)
            send(row, count, value)

    @pl.when(upper)
    def _():
        for row, count in chunks(0, rows + 1):
            h.write(row, eb.read(row, count) + stencil.coarse(xa, row, count, True))
        for row, count in chunks(0, rows):
            send(row, count, ea.read(row, count) + stencil.coarse(h, row, count, True))


def base_kernel(rows, wide, where_ref, coef_ref, h_ref, xa_ref, eb_ref, start_a, start_b, base_out, edge_out, t1_s, t2_s):
    slab, core = where_ref[0], where_ref[2]
    odd = slab % 2 == 1
    upper = slab >= 2
    stencil = Stencil(coef_ref, wide)
    h, xa, eb, t1, t2 = (Rows(r, wide) for r in (h_ref, xa_ref, eb_ref, t1_s, t2_s))
    for field in (t1, t2):
        field.write(-1, zeros(field))

    def put(source):
        for row in range(rows):
            start = start_a[row] if row < start_a.shape[0] else start_b[row - start_a.shape[0]]
            value = start + mid(core, source.read(row))
            base_out[row] = value
            if row >= rows - LATE:
                edge_out[rows - 1 - row] = value

    @pl.when(jnp.logical_not(upper))
    def _():
        for row, count in chunks(0, rows + FAR_X - 2):
            t1.write(row, stencil.coarse(h, row, count, False))
        for row, count in chunks(0, rows + FAR_X - 3):
            t2.write(row, h.read(row, count) + stencil.coarse(t1, row, count, True))
        for row, count in chunks(0, rows + FAR_X - 4):
            t1.write(row, xa.read(row, count) + stencil.coarse(t2, row, count, True))

        @pl.when(odd)
        def _():
            put(t1)

        @pl.when(jnp.logical_not(odd))
        def _():
            for row, count in chunks(0, rows):
                t2.write(row, eb.read(row, count) + stencil.coarse(t1, row, count, True))
            put(t2)

    @pl.when(upper & odd)
    def _():
        put(xa)

    @pl.when(upper & jnp.logical_not(odd))
    def _():
        put(h)


def last_kernel(rows, wide, where_ref, coef_ref, msg, msg_y, base, base_y, xa_ref, state_a, state_b, control_ref,
                state_hbm, gradient_hbm, m_s, t0_s, t1_s, total_s, state_out, gradient_out, sem):
    slab, space, core = where_ref[0], where_ref[1], where_ref[2]
    stencil = Stencil(coef_ref, wide)
    m, t0, t1, total, xa = (Rows(r, wide) for r in (m_s, t0_s, t1_s, total_s, xa_ref))
    for field in (m, t0, t1):
        field.write(-1, zeros(field))

    def natural(row):
        return jnp.where(space == 1, rows - 1 - row, row)

    def state(came):
        for row in range(rows):
            before = state_a[row] if row < state_a.shape[0] else state_b[row - state_a.shape[0]]
            state_out[natural(row)] = before + mid(core, came(row)) if came else before

    def begin(extra):
        for row, count in chunks(0, rows + LATE):
            ready = jnp.concatenate([joined(core, base[r], base_y[r]) for r in range(row, row + count)], 0)
            t1.write(row, ready + extra(row, count))

    for row in range(rows + MSG):
        m.write(row, joined(core, msg[row], msg_y[row]))

    @pl.when(slab == 0)
    def _():
        begin(lambda row, count: stencil.coarse(m, row, count, True))
        state(None)

    @pl.when(slab == 1)
    def _():
        begin(m.read)
        state(xa.read)

    @pl.when(slab >= 2)
    def _():
        for row, count in chunks(0, rows + MSG - 1):
            t0.write(row, stencil.coarse(m, row, count, False))

    @pl.when(slab == 2)
    def _():
        begin(lambda row, count: m.read(row, count) + stencil.coarse(t0, row, count, True))
        state(m.read)

    @pl.when(slab == 3)
    def _():
        begin(t0.read)
        state(lambda row: xa.read(row) + t0.read(row))

    copies = [pltpu.make_async_copy(state_out, state_hbm.at[0], sem.at[0])]
    copies[0].start()
    pair = (t1, m)
    for step in range(STEPS - 1):
        now, later = pair[step % 2], pair[1 - step % 2]
        for row, count in chunks(0, rows + LATE - 1 - step):
            (value,) = stencil.fine((now,), row, count, True)
            if step < STEPS - 2:
                later.write(row, value)
            count = min(count, rows - row)
            if count > 0:
                value = value[: count * wide] + (total if step else now).read(row, count)
                if step < STEPS - 2:
                    total.write(row, value)
                else:
                    for r in range(count):
                        at = natural(row + r)
                        own = mid(core, value[r * wide : (r + 1) * wide])
                        gradient_out[at] = own / float(STEPS) + 0.5 * control_ref[0, at]
                    if (row + count) % 8 and row + count < rows:
                        continue
                    begin_at, size = row + count - 8, 8
                    part = pl.ds(jnp.where(space == 1, rows - begin_at - size, begin_at), size)
                    copies.append(pltpu.make_async_copy(gradient_out.at[part], gradient_hbm.at[0, part], sem.at[len(copies)]))
                    copies[-1].start()
    for copy in copies:
        copy.wait()


def call(kernel, outs, scratch, *args, alias=None, in_hbm=0, target=pltpu.VMEM):
    return pl.pallas_call(
        kernel,
        out_shape=[jax.ShapeDtypeStruct(shape, jnp.float32) for shape in outs],
        in_specs=[pl.BlockSpec(memory_space=pltpu.SMEM)]
        + [pl.BlockSpec(memory_space=pltpu.HBM if i < in_hbm else pltpu.VMEM) for i in range(len(args) - 1)],
        out_specs=[pl.BlockSpec(memory_space=target)] * len(outs),
        scratch_shapes=[pltpu.VMEM(shape, jnp.float32) if isinstance(shape, tuple) else shape for shape in scratch],
        input_output_aliases=alias or {},
        compiler_params=pltpu.CompilerParams(vmem_limit_bytes=24 * 1024 * 1024),
        cost_estimate=pl.CostEstimate(flops=1000, bytes_accessed=1000, transcendentals=0),
    )(*args)


def swapped(block, axis):
    return lax.ppermute(block, axis, [(0, 1), (1, 0)])


def across(block, distance):
    return lax.ppermute(block, "tm", [(i, i ^ distance) for i in range(4)])


def across_turned(block, distance):
    route = [(2 * i + j, 2 * (i ^ distance) + 1 - j) for i in range(4) for j in range(2)]
    return lax.ppermute(block, ("tm", "space"), route)


def four_slabs(initial, diffusion, velocity, control, target, state_guess, adjoint_guess):
    rows, own, depth = diffusion.shape
    wide = own + SIDE
    slab, space, core = lax.axis_index("tm"), lax.axis_index("space"), lax.axis_index("yz")
    where = jnp.stack([slab, space, core]).astype(jnp.int32)
    def edge(block):
        return lax.dynamic_slice_in_dim(block, jnp.where(core == 0, own - SIDE, 0), SIDE, axis=block.ndim - 2)

    def flat(count):
        return (count * wide, depth)

    def sent(*groups):
        sizes = [sum(e.shape[0] for e in group) for group in groups]
        got = swapped(jnp.concatenate([e for group in groups for e in group], 0), "yz")
        return [got[sum(sizes[:i]) : sum(sizes[: i + 1])] for i in range(len(sizes))]

    inputs = (diffusion, velocity, control, state_guess, adjoint_guess, initial, target)
    shapes = [a.shape for a in inputs]
    inputs = [pltpu.with_memory_space_constraint(a, pltpu.HBM) for a in inputs]
    cells = lambda count: (count, own, depth)
    edges = (rows, SIDE, depth)
    x_send, side_send = call(
        functools.partial(pack_kernel, rows, own),
        [cells(sum(RIMS)), (len(RIMS), *edges)],
        [(2, *cells(RIMS[6])), (2, *edges), pltpu.SemaphoreType.DMA((2 * len(RIMS) + 2,))],
        where, *inputs,
        in_hbm=len(inputs),
    )
    x_here = swapped(x_send, "space")
    side = swapped(side_send, "yz")
    coefs = (len(NAMES), *flat(rows + NEAR + 1))
    inner = rows - NEAR - 1
    tall = flat(rows + MSG + 2)
    loaded = [shape for i, shape in enumerate(shapes) if i != 2]
    coef, hist, last, z_a, base_a, state_a, control = call(
        functools.partial(inner_kernel, rows, wide),
        [coefs, (4, STEPS + 1, *flat(2)), (4, *flat(NEAR)), cells(2 * inner), cells(inner + 1), cells(inner + 1), shapes[2]],
        [flat(rows + 2)] * 6 + [flat(rows)] + loaded + [pltpu.SemaphoreType.DMA((len(inputs),))],
        where, *inputs, side,
        in_hbm=len(inputs),
    )
    r_a = across(z_a, 1)
    x_here, coef = lax.optimization_barrier((x_here, coef))
    x_side = swapped(edge(x_here), "yz")
    coef, z_b, x_out, base_b, state_b = call(
        functools.partial(wedge_kernel, rows, wide),
        [coefs, cells(2 * NEAR + 2), cells(FAR_X + FAR_E), cells(NEAR), cells(NEAR)],
        [flat(NEAR + 5)] * 6 + [flat(2 * NEAR)],
        where, coef, hist, last, x_here, x_side,
        alias={1: 0},
    )
    x_in = swapped(x_out, "space")
    xz_in = across_turned(x_out, 1)
    r_b = across(z_b, 1)
    za_y, ra_y = sent([edge(z_a)], [edge(r_a)])
    r_b, za_y, ra_y = lax.optimization_barrier((r_b, za_y, ra_y))
    xr_y, xzr_y, zb_y, rb_y = sent([edge(x_in)], [edge(xz_in)], [edge(z_b)], [edge(r_b)])
    msg, turn, h, xa, eb = call(
        functools.partial(message_kernel, rows, wide),
        [cells(rows), cells(MSG), tall, tall, tall],
        [tall, tall],
        where, coef, z_a, z_b, r_a, r_b, x_in, xz_in, za_y, zb_y, ra_y, rb_y, xr_y, xzr_y,
    )
    msg_in = across(msg, 3)
    turn_in = across_turned(turn, 3)
    base, base_edge = call(
        functools.partial(base_kernel, rows, wide),
        [cells(rows), cells(LATE)],
        [tall, tall],
        where, coef, h, xa, eb, base_a, base_b,
    )
    base_x = swapped(base_edge, "space")
    msg_in, base_x = lax.optimization_barrier((jnp.concatenate([msg_in, turn_in], 0), base_x))
    base = jnp.concatenate([base, base_x], 0)
    msg_y, base_y = sent([edge(msg_in)], [edge(base)])
    return call(
        functools.partial(last_kernel, rows, wide),
        [(1, *cells(rows)), (1, *cells(rows))],
        [tall] * 4 + [cells(rows)] * 2 + [pltpu.SemaphoreType.DMA((1 + rows // 8,))],
        where, coef, msg_in, msg_y, base, base_y, xa, state_a, state_b, control,
        target=pltpu.HBM,
    )


def solution(mesh):
    sizes = mesh.shape

    def local(*args):
        rows, own, depth = args[1].shape
        fits = (sizes["tm"], sizes["space"], sizes["yz"]) == (4, 2, 2)
        fits = fits and rows >= 2 * (NEAR + 1) and rows % 8 == 0 and own % 8 == 0 and own >= SIDE and depth % 128 == 0
        return four_slabs(*args) if fits else any_mesh(*args)

    field = P(("groups", "space"), "yz", None)
    slabs = P("tm", ("groups", "space"), "yz", None)
    return jax.shard_map(
        local,
        mesh=mesh,
        in_specs=(field, field, P(None, ("groups", "space"), "yz", None), slabs, slabs, slabs, slabs),
        out_specs=(slabs, slabs),
        check_vma=False,
    )
```

```python
import functools

import jax
import jax.numpy as jnp
from jax import lax
from jax.experimental import pallas as pl
from jax.experimental.pallas import tpu as pltpu
from jax.sharding import PartitionSpec as P

STEPS = 6
SIDE = 8
NEAR = 6
LATE = 5
MSG = 7
FAR_X = 5
FAR_E = 1
RIMS = (NEAR, NEAR, NEAR, NEAR, NEAR, NEAR, NEAR + 1, 1)
STARTS = tuple(sum(RIMS[:i]) for i in range(len(RIMS)))


def extended(array, sides, width):
    for axis, dim in sides:
        peers, length = (lax.axis_size(axis), array.shape[dim])
        up = [(i, (i + 1) % peers) for i in range(peers - 1)]
        down = [(j, i) for i, j in up]
        last = lax.slice_in_dim(array, length - width, length, axis=dim)
        first = lax.slice_in_dim(array, 0, width, axis=dim)
        before = lax.ppermute(last, axis, up)
        after = lax.ppermute(first, axis, down)
        array = jnp.concatenate([before, array, after], axis=dim)
    return array


def passed_along(block, axis, distance):
    devices = range(lax.axis_size(axis))
    route = [(i - distance, i) for i in devices if i - distance in devices]
    return lax.ppermute(block, axis, route)


def depth_pad(field):
    return jnp.pad(field, ((0, 0), (0, 0), (1, 1)))


def local_map(padded, coefficients, factor, adjoint):
    centre = padded[1:-1, 1:-1, :]
    if adjoint:
        spread = coefficients[0] * padded
        carried = coefficients[1:4] * padded
        inner_spread = spread[1:-1, 1:-1, :]
        deep = depth_pad(inner_spread)
        laplace = (
            spread[2:, 1:-1, :]
            + spread[:-2, 1:-1, :]
            + spread[1:-1, 2:, :]
            + spread[1:-1, :-2, :]
            + deep[:, :, 2:]
            + deep[:, :, :-2]
            - 6.0 * inner_spread
        )
        deep_carry = depth_pad(carried[2, 1:-1, 1:-1, :])
        transport = (
            carried[0, 2:, 1:-1, :]
            - carried[0, :-2, 1:-1, :]
            + (carried[1, 1:-1, 2:, :] - carried[1, 1:-1, :-2, :])
            + (deep_carry[:, :, 2:] - deep_carry[:, :, :-2])
        )
        return (centre + factor * (laplace + transport)) * coefficients[4, 1:-1, 1:-1, :]
    inner = coefficients[:, 1:-1, 1:-1, :]
    deep = depth_pad(centre)
    laplace = (
        padded[2:, 1:-1, :]
        + padded[:-2, 1:-1, :]
        + padded[1:-1, 2:, :]
        + padded[1:-1, :-2, :]
        + deep[:, :, 2:]
        + deep[:, :, :-2]
        - 6.0 * centre
    )
    transport = (
        inner[1] * (padded[2:, 1:-1, :] - padded[:-2, 1:-1, :])
        + inner[2] * (padded[1:-1, 2:, :] - padded[1:-1, :-2, :])
        + inner[3] * (deep[:, :, 2:] - deep[:, :, :-2])
    )
    return centre + factor * (inner[0] * laplace - transport)


def halo_cells(field):
    return extended(field, (("space", 0), ("yz", 1)), 1)


def coarse_chain(residual, near_coefficients, adjoint, direction):
    factor = float(STEPS)

    def one_turn(turn_index, correction):
        moved = local_map(halo_cells(correction), near_coefficients, factor, adjoint)
        arrived = passed_along(moved, "tm", direction)
        return residual + arrived

    return lax.fori_loop(0, lax.axis_size("tm") - 1, one_turn, residual)


def any_mesh(initial, diffusion, velocity, control, target, state_guess, adjoint_guess):
    source = control[0]
    guess_state = state_guess[0]
    guess_adjoint = adjoint_guess[0]
    stacked = jnp.concatenate([diffusion[None], velocity, jnp.ones_like(diffusion)[None]], 0)
    near_coefficients = extended(stacked, (("space", 1), ("yz", 2)), 1)
    arrived = passed_along(guess_state, "tm", 1)
    fine = jnp.where(lax.axis_index("tm") == 0, initial, arrived)
    sweep = guess_adjoint
    for step_index in range(STEPS):
        fine = local_map(halo_cells(fine), near_coefficients, 1.0, False) + source
    for step_index in range(STEPS):
        sweep = local_map(halo_cells(sweep), near_coefficients, 1.0, True)
    state_residual = fine - guess_state
    state_new = guess_state + coarse_chain(state_residual, near_coefficients, False, 1)
    from_next = passed_along(sweep, "tm", -1)
    adjoint_residual = from_next + state_new - target[0] - guess_adjoint
    multiplier = guess_adjoint + coarse_chain(adjoint_residual, near_coefficients, True, -1)
    running_sum = multiplier
    for step_index in range(STEPS - 1):
        multiplier = local_map(halo_cells(multiplier), near_coefficients, 1.0, True)
        running_sum = running_sum + multiplier
    gradient = running_sum / float(STEPS) + 0.5 * source
    return (state_new[None], gradient[None])


NAMES = ("c0", "xp", "xm", "yp", "ym", "zp", "zm", "qyp", "qym", "qzp", "qzm")
CHUNK = 2


class Rows:
    def __init__(self, ref, wide, first=-1):
        self.ref, self.wide, self.first = ref, wide, first

    def read(self, row, count=1):
        return self.ref[pl.ds((row - self.first) * self.wide, count * self.wide)]

    def write(self, row, value):
        self.ref[pl.ds((row - self.first) * self.wide, value.shape[0])] = value


def shifted(value, step):
    return pltpu.roll(value, step % value.shape[1], 1)


def next_cells(value, step):
    return pltpu.roll(value, step % value.shape[0], 0)


class Stencil:
    def __init__(self, ref, wide):
        self.at = {name: Rows(ref.at[i], wide) for i, name in enumerate(NAMES)}

    def fill(self, row, raw, space, core):
        d, u0, u1, u2 = raw
        u0 = u0 * (1 - 2 * space).astype(jnp.float32)
        cell = lax.broadcasted_iota(jnp.int32, d.shape, 0)
        depth = lax.broadcasted_iota(jnp.int32, d.shape, 1)
        top = (cell == d.shape[0] - 1) & (core == 1)
        bottom = (cell == 0) & (core == 0)
        last, first = depth == d.shape[1] - 1, depth == 0
        zero = jnp.zeros_like(d)
        values = {
            "c0": 1.0 - 6.0 * d,
            "xp": d - u0,
            "xm": d + u0,
            "yp": jnp.where(top, zero, d - u1),
            "ym": jnp.where(bottom, zero, d + u1),
            "zp": jnp.where(last, zero, d - u2),
            "zm": jnp.where(first, zero, d + u2),
            "qyp": jnp.where(top, zero, next_cells(d + u1, -1)),
            "qym": jnp.where(bottom, zero, next_cells(d - u1, 1)),
            "qzp": jnp.where(last, zero, shifted(d + u2, -1)),
            "qzm": jnp.where(first, zero, shifted(d - u2, 1)),
        }
        for name in NAMES:
            self.at[name].write(row, values[name])

    def edge(self):
        for name in NAMES:
            rows = self.at[name]
            rows.write(-1, jnp.zeros((rows.wide, rows.ref.shape[-1]), jnp.float32))

    def terms(self, fields, row, count, adjoint):
        at = self.at
        if adjoint:
            up, low, ends = at["xm"].read(row + 1, count), at["xp"].read(row - 1, count), ("qyp", "qym", "qzp", "qzm")
        else:
            up, low, ends = at["xp"].read(row, count), at["xm"].read(row, count), ("yp", "ym", "zp", "zm")
        yp, ym, zp, zm = (at[n].read(row, count) for n in ends)
        same = at["c0"].read(row, count)
        result = []
        for v in fields:
            c = v.read(row, count)
            around = up * v.read(row + 1, count) + low * v.read(row - 1, count)
            around = around + (yp * next_cells(c, -1) + ym * next_cells(c, 1))
            around = around + (zp * shifted(c, -1) + zm * shifted(c, 1))
            result.append((around, c, same * c))
        return result

    def fine(self, fields, row, count, adjoint):
        return [own + around for around, c, own in self.terms(fields, row, count, adjoint)]

    def coarse(self, v, row, count, adjoint):
        ((around, c, own),) = self.terms([v], row, count, adjoint)
        return c + float(STEPS) * (around + (own - c))


def chunks(start, stop, size=CHUNK):
    return [(row, min(size, stop - row)) for row in range(start, stop, size)]


def joined(core, own, side):
    return jnp.where(core == 1, jnp.concatenate([side, own], 0), jnp.concatenate([own, side], 0))


def mid(core, cells):
    return jnp.where(core == 1, cells[SIDE:], cells[:-SIDE])


def zeros(rows):
    return jnp.zeros((rows.wide, rows.ref.shape[-1]), jnp.float32)


def pack_kernel(rows, own, where_ref, d_ref, u_ref, control_ref, sg_ref, ag_ref, initial_ref, target_ref,
                x_out, side_out, sem):
    slab, space, core = where_ref[0], where_ref[1], where_ref[2]
    fields = (d_ref, u_ref.at[0], u_ref.at[1], u_ref.at[2], control_ref.at[0], sg_ref.at[0], None, target_ref.at[0])
    starts = (ag_ref.at[0], initial_ref)
    beside = pl.multiple_of(jnp.where(core == 0, own - SIDE, 0), SIDE)
    copies = []

    def bring(source, to):
        copies.append(pltpu.make_async_copy(source, to, sem.at[len(copies)]))
        copies[-1].start()

    def rim(i):
        return pl.ds(jnp.where(space == 0, rows - RIMS[i], 0), RIMS[i])

    def edge(field):
        return field.at[:, pl.ds(beside, SIDE)]

    def begin(field):
        at = pl.ds(STARTS[6], RIMS[6])
        return [
            pltpu.make_async_copy(field.at[rim(6)], x_out.at[at], sem.at[2 * len(RIMS)]),
            pltpu.make_async_copy(edge(field), side_out.at[6], sem.at[2 * len(RIMS) + 1]),
        ]

    for wanted, field in zip((slab != 0, slab == 0), starts):

        @pl.when(wanted)
        def _(field=field):
            for copy in begin(field):
                copy.start()

    for i, field in enumerate(fields):
        if field is not None:
            bring(field.at[rim(i)], x_out.at[pl.ds(STARTS[i], RIMS[i])])
            bring(edge(field), side_out.at[i])
    for copy in copies:
        copy.wait()
    for wanted, field in zip((slab != 0, slab == 0), starts):

        @pl.when(wanted)
        def _(field=field):
            for copy in begin(field):
                copy.wait()


def inner_kernel(rows, wide, where_ref, d_hbm, u_hbm, control_hbm, sg_hbm, ag_hbm, initial_hbm, target_hbm, side_ref,
                 coef_out, hist_out, kept_out, z_out, base_out, state_out, control_ref,
                 c_a, c_b, g_a, g_b, s_a, s_b, con_ref, d_ref, u_ref, sg_ref, ag_ref, initial_ref, target_ref, sem):
    ins = (d_hbm, u_hbm, control_hbm, sg_hbm, ag_hbm, initial_hbm, target_hbm)
    outs = (d_ref, u_ref, control_ref, sg_ref, ag_ref, initial_ref, target_ref)
    copies = [pltpu.make_async_copy(a, b, sem.at[i]) for i, (a, b) in enumerate(zip(ins, outs))]
    for copy in copies:
        copy.start()
    for copy in copies:
        copy.wait()
    slab, space, core = where_ref[0], where_ref[1], where_ref[2]
    first = slab == 0
    c, g, s = ([Rows(r, wide) for r in pair] for pair in ((c_a, c_b), (g_a, g_b), (s_a, s_b)))
    con = Rows(con_ref, wide, 0)
    for field in (*c, *g, *s):
        field.write(-1, zeros(field))
    stencil = Stencil(coef_out, wide)
    stencil.edge()

    def natural(row):
        return jnp.where(space == 1, rows - 1 - row, row)

    def mine(i, own, row):
        return joined(core, own, side_ref[i, natural(row)])

    for row in range(rows):
        at = natural(row)
        stencil.fill(row, [mine(0, d_ref[at], row)] + [mine(1 + i, u_ref[i, at], row) for i in range(3)], space, core)
        con.write(row, mine(4, control_ref[0, at], row))
        g[0].write(row, mine(5, sg_ref[0, at], row))
        start = mine(6, initial_ref[at], row)
        c[0].write(row, jnp.where(first, start, jnp.zeros_like(start)))
        s[0].write(row, mine(6, ag_ref[0, at], row))

    low = rows - STEPS
    for row in range(low, rows):
        values = (con.read(row), g[0].read(row), s[0].read(row), mine(7, target_ref[0, natural(row)], row))
        for i, value in enumerate(values):
            kept_out[i, pl.ds((row - low) * wide, wide)] = value

    def keep(level, fields):
        for i, field in enumerate(fields):
            hist_out[i, level] = field.read(rows - 2 - level, 2)

    keep(0, (c[0], g[0], s[0]))
    for step in range(STEPS):
        now, later = step % 2, 1 - step % 2
        for row, count in chunks(0, rows - 1 - step):
            to_c, to_g = stencil.fine((c[now], g[now]), row, count, False)
            (to_s,) = stencil.fine((s[now],), row, count, True)
            c[later].write(row, to_c + con.read(row, count))
            g[later].write(row, to_g)
            s[later].write(row, to_s)
        if step < STEPS - 1:
            keep(step + 1, (c[later], g[later], s[later]))
    cc, dd = c[1], s[1]
    ready = rows - STEPS
    for row in range(ready):
        sg = mine(5, sg_ref[0, natural(row)], row)
        gap = c[0].read(row) - sg
        ag = mine(6, ag_ref[0, natural(row)], row)
        state = sg + gap
        rest = state - mine(7, target_ref[0, natural(row)], row) - ag
        cc.write(row, gap)
        dd.write(row, rest)
        state_out[row] = mid(core, state)
        base_out[row] = mid(core, ag + rest)
    keep(STEPS, (cc, g[0], s[0], dd))
    for row, count in chunks(0, ready - 1):
        x = g[0].read(row, count) + stencil.coarse(cc, row, count, False)
        e = s[0].read(row, count) + stencil.coarse(dd, row, count, True)
        for r in range(count):
            z_out[row + r] = mid(core, x[r * wide : (r + 1) * wide])
            z_out[ready - 1 + row + r] = mid(core, e[r * wide : (r + 1) * wide])


def wedge_kernel(rows, wide, where_ref, coef_in, hist_ref, kept_ref, xr_ref, ys_ref,
                 coef_out, z_out, x_out, base_out, state_out, c_a, c_b, g_a, g_b, s_a, s_b, con_ref):
    slab, space, core = where_ref[0], where_ref[1], where_ref[2]
    first = slab == 0
    flip = space == 1
    c, g, s = (
        [[Rows(r, wide, rows - 2 - level) for r in pair] for level in range(STEPS + 1)]
        for pair in ((c_a, c_b), (g_a, g_b), (s_a, s_b))
    )
    at_level = lambda field, level: field[level][level % 2]
    low = rows - STEPS
    con = Rows(con_ref, wide, low)
    con.write(low, kept_ref[0])
    stencil = Stencil(coef_out, wide)

    def natural(row):
        return jnp.where(flip, rows - 1 - row, row)

    def rim(i, j):
        at = STARTS[i] + jnp.where(flip, RIMS[i] - 1 - j, j)
        return joined(core, xr_ref[at], ys_ref[at])

    for j in range(NEAR):
        stencil.fill(rows + j, [rim(i, j) for i in range(4)], space, core)
    for j in range(NEAR):
        con.write(rows + j, rim(4, j))
    for j in range(NEAR + 1):
        start = rim(6, j)
        c[0][0].write(rows + j, jnp.where(first, start, jnp.zeros_like(start)))
        if j < NEAR:
            s[0][0].write(rows + j, start)
            g[0][0].write(rows + j, rim(5, j))

    def restore(level, fields):
        for i, field in enumerate(fields):
            field.write(rows - 2 - level, hist_ref[i, level])

    restore(0, (c[0][0], g[0][0], s[0][0]))
    for level in range(STEPS):
        row = rows - 1 - level
        nc, ng, ns = (at_level(f, level) for f in (c, g, s))
        lc, lg, ls = (at_level(f, level + 1) for f in (c, g, s))
        for r, count in chunks(row, row + NEAR):
            to_c, to_g = stencil.fine((nc, ng), r, count, False)
            (to_s,) = stencil.fine((ns,), r, count, True)
            lc.write(r, to_c + con.read(r, count))
            lg.write(r, to_g)
            ls.write(r, to_s)
        (to_c,) = stencil.fine((nc,), row + NEAR, 1, False)
        lc.write(row + NEAR, to_c + con.read(row + NEAR))
        if level < STEPS - 1:
            restore(level + 1, (lc, lg, ls))
    fc, fg, fs = (at_level(f, STEPS) for f in (c, g, s))
    cc, dd = c[STEPS][1], s[STEPS][1]
    restore(STEPS, (cc, fg, fs, dd))
    count = NEAR + 1
    sg = jnp.concatenate([kept_ref[1], rim(5, 0)], 0)
    gap = fc.read(low, count) - sg
    state = sg + gap
    ag = jnp.concatenate([kept_ref[2], rim(6, 0)], 0)
    rest = state - jnp.concatenate([kept_ref[3], rim(7, 0)], 0) - ag
    cc.write(low, gap)
    dd.write(low, rest)
    base = ag + rest

    def cells(value, r):
        return mid(core, value[r * wide : (r + 1) * wide])

    for r in range(NEAR):
        state_out[r] = cells(state, r)
        base_out[r] = cells(base, r)
    for r in range(count):
        row = low - 1 + r
        x_row = mid(core, fg.read(row) + stencil.coarse(cc, row, 1, False))
        e_row = mid(core, fs.read(row) + stencil.coarse(dd, row, 1, True))
        z_out[r] = x_row
        z_out[count + r] = e_row
        if count - 1 - r < FAR_X:
            x_out[count - 1 - r] = x_row
        if count - 1 - r < FAR_E:
            x_out[FAR_X + count - 1 - r] = e_row


def sorted_pair(core, odd, lower, higher, row, mine, mine_y, other, other_y, at):
    a, b = joined(core, mine[at], mine_y[at]), joined(core, other[at], other_y[at])
    lower.write(row, jnp.where(odd, b, a))
    higher.write(row, jnp.where(odd, a, b))


def message_kernel(rows, wide, where_ref, coef_ref, za, zb, ra, rb, xr, xzr, za_y, zb_y, ra_y, rb_y, xr_y, xzr_y,
                   msg_out, turn_out, h_out, xa_out, eb_out, xb_s, ea_s):
    slab, space, core = where_ref[0], where_ref[1], where_ref[2]
    odd = slab % 2 == 1
    upper = slab >= 2
    stencil = Stencil(coef_ref, wide)
    xa, xb, ea, eb, h = fields = [Rows(r, wide) for r in (xa_out, xb_s, ea_s, eb_out, h_out)]
    for field in fields:
        field.write(-1, zeros(field))
    inner = rows - NEAR - 1
    for row in range(inner):
        sorted_pair(core, odd, xa, xb, row, za, za_y, ra, ra_y, row)
        sorted_pair(core, odd, ea, eb, row, za, za_y, ra, ra_y, inner + row)
    for row in range(inner, rows):
        sorted_pair(core, odd, xa, xb, row, zb, zb_y, rb, rb_y, row - inner)
        sorted_pair(core, odd, ea, eb, row, zb, zb_y, rb, rb_y, rows - inner + row - inner)
    for j in range(FAR_X):
        sorted_pair(core, odd, xa, xb, rows + j, xr, xr_y, xzr, xzr_y, j)
    for j in range(FAR_E):
        sorted_pair(core, odd, ea, eb, rows + j, xr, xr_y, xzr, xzr_y, FAR_X + j)

    def send(row, count, value):
        for r in range(row, min(row + count, rows)):
            cells = mid(core, value[(r - row) * wide : (r - row + 1) * wide])
            msg_out[r] = cells
            if r >= rows - MSG:
                turn_out[rows - 1 - r] = cells

    @pl.when(jnp.logical_not(upper))
    def _():
        for row, count in chunks(0, rows + FAR_X - 1):
            value = xb.read(row, count) + stencil.coarse(xa, row, count, False)
            h.write(row, value)
            send(row, count, value)

    @pl.when(upper)
    def _():
        for row, count in chunks(0, rows + 1):
            h.write(row, eb.read(row, count) + stencil.coarse(xa, row, count, True))
        for row, count in chunks(0, rows):
            send(row, count, ea.read(row, count) + stencil.coarse(h, row, count, True))


def base_kernel(rows, wide, where_ref, coef_ref, h_ref, xa_ref, eb_ref, start_a, start_b, base_out, edge_out, t1_s, t2_s):
    slab, core = where_ref[0], where_ref[2]
    odd = slab % 2 == 1
    upper = slab >= 2
    stencil = Stencil(coef_ref, wide)
    h, xa, eb, t1, t2 = (Rows(r, wide) for r in (h_ref, xa_ref, eb_ref, t1_s, t2_s))
    for field in (t1, t2):
        field.write(-1, zeros(field))

    def put(source):
        for row in range(rows):
            start = start_a[row] if row < start_a.shape[0] else start_b[row - start_a.shape[0]]
            value = start + mid(core, source.read(row))
            base_out[row] = value
            if row >= rows - LATE:
                edge_out[rows - 1 - row] = value

    @pl.when(jnp.logical_not(upper))
    def _():
        for row, count in chunks(0, rows + FAR_X - 2):
            t1.write(row, stencil.coarse(h, row, count, False))
        for row, count in chunks(0, rows + FAR_X - 3):
            t2.write(row, h.read(row, count) + stencil.coarse(t1, row, count, True))
        for row, count in chunks(0, rows + FAR_X - 4):
            t1.write(row, xa.read(row, count) + stencil.coarse(t2, row, count, True))

        @pl.when(odd)
        def _():
            put(t1)

        @pl.when(jnp.logical_not(odd))
        def _():
            for row, count in chunks(0, rows):
                t2.write(row, eb.read(row, count) + stencil.coarse(t1, row, count, True))
            put(t2)

    @pl.when(upper & odd)
    def _():
        put(xa)

    @pl.when(upper & jnp.logical_not(odd))
    def _():
        put(h)


def last_kernel(rows, wide, where_ref, coef_ref, msg, msg_y, base, base_y, xa_ref, state_a, state_b, control_ref,
                state_hbm, gradient_hbm, m_s, t0_s, t1_s, total_s, state_out, gradient_out, sem):
    slab, space, core = where_ref[0], where_ref[1], where_ref[2]
    stencil = Stencil(coef_ref, wide)
    m, t0, t1, total, xa = (Rows(r, wide) for r in (m_s, t0_s, t1_s, total_s, xa_ref))
    for field in (m, t0, t1):
        field.write(-1, zeros(field))

    def natural(row):
        return jnp.where(space == 1, rows - 1 - row, row)

    def state(came):
        for row in range(rows):
            before = state_a[row] if row < state_a.shape[0] else state_b[row - state_a.shape[0]]
            state_out[natural(row)] = before + mid(core, came(row)) if came else before

    def begin(extra):
        for row, count in chunks(0, rows + LATE):
            ready = jnp.concatenate([joined(core, base[r], base_y[r]) for r in range(row, row + count)], 0)
            t1.write(row, ready + extra(row, count))

    for row in range(rows + MSG):
        m.write(row, joined(core, msg[row], msg_y[row]))

    @pl.when(slab == 0)
    def _():
        begin(lambda row, count: stencil.coarse(m, row, count, True))
        state(None)

    @pl.when(slab == 1)
    def _():
        begin(m.read)
        state(xa.read)

    @pl.when(slab >= 2)
    def _():
        for row, count in chunks(0, rows + MSG - 1):
            t0.write(row, stencil.coarse(m, row, count, False))

    @pl.when(slab == 2)
    def _():
        begin(lambda row, count: m.read(row, count) + stencil.coarse(t0, row, count, True))
        state(m.read)

    @pl.when(slab == 3)
    def _():
        begin(t0.read)
        state(lambda row: xa.read(row) + t0.read(row))

    copies = [pltpu.make_async_copy(state_out, state_hbm.at[0], sem.at[0])]
    copies[0].start()
    pair = (t1, m)
    for step in range(STEPS - 1):
        now, later = pair[step % 2], pair[1 - step % 2]
        for row, count in chunks(0, rows + LATE - 1 - step):
            (value,) = stencil.fine((now,), row, count, True)
            if step < STEPS - 2:
                later.write(row, value)
            count = min(count, rows - row)
            if count > 0:
                value = value[: count * wide] + (total if step else now).read(row, count)
                if step < STEPS - 2:
                    total.write(row, value)
                else:
                    for r in range(count):
                        at = natural(row + r)
                        own = mid(core, value[r * wide : (r + 1) * wide])
                        gradient_out[at] = own / float(STEPS) + 0.5 * control_ref[0, at]
                    if (row + count) % 8 and row + count < rows:
                        continue
                    begin_at, size = row + count - 8, 8
                    part = pl.ds(jnp.where(space == 1, rows - begin_at - size, begin_at), size)
                    copies.append(pltpu.make_async_copy(gradient_out.at[part], gradient_hbm.at[0, part], sem.at[len(copies)]))
                    copies[-1].start()
    for copy in copies:
        copy.wait()


def call(kernel, outs, scratch, *args, alias=None, in_hbm=0, target=pltpu.VMEM):
    return pl.pallas_call(
        kernel,
        out_shape=[jax.ShapeDtypeStruct(shape, jnp.float32) for shape in outs],
        in_specs=[pl.BlockSpec(memory_space=pltpu.SMEM)]
        + [pl.BlockSpec(memory_space=pltpu.HBM if i < in_hbm else pltpu.VMEM) for i in range(len(args) - 1)],
        out_specs=[pl.BlockSpec(memory_space=target)] * len(outs),
        scratch_shapes=[pltpu.VMEM(shape, jnp.float32) if isinstance(shape, tuple) else shape for shape in scratch],
        input_output_aliases=alias or {},
        compiler_params=pltpu.CompilerParams(vmem_limit_bytes=24 * 1024 * 1024),
        cost_estimate=pl.CostEstimate(flops=1000, bytes_accessed=1000, transcendentals=0),
    )(*args)


def swapped(block, axis):
    return lax.ppermute(block, axis, [(0, 1), (1, 0)])


def across(block, distance):
    return lax.ppermute(block, "tm", [(i, i ^ distance) for i in range(4)])


def across_turned(block, distance):
    route = [(2 * i + j, 2 * (i ^ distance) + 1 - j) for i in range(4) for j in range(2)]
    return lax.ppermute(block, ("tm", "space"), route)


def four_slabs(initial, diffusion, velocity, control, target, state_guess, adjoint_guess):
    rows, own, depth = diffusion.shape
    wide = own + SIDE
    slab, space, core = lax.axis_index("tm"), lax.axis_index("space"), lax.axis_index("yz")
    where = jnp.stack([slab, space, core]).astype(jnp.int32)
    def edge(block):
        return lax.dynamic_slice_in_dim(block, jnp.where(core == 0, own - SIDE, 0), SIDE, axis=block.ndim - 2)

    def flat(count):
        return (count * wide, depth)

    def sent(*groups):
        sizes = [sum(e.shape[0] for e in group) for group in groups]
        got = swapped(jnp.concatenate([e for group in groups for e in group], 0), "yz")
        return [got[sum(sizes[:i]) : sum(sizes[: i + 1])] for i in range(len(sizes))]

    inputs = (diffusion, velocity, control, state_guess, adjoint_guess, initial, target)
    shapes = [a.shape for a in inputs]
    inputs = [pltpu.with_memory_space_constraint(a, pltpu.HBM) for a in inputs]
    cells = lambda count: (count, own, depth)
    edges = (rows, SIDE, depth)
    x_send, side_send = call(
        functools.partial(pack_kernel, rows, own),
        [cells(sum(RIMS)), (len(RIMS), *edges)],
        [pltpu.SemaphoreType.DMA((2 * len(RIMS) + 2,))],
        where, *inputs,
        in_hbm=len(inputs),
    )
    x_here = swapped(x_send, "space")
    side = swapped(side_send, "yz")
    coefs = (len(NAMES), *flat(rows + NEAR + 1))
    inner = rows - NEAR - 1
    tall = flat(rows + MSG + 2)
    loaded = [shape for i, shape in enumerate(shapes) if i != 2]
    coef, hist, last, z_a, base_a, state_a, control = call(
        functools.partial(inner_kernel, rows, wide),
        [coefs, (4, STEPS + 1, *flat(2)), (4, *flat(NEAR)), cells(2 * inner), cells(inner + 1), cells(inner + 1), shapes[2]],
        [flat(rows + 2)] * 6 + [flat(rows)] + loaded + [pltpu.SemaphoreType.DMA((len(inputs),))],
        where, *inputs, side,
        in_hbm=len(inputs),
    )
    r_a = across(z_a, 1)
    x_here, coef = lax.optimization_barrier((x_here, coef))
    x_side = swapped(edge(x_here), "yz")
    coef, z_b, x_out, base_b, state_b = call(
        functools.partial(wedge_kernel, rows, wide),
        [coefs, cells(2 * NEAR + 2), cells(FAR_X + FAR_E), cells(NEAR), cells(NEAR)],
        [flat(NEAR + 5)] * 6 + [flat(2 * NEAR)],
        where, coef, hist, last, x_here, x_side,
        alias={1: 0},
    )
    x_in = swapped(x_out, "space")
    xz_in = across_turned(x_out, 1)
    r_b = across(z_b, 1)
    za_y, ra_y = sent([edge(z_a)], [edge(r_a)])
    r_b, za_y, ra_y = lax.optimization_barrier((r_b, za_y, ra_y))
    xr_y, xzr_y, zb_y, rb_y = sent([edge(x_in)], [edge(xz_in)], [edge(z_b)], [edge(r_b)])
    msg, turn, h, xa, eb = call(
        functools.partial(message_kernel, rows, wide),
        [cells(rows), cells(MSG), tall, tall, tall],
        [tall, tall],
        where, coef, z_a, z_b, r_a, r_b, x_in, xz_in, za_y, zb_y, ra_y, rb_y, xr_y, xzr_y,
    )
    msg_in = across(msg, 3)
    turn_in = across_turned(turn, 3)
    base, base_edge = call(
        functools.partial(base_kernel, rows, wide),
        [cells(rows), cells(LATE)],
        [tall, tall],
        where, coef, h, xa, eb, base_a, base_b,
    )
    base_x = swapped(base_edge, "space")
    msg_in, base_x = lax.optimization_barrier((jnp.concatenate([msg_in, turn_in], 0), base_x))
    base = jnp.concatenate([base, base_x], 0)
    msg_y, base_y = sent([edge(msg_in)], [edge(base)])
    return call(
        functools.partial(last_kernel, rows, wide),
        [(1, *cells(rows)), (1, *cells(rows))],
        [tall] * 4 + [cells(rows)] * 2 + [pltpu.SemaphoreType.DMA((1 + rows // 8,))],
        where, coef, msg_in, msg_y, base, base_y, xa, state_a, state_b, control,
        target=pltpu.HBM,
    )


def solution(mesh):
    sizes = mesh.shape

    def local(*args):
        rows, own, depth = args[1].shape
        fits = (sizes["tm"], sizes["space"], sizes["yz"]) == (4, 2, 2)
        fits = fits and rows >= 2 * (NEAR + 1) and rows % 8 == 0 and own % 8 == 0 and own >= SIDE and depth % 128 == 0
        return four_slabs(*args) if fits else any_mesh(*args)

    field = P(("groups", "space"), "yz", None)
    slabs = P("tm", ("groups", "space"), "yz", None)
    return jax.shard_map(
        local,
        mesh=mesh,
        in_specs=(field, field, P(None, ("groups", "space"), "yz", None), slabs, slabs, slabs, slabs),
        out_specs=(slabs, slabs),
        check_vma=False,
    )
```
